32 devices in a mesh: section: 4 (over y, core), dp: 8 (over z, x).
Axes of the slice: x: 2, y: 2, z: 4, core: 2. Of those that a mesh axis runs over, the one named last changes fastest.
Arguments:
- acts: bfloat16 [4, 2, 1024, 512], P('section', None, 'dp'), may hold values from -12 to 12
- weights: bfloat16 [4, 512, 512], P('section'), may hold values from -0.25 to 0.25
- cot_last: bfloat16 [2, 1024, 512], P(None, 'dp'), may hold values from -1.796875 to 1.796875
Outputs:
- input_cots: bfloat16 [4, 2, 1024, 512], P('section', None, 'dp')
- update: float32 [4, 512, 512], P('section')
The draws below stay inside these ranges and needn't reach their ends.
All inputs are finite; a program needn't handle non-finite values.
Results may differ from the reference program's by a relative error of at most 0.025.
Values may be sent and summed in bfloat16 or wider, within the bound.
No kernel may reach another device: no remote copies, remote signals or barrier semaphores. Data moves between devices by JAX's collectives and lax.ppermute only.
A program may use at most 64 MiB of HBM per device.

```python
import jax
import jax.numpy as jnp
from jax import lax

BLK = 512
MB = 2
NS_STEPS = 3
SECTIONS = 4
TOKENS = 1024


def draw_acts(key, part):
    first, second = jax.random.split(key, 2)
    scales = jnp.exp(jax.random.uniform(first, (SECTIONS, 1, 1, BLK), jnp.float32, jnp.log(0.3), jnp.log(3.0)))
    base = jax.random.normal(second, (SECTIONS, MB, TOKENS, BLK), jnp.float32)
    base = jnp.clip(base, -4.0, 4.0)
    return (base * scales).astype(jnp.bfloat16)


def shard_levels(key, extent, pieces, smallest, top_value):
    level, own = 1.0, jax.random.fold_in(key, 6)
    for dim, blocks in pieces:
        draws = jnp.exp(jax.random.uniform(jax.random.fold_in(own, dim), (blocks,), jnp.float32, smallest / len(pieces), top_value / len(pieces)))
        level = level * jnp.repeat(draws, extent[dim] // blocks).reshape([-1 if axis == dim else 1 for axis in range(len(extent))])
    return level


def scatter_about(stream_key, dims, scale, limit, pieces=(), kind=jnp.bfloat16):
    drawn = scale * jax.random.normal(stream_key, dims, jnp.float32)
    if pieces:
        drawn = drawn * shard_levels(stream_key, dims, pieces, -0.22, 0.18)
    return jnp.clip(drawn, -limit, limit).astype(kind)


def setup_inputs(seed: int = 0) -> dict:
    streams_of = jax.random.split(jax.random.key(seed), 4)
    return {
        "acts": draw_acts(jax.random.fold_in(streams_of[3], 71), 0),
        "weights": scatter_about(streams_of[1], (SECTIONS, BLK, BLK), BLK ** -0.5, 0.25, ((0, 4),)),
        "cot_last": scatter_about(streams_of[2], (MB, TOKENS, BLK), 0.3, 1.796875, ((1, 8),)),
    }


def silu_slope(pre):
    sig = jax.nn.sigmoid(pre)
    return sig * (1.0 + pre * (1.0 - sig))

def moment(left, right):
    return lax.dot_general(left, right, (((0,), (0,)), ((), ())), preferred_element_type=jnp.float32)

def newton(matrix):
    eye = jnp.eye(matrix.shape[0], dtype=jnp.float32)
    approx = eye / jnp.sqrt(jnp.sum(matrix * matrix))
    for step in range(NS_STEPS):
        inner = jnp.dot(matrix, approx, precision=lax.Precision.HIGHEST)
        approx = 2.0 * approx - jnp.dot(approx, inner, precision=lax.Precision.HIGHEST)
    return approx

def reference(acts, weights, cot_last):
    count = MB * TOKENS
    eye = jnp.eye(BLK, dtype=jnp.float32)
    upstream = cot_last.reshape(MB * TOKENS, BLK)
    cots = [None] * SECTIONS
    updates = [None] * SECTIONS
    for section in range(SECTIONS - 1, -1, -1):
        inputs = acts[section].reshape(MB * TOKENS, BLK)
        weight = weights[section]
        pre = jnp.dot(inputs, weight, preferred_element_type=jnp.float32)
        slope_dh = (upstream.astype(jnp.float32) * silu_slope(pre)).astype(jnp.bfloat16)
        back = lax.dot_general(slope_dh, weight, (((1,), (1,)), ((), ())), preferred_element_type=jnp.float32)
        result = (upstream.astype(jnp.float32) + back).astype(jnp.bfloat16)
        cots[section] = result.reshape(MB, TOKENS, BLK)
        act_factor = moment(inputs, inputs) / count + 0.01 * eye
        out_factor = moment(slope_dh, slope_dh) / count + 0.01 * eye
        grad = moment(inputs, slope_dh)
        act_inv = newton(act_factor)
        out_inv = newton(out_factor)
        updates[section] = jnp.dot(jnp.dot(act_inv, grad, precision=lax.Precision.HIGHEST), out_inv, precision=lax.Precision.HIGHEST)
        upstream = result
    return (jnp.stack(cots), jnp.stack(updates))
```

```python
import jax
import jax.numpy as jnp
from jax import lax
from jax.sharding import PartitionSpec as P


def silu_slope(pre):
    sig = jax.nn.sigmoid(pre)
    return sig * (1.0 + pre * (1.0 - sig))


def moment(left, right):
    return lax.dot_general(
        left, right, (((0,), (0,)), ((), ())), preferred_element_type=jnp.float32
    )


def mul(left, right):
    return jnp.dot(left, right, precision=lax.Precision.HIGH)


def inverse(matrix):
    eye = jnp.eye(matrix.shape[0], dtype=jnp.float32)
    scale = lax.rsqrt(jnp.sum(matrix * matrix))
    first = matrix * scale
    second = 2.0 * first - mul(first, first)
    square = mul(second, second)
    tail = mul(2.0 * eye - second, 2.0 * eye - 2.0 * second + square)
    return mul(2.0 * eye - first, tail) * scale


def body(acts, weights, cot_last):
    sections = lax.axis_size("section")
    here = lax.axis_index("section")
    pairs = sections // 2
    odd = (here % 2) == 1
    weight = weights[0]
    micro, rows, width = acts.shape[1:]
    tokens = micro * rows
    count = tokens * lax.axis_size("dp")
    eye = jnp.eye(width, dtype=jnp.float32)
    flat = acts[0].reshape(tokens, width)

    to_even = [(s, s - 1) for s in range(1, sections, 2)]
    odd_weight = jnp.where(odd, weight, lax.ppermute(weight, "section", to_even))
    odd_flat = jnp.where(odd, flat, lax.ppermute(flat, "section", to_even))

    every = lax.all_gather(flat, "dp", tiled=True)
    act_inv = inverse(moment(every, every) / count + 0.01 * eye)

    slope_odd = silu_slope(jnp.dot(odd_flat, odd_weight, preferred_element_type=jnp.float32))
    slope_own = silu_slope(jnp.dot(flat, weight, preferred_element_type=jnp.float32))

    def layer(upstream, slope, matrix):
        dh = (upstream.astype(jnp.float32) * slope).astype(jnp.bfloat16)
        back = lax.dot_general(dh, matrix, (((1,), (1,)), ((), ())), preferred_element_type=jnp.float32)
        return dh, (upstream.astype(jnp.float32) + back).astype(jnp.bfloat16)

    upstream = cot_last.reshape(tokens, width)
    for turn in range(pairs):
        dh_odd, cot_odd = layer(upstream, slope_odd, odd_weight)
        dh_even, cot_even = layer(cot_odd, slope_own, weight)
        mine_dh = jnp.where(odd, dh_odd, dh_even)
        mine_cot = jnp.where(odd, cot_odd, cot_even)
        if turn == 0:
            dh, cot = mine_dh, mine_cot
        else:
            now = (here // 2) == pairs - 1 - turn
            dh, cot = jnp.where(now, mine_dh, dh), jnp.where(now, mine_cot, cot)
        if turn < pairs - 1:
            low = lax.ppermute(cot_even, "section", [(s, s - 2) for s in range(2, sections, 2)])
            high = lax.ppermute(cot_even, "section", [(s, s - 1) for s in range(2, sections, 2)])
            upstream = jnp.where(odd, high, low)

    out_sum, grad = lax.psum(
        (moment(dh, dh).astype(jnp.bfloat16), moment(flat, dh).astype(jnp.bfloat16)), "dp"
    )
    out_inv = inverse(out_sum.astype(jnp.float32) / count + 0.01 * eye)
    update = mul(mul(act_inv, grad.astype(jnp.float32)), out_inv)
    return (cot.reshape(1, micro, rows, width), update[None])


def solution(mesh):
    placed = (P("section", None, "dp", None), P("section", None, None), P(None, "dp", None))
    return jax.shard_map(
        body,
        mesh=mesh,
        in_specs=placed,
        out_specs=(P("section", None, "dp", None), P("section", None, None)),
        check_vma=False,
    )
```

```python
import jax
import jax.numpy as jnp
import numpy as np
from jax import lax
from jax.sharding import Mesh, PartitionSpec as P

BF16 = jnp.bfloat16


def silu_slope(pre):
    sig = jax.nn.sigmoid(pre)
    return sig * (1.0 + pre * (1.0 - sig))


def moment(left, right):
    return lax.dot_general(
        left, right, (((0,), (0,)), ((), ())), preferred_element_type=jnp.float32
    )


def mul(left, right):
    return jnp.dot(left, right, precision=lax.Precision.HIGH)


def inverse(matrix):
    eye = jnp.eye(matrix.shape[0], dtype=jnp.float32)
    scale = lax.rsqrt(jnp.sum(matrix * matrix))
    first = matrix * scale
    second = 2.0 * first - mul(first, first)
    square = mul(second, second)
    tail = mul(2.0 * eye - second, 2.0 * eye - 2.0 * second + square)
    return mul(2.0 * eye - first, tail) * scale


def packed(full):
    half = full.shape[1] // 2
    return jnp.concatenate([full[:, :half], full[:, half:]], axis=0)


def unpacked(rows):
    half = rows.shape[0] // 2
    return jnp.concatenate([rows[:half], rows[half:]], axis=1)


def packed_symmetric(full):
    half = full.shape[1] // 2
    return jnp.concatenate([full[:, :half], full[half:, half:]], axis=0)


def unpacked_symmetric(rows):
    half = rows.shape[1]
    low = rows[half:2 * half]
    return jnp.concatenate(
        [
            jnp.concatenate([rows[:half], low.T], axis=1),
            jnp.concatenate([low, rows[2 * half:]], axis=1),
        ],
        axis=0,
    )


def body(acts, weights, cot_last):
    pairs = lax.axis_size("row")
    line = lax.axis_size("line")
    row = lax.axis_index("row")
    core = lax.axis_index("core")
    side = lax.axis_index("side")
    weight = weights[0]
    local = acts[0]
    micro, rows, width = local.shape
    count = micro * rows * line * lax.axis_size("side")
    eye = jnp.eye(width, dtype=jnp.float32)
    odd = core == 1
    swap = [(0, 1), (1, 0)]

    partner_weight = lax.ppermute(weight, "core", swap)
    mine = jnp.where(odd, local[1], local[0])
    partner = lax.ppermute(jnp.where(odd, local[0], local[1]), "core", swap)
    weight_odd = jnp.where(odd, weight, partner_weight)
    weight_even = jnp.where(odd, partner_weight, weight)
    x_odd = jnp.where(odd, mine, partner)
    x_even = jnp.where(odd, partner, mine)
    slope_odd = silu_slope(jnp.dot(x_odd, weight_odd, preferred_element_type=jnp.float32))
    slope_even = silu_slope(jnp.dot(x_even, weight_even, preferred_element_type=jnp.float32))

    def layer(upstream, slope, matrix):
        dh = (upstream.astype(jnp.float32) * slope).astype(BF16)
        back = lax.dot_general(dh, matrix, (((1,), (1,)), ((), ())), preferred_element_type=jnp.float32)
        return dh, (upstream.astype(jnp.float32) + back).astype(BF16)

    upstream = jnp.where(odd, cot_last[1], cot_last[0])
    for turn in range(pairs):
        now = (layer(upstream, slope_odd, weight_odd),)
        now += (layer(now[0][1], slope_even, weight_even),)
        if turn == 0:
            kept = now
        else:
            here = row == pairs - 1 - turn
            kept = jax.tree.map(lambda new, old: jnp.where(here, new, old), now, kept)
        if turn < pairs - 1:
            upstream = lax.ppermute(now[1][1], "row", [(r, r - 1) for r in range(1, pairs)])
    (dh_odd, cot_odd), (dh_even, cot_even) = kept

    other_cot = lax.ppermute(jnp.where(odd, cot_even, cot_odd), "core", swap)
    own_cot = jnp.where(odd, cot_odd, cot_even)
    cot = jnp.stack([jnp.where(odd, other_cot, own_cot), jnp.where(odd, own_cot, other_cot)])

    dh = lax.all_to_all(
        jnp.concatenate([dh_even, dh_even, dh_odd, dh_odd]), ("core", "side"), 0, 0, tiled=True
    )
    far = lax.ppermute(local, "side", swap)
    first = jnp.where(side == 0, local, far)
    second = jnp.where(side == 0, far, local)
    x = jnp.stack([first, second], axis=1).reshape(-1, width)

    sums = jnp.concatenate(
        [
            packed_symmetric(moment(dh, dh).astype(BF16)),
            packed_symmetric(moment(x, x).astype(BF16)),
            packed(moment(x, dh).astype(BF16)),
        ]
    )
    height, across = sums.shape
    part = height // 2 // line
    half = lax.dynamic_slice_in_dim(sums, side * (height // 2), height // 2, 0)
    parts = lax.all_to_all(half, "line", 0, 0, tiled=True).reshape(line, part, across)
    total = jnp.sum(parts.astype(jnp.float32), axis=0).astype(BF16)
    copies = jnp.broadcast_to(total[None], (line * 2, part, across))
    every = lax.all_to_all(copies, ("line", "side"), 0, 0, tiled=True)
    every = every.reshape(line, 2, part, across).swapaxes(0, 1).reshape(height, across)
    every = every.astype(jnp.float32)
    cut = 3 * width // 2
    out_inv = inverse(unpacked_symmetric(every[:cut]) / count + 0.01 * eye)
    act_inv = inverse(unpacked_symmetric(every[cut:2 * cut]) / count + 0.01 * eye)
    update = mul(mul(act_inv, unpacked(every[2 * cut:])), out_inv)
    return (cot[None], update[None])


def solution(mesh):
    sections, shards = mesh.devices.shape
    finer = Mesh(
        np.reshape(mesh.devices, (sections // 2, 2, shards // 2, 2)),
        ("row", "core", "line", "side"),
    )
    section, dp = ("row", "core"), ("line", "side")
    placed = (P(section, None, dp, None), P(section, None, None), P(None, dp, None))
    return jax.shard_map(
        body,
        mesh=finer,
        in_specs=placed,
        out_specs=(P(section, None, dp, None), P(section, None, None)),
        check_vma=False,
    )
```

```python
import jax
import jax.numpy as jnp
import numpy as np
from jax import lax
from jax.sharding import Mesh, PartitionSpec as P

BF16 = jnp.bfloat16
SWAP = [(0, 1), (1, 0)]


def silu_slope(pre):
    sig = jax.nn.sigmoid(pre)
    return sig * (1.0 + pre * (1.0 - sig))


def moment(left, right):
    return lax.dot_general(
        left, right, (((0,), (0,)), ((), ())), preferred_element_type=jnp.float32
    )


def mul(left, right):
    return jnp.dot(left, right, precision=lax.Precision.HIGH)


def inverse(matrix):
    eye = jnp.eye(matrix.shape[0], dtype=jnp.float32)
    scale = lax.rsqrt(jnp.sum(matrix * matrix))
    first = matrix * scale
    second = 2.0 * first - mul(first, first)
    square = mul(second, second)
    tail = mul(2.0 * eye - second, 2.0 * eye - 2.0 * second + square)
    return mul(2.0 * eye - first, tail) * scale


def rolled(full, side, axis):
    half = full.shape[axis] // 2
    low = lax.slice_in_dim(full, 0, half, axis=axis)
    high = lax.slice_in_dim(full, half, 2 * half, axis=axis)
    return jnp.where(side == 0, full, jnp.concatenate([high, low], axis=axis))


def half_factor(full, side):
    quarter = full.shape[0] // 4
    mine = lax.dynamic_slice_in_dim(full, side * 2 * quarter, 2 * quarter, 0)
    mine = rolled(mine, side, 1)
    top = (jnp.arange(2 * quarter) < quarter)[:, None]
    return jnp.where(top, mine[:, :3 * quarter], mine[:, quarter:])


def whole_factor(mine, other):
    quarter = mine.shape[0] // 2

    def block(source, row, column):
        return source[row * quarter:(row + 1) * quarter, column * quarter:(column + 1) * quarter]

    def across(row):
        return jnp.concatenate(row, axis=1)

    return jnp.concatenate(
        [
            across([mine[:quarter], block(other, 1, 1).T]),
            across([block(mine, 0, 1).T, mine[quarter:]]),
            across([block(other, 0, 2), block(mine, 1, 1).T, other[:quarter, :2 * quarter]]),
            across([other[quarter:, quarter:], block(other, 0, 1).T, block(other, 1, 0)]),
        ]
    )


def scatter_sum(parts):
    line = lax.axis_size("line")
    place = lax.axis_index("line")
    total = lax.dynamic_index_in_dim(parts, place, 0, keepdims=False).astype(jnp.float32)
    for step in sorted(range(1, line), key=lambda k: -min(k, line - k)):
        term = lax.dynamic_index_in_dim(parts, (place + step) % line, 0, keepdims=False)
        route = [(i, (i + step) % line) for i in range(line)]
        total += lax.ppermute(term, "line", route).astype(jnp.float32)
    return total


def gather(part):
    line = lax.axis_size("line")
    place = lax.axis_index("line")
    every = jnp.zeros((line,) + part.shape, part.dtype)
    every = lax.dynamic_update_index_in_dim(every, part, place, 0)
    for step in sorted(range(1, line), key=lambda k: -min(k, line - k)):
        route = [(i, (i + step) % line) for i in range(line)]
        got = lax.ppermute(part, "line", route)
        every = lax.dynamic_update_index_in_dim(every, got, (place - step) % line, 0)
    return every.reshape((line * part.shape[0],) + part.shape[1:])


def body(acts, weights, cot_last):
    pairs = lax.axis_size("row")
    line = lax.axis_size("line")
    row = lax.axis_index("row")
    core = lax.axis_index("core")
    side = lax.axis_index("side")
    weight = weights[0]
    local = acts[0]
    micro, rows, width = local.shape
    count = micro * rows * line * 2
    eye = jnp.eye(width, dtype=jnp.float32)
    odd = core == 1

    def mine_of(pair):
        return jnp.where(odd, pair[1], pair[0])

    def others_of(pair):
        return jnp.where(odd, pair[0], pair[1])

    partner_weight = lax.ppermute(weight, "core", SWAP)
    partner_x = lax.ppermute(others_of(local), "core", SWAP)
    weight_odd = jnp.where(odd, weight, partner_weight)
    weight_even = jnp.where(odd, partner_weight, weight)

    def slopes(own, partner):
        def slope(inputs, matrix):
            return silu_slope(jnp.dot(inputs, matrix, preferred_element_type=jnp.float32))

        return (
            slope(jnp.where(odd, own, partner), weight_odd),
            slope(jnp.where(odd, partner, own), weight_even),
        )

    def layer(upstream, slope, matrix):
        dh = (upstream.astype(jnp.float32) * slope).astype(BF16)
        back = lax.dot_general(dh, matrix, (((1,), (1,)), ((), ())), preferred_element_type=jnp.float32)
        return dh, (upstream.astype(jnp.float32) + back).astype(BF16)

    def layers(upstream, slope):
        dh_odd, cot_odd = layer(upstream, slope[0], weight_odd)
        return (dh_odd, cot_odd) + layer(cot_odd, slope[1], weight_even)

    slope_near = slopes(mine_of(local), partner_x)
    last = mine_of(cot_last)
    near = layers(last, slope_near)
    upstream_far = lax.ppermute(last, "side", SWAP)
    far = lax.ppermute(local, "side", SWAP)
    slope_far = slopes(mine_of(far), lax.ppermute(others_of(far), "core", SWAP))
    latest = near
    for turn in range(1, pairs):
        straight = [(r, r - 1) for r in range(1, pairs)]
        diagonal = [(2 * r + s, 2 * r - 1 - s) for r in range(1, pairs) for s in range(2)]
        upstream = lax.ppermute(latest[3], "row", straight)
        crossing = lax.ppermute(latest[3], ("row", "side"), diagonal)
        latest = layers(upstream, slope_near)
        here = row == pairs - 1 - turn
        near = jax.tree.map(lambda new, old: jnp.where(here, new, old), latest, near)
        upstream_far = jnp.where(here, crossing, upstream_far)

    x = jnp.concatenate([mine_of(local), mine_of(far), others_of(local), others_of(far)])
    act_half = half_factor(moment(x, x).astype(BF16), side)
    act_half = gather(scatter_sum(act_half.reshape(line, -1, act_half.shape[1])).astype(BF16))
    act_sum = whole_factor(act_half, lax.ppermute(act_half, "side", SWAP)).astype(jnp.float32)
    act_sum = rolled(rolled(act_sum, side, 0), side, 1)
    act_inv = inverse(act_sum / count + 0.01 * eye)

    away = layers(upstream_far, slope_far)
    other_cot = lax.ppermute(others_of((near[3], near[1])), "core", SWAP)
    own_cot = mine_of((near[3], near[1]))
    cot = jnp.stack([mine_of((own_cot, other_cot)), mine_of((other_cot, own_cot))])
    own_dh = jnp.concatenate([mine_of((near[2], near[0])), mine_of((away[2], away[0]))])
    give_dh = jnp.concatenate([others_of((near[2], near[0])), others_of((away[2], away[0]))])
    dh = jnp.concatenate([own_dh, lax.ppermute(give_dh, "core", SWAP)])

    out_half = half_factor(moment(dh, dh).astype(BF16), side)
    grad_half = lax.dynamic_slice_in_dim(moment(dh, x).astype(BF16), side * (width // 2), width // 2, 0)
    both = jnp.concatenate([out_half, grad_half], axis=1)
    total = scatter_sum(both.reshape(line, -1, both.shape[1]))
    cut = out_half.shape[1]
    out_half = gather(total[:, :cut].astype(BF16))
    out_other = lax.ppermute(out_half, "side", SWAP)
    half = gather(mul(total[:, cut:], act_inv).astype(BF16))
    other = lax.ppermute(half, "side", SWAP)
    out_inv = inverse(whole_factor(out_half, out_other).astype(jnp.float32) / count + 0.01 * eye)
    rows_of = jnp.concatenate([half, other]).astype(jnp.float32)
    update = lax.dot_general(rows_of, out_inv, (((0,), (0,)), ((), ())), precision=lax.Precision.HIGH)
    return (cot[None], rolled(update, side, 1)[None])


def solution(mesh):
    sections, shards = mesh.devices.shape
    finer = Mesh(
        np.reshape(mesh.devices, (sections // 2, 2, shards // 2, 2)),
        ("row", "core", "line", "side"),
    )
    section, dp = ("row", "core"), ("line", "side")
    placed = (P(section, None, dp, None), P(section, None, None), P(None, dp, None))
    return jax.shard_map(
        body,
        mesh=finer,
        in_specs=placed,
        out_specs=(P(section, None, dp, None), P(section, None, None)),
        check_vma=False,
    )
```

```python
import functools

import jax
import jax.numpy as jnp
import numpy as np
from jax import lax
from jax.experimental import pallas as pl
from jax.experimental.pallas import tpu as pltpu
from jax.sharding import Mesh, PartitionSpec as P

BF16 = jnp.bfloat16
F32 = jnp.float32
SWAP = [(0, 1), (1, 0)]
SMEM = pl.BlockSpec(memory_space=pltpu.SMEM)
VMEM = pl.BlockSpec(memory_space=pltpu.VMEM)
ANY = pl.BlockSpec(memory_space=pl.ANY)


def silu_slope(pre):
    sig = jax.nn.sigmoid(pre)
    return sig * (1.0 + pre * (1.0 - sig))


def slope_of(inputs, matrix):
    return silu_slope(jnp.dot(inputs, matrix, preferred_element_type=F32))


def layer(upstream, slope, matrix):
    dh = (upstream.astype(F32) * slope).astype(BF16)
    back = lax.dot_general(dh, matrix, (((1,), (1,)), ((), ())), preferred_element_type=F32)
    return dh, (upstream.astype(F32) + back).astype(BF16)


def by_core(core, run, own, partner):
    @pl.when(core == 1)
    def _():
        run(own, partner)

    @pl.when(core == 0)
    def _():
        run(partner, own)


def first_kernel(where, own, partner, local, partner_x, cot_last, slope_odd, slope_even, down, cross):
    core = where[2]
    upstream = cot_last[core]

    def run(odd, even):
        slope_odd[...] = slope_of(odd[1], odd[0][...])
        slope_even[...] = slope_of(even[1], even[0][...])
        cot = layer(upstream, slope_odd[...], odd[0][...])[1]
        down[...] = layer(cot, slope_even[...], even[0][...])[1]

    by_core(core, run, (own, local[core]), (partner, partner_x[...]))
    cross[...] = jnp.where(where[3] == 0, upstream, down[...])


def far_kernel(where, own, partner, far, partner_far, slope_odd, slope_even):
    core = where[2]

    def run(odd, even):
        slope_odd[...] = slope_of(odd[1], odd[0][...])
        slope_even[...] = slope_of(even[1], even[0][...])

    by_core(core, run, (own, far[core]), (partner, partner_far[...]))


def layers_kernel(
    where, own, partner, near_odd, near_even, far_odd, far_even, near, far, cot_last,
    own_dh, give_dh, own_cot, give_cot, upstream,
):
    rows = near.shape[0]
    top = where[3] == where[4] - 1
    upstream[:rows] = jnp.where(top, cot_last[where[2]], near[...])
    upstream[rows:] = far[...]

    def run(odd, even):
        slope = jnp.concatenate([near_odd[...], far_odd[...]])
        dh, cot = layer(upstream[...], slope, odd[0][...])
        odd[1][...] = dh
        odd[2][...] = cot[:rows]
        slope = jnp.concatenate([near_even[...], far_even[...]])
        dh, cot = layer(cot, slope, even[0][...])
        even[1][...] = dh
        even[2][...] = cot[:rows]

    by_core(where[2], run, (own, own_dh, own_cot), (partner, give_dh, give_cot))


def moment(left, right):
    return lax.dot_general(left, right, (((0,), (0,)), ((), ())), preferred_element_type=F32)


def split(value):
    high = value.astype(BF16)
    return high, (value - high.astype(F32)).astype(BF16)


def product(left, right, dims=((1,), (0,))):
    def dot(a, b):
        return lax.dot_general(a, b, (dims, ((), ())), preferred_element_type=F32)

    total = dot(left[0], right[0])
    if len(right) > 1:
        total += dot(left[0], right[1])
    if len(left) > 1:
        total += dot(left[1], right[0])
    return total


def call(kernel, flops, out_shape, in_specs, scratch=()):
    return pl.pallas_call(
        kernel,
        out_shape=out_shape,
        in_specs=in_specs,
        out_specs=jax.tree.map(lambda _: VMEM, out_shape),
        scratch_shapes=list(scratch),
        cost_estimate=pl.CostEstimate(flops=flops, bytes_accessed=1 << 20, transcendentals=0),
        compiler_params=pltpu.CompilerParams(vmem_limit_bytes=40 << 20),
    )


def packed_moment(tokens, side, place_in):
    half = tokens.shape[1] // 2
    quarter = half // 2
    own = pl.multiple_of(side * half, half)
    other = pl.multiple_of(half - side * half, half)
    mine = tokens[:, pl.ds(own, half)]
    rest = tokens[:, pl.ds(other, half)]
    place_in[:quarter, :half] = moment(mine[:, :quarter], mine).astype(BF16)
    place_in[:quarter, half:3 * quarter] = moment(mine[:, :quarter], rest[:, :quarter]).astype(BF16)
    place_in[quarter:, :quarter] = moment(mine[:, quarter:], mine[:, quarter:]).astype(BF16)
    place_in[quarter:, quarter:3 * quarter] = moment(mine[:, quarter:], rest).astype(BF16)
    return mine


def act_kernel(where, local, far, after, *refs):
    parts, (tokens, whole) = refs[:-2], refs[-2:]
    micro, rows = local.shape[:2]
    for m in range(micro):
        tokens[m * rows:(m + 1) * rows] = local[m]
        tokens[(micro + m) * rows:(micro + m + 1) * rows] = far[m]
    packed_moment(tokens, where[1], whole)
    cut_parts(where[0], whole, parts)


def cut_parts(place, whole, parts):
    rows = parts[0].shape[0]
    for step, part in enumerate(parts):
        start = pl.multiple_of((place ^ step) * rows, rows)
        part[:, :whole.shape[1]] = whole[pl.ds(start, rows)]


def grad_kernel(where, local, far, dh_own, dh_got, act_part, *refs):
    parts, (inputs, tokens, whole) = refs[:-3], refs[-3:]
    rows, width = local.shape[1:]
    core = where[2]
    inputs[:rows] = local[core]
    inputs[rows:2 * rows] = far[core]
    inputs[2 * rows:3 * rows] = local[1 - core]
    inputs[3 * rows:] = far[1 - core]
    tokens[:2 * rows] = dh_own[...]
    tokens[2 * rows:] = dh_got[...]
    cut = 3 * width // 4
    mine = packed_moment(tokens, where[1], whole)
    whole[:, cut:] = moment(mine, inputs[...]).astype(BF16)
    cut_parts(where[0], whole, parts)
    for part in parts:
        part[:, whole.shape[1]:] = act_part[...]


def inverse_kernel(unroll, count, where, mine, other, result, ours, theirs, matrix):
    line, rows = mine.shape[:2]
    for step in range(line):
        start = pl.multiple_of((where[0] ^ step) * rows, rows)
        ours[pl.ds(start, rows)] = mine[step].astype(F32)
        theirs[pl.ds(start, rows)] = other[step].astype(F32)
    q = ours.shape[0] // 2
    matrix[:q, :3 * q] = ours[:q]
    matrix[:q, 3 * q:] = theirs[q:, q:2 * q].T
    matrix[q:2 * q, :q] = ours[:q, q:2 * q].T
    matrix[q:2 * q, q:] = ours[q:]
    matrix[2 * q:3 * q, :q] = theirs[:q, 2 * q:]
    matrix[2 * q:3 * q, q:2 * q] = ours[q:, q:2 * q].T
    matrix[2 * q:3 * q, 2 * q:] = theirs[:q, :2 * q]
    matrix[3 * q:, :2 * q] = theirs[q:, q:]
    matrix[3 * q:, 2 * q:3 * q] = theirs[:q, q:2 * q].T
    matrix[3 * q:, 3 * q:] = theirs[q:, :q]
    width = 4 * q
    row = lax.broadcasted_iota(jnp.int32, (width, width), 0)
    column = lax.broadcasted_iota(jnp.int32, (width, width), 1)
    eye = (row == column).astype(F32)
    full = matrix[...] * (1.0 / count) + 0.01 * eye
    scale = lax.rsqrt(jnp.sum(full * full, keepdims=True))
    first = full * scale
    first_terms = split(first)
    second = 2.0 * first - product(first_terms, first_terms)
    second_terms = split(second)
    square = product(second_terms, second_terms)
    last = 2.0 * (eye - second) + square
    tail = 2.0 * last - product(second_terms, split(last))
    inverse = (2.0 * tail - product(first_terms, split(tail))) * scale
    if unroll:
        half = 2 * q
        own = pl.multiple_of(where[1] * half, half)
        away = pl.multiple_of(half - where[1] * half, half)
        for i, a in enumerate((own, away)):
            for j, b in enumerate((own, away)):
                result[pl.ds(a, half), pl.ds(b, half)] = inverse[
                    i * half:(i + 1) * half, j * half:(j + 1) * half
                ]
    else:
        result[...] = inverse


def update_kernel(where, mine, other, act_inv, out_inv, result, rows_of):
    line, rows = mine.shape[:2]
    half = line * rows
    for step in range(line):
        start = pl.multiple_of((where[0] ^ step) * rows, rows)
        rows_of[pl.ds(start, rows)] = mine[step]
        rows_of[pl.ds(half + start, rows)] = other[step]
    left = product((rows_of[...],), split(act_inv[...]))
    update = product(split(left), split(out_inv[...]), ((0,), (0,)))
    own = pl.multiple_of(where[1] * half, half)
    away = pl.multiple_of(half - where[1] * half, half)
    result[:, pl.ds(own, half)] = update[:, :half]
    result[:, pl.ds(away, half)] = update[:, half:]


def send(parts):
    line = len(parts)
    got = {0: parts[0]}
    for step in sorted(range(1, line), key=lambda k: (-(k & (line // 2)), k)):
        got[step] = lax.ppermute(parts[step], "line", [(i, i ^ step) for i in range(line)])
    return [got[step] for step in range(line)]


def body(acts, weights, cot_last):
    pairs = lax.axis_size("row")
    line = lax.axis_size("line")
    row = lax.axis_index("row")
    core = lax.axis_index("core")
    side = lax.axis_index("side")
    weight = weights[0]
    local = acts[0]
    micro, rows, width = local.shape
    count = micro * rows * line * 2
    odd = core == 1
    where = jnp.stack([lax.axis_index("line"), side, core, row, pairs]).astype(jnp.int32)

    def mine_of(pair):
        return jnp.where(odd, pair[1], pair[0])

    def others_of(pair):
        return jnp.where(odd, pair[0], pair[1])

    partner = lax.ppermute(weight, "core", SWAP)
    partner_x = lax.ppermute(others_of(local), "core", SWAP)
    far = lax.ppermute(local, "side", SWAP)
    partner_far = lax.ppermute(partner_x, "side", SWAP)
    block = jax.ShapeDtypeStruct((rows, width), BF16)
    slope = jax.ShapeDtypeStruct((rows, width), F32)
    near_odd, near_even, down, cross = call(
        first_kernel, 8 * rows * width**2, [slope, slope, block, block], [SMEM] + [VMEM] * 5
    )(where, weight, partner, local, partner_x, cot_last)
    first = down
    for turn in range(1, pairs):
        straight = [(r, r - 1) for r in range(1, pairs)]
        diagonal = [(2 * r + s, 2 * ((r - 1) % pairs) + 1 - s) for r in range(pairs) for s in range(2)]
        upstream = lax.ppermute(down, "row", straight)
        crossing = lax.ppermute(cross, ("row", "side"), diagonal)
        here = row == pairs - 1 - turn
        if turn == 1:
            near_up, far_up = upstream, crossing
        else:
            near_up = jnp.where(here, upstream, near_up)
            far_up = jnp.where(here, crossing, far_up)
        if turn < pairs - 1:
            cot = layer(upstream, near_odd, jnp.where(odd, weight, partner))[1]
            down = layer(cot, near_even, jnp.where(odd, partner, weight))[1]
            cross = jnp.where(row == 0, mine_of(cot_last), down)

    tokens = 2 * micro * rows
    half, cut = width // 2, 3 * width // 4
    part = half // line
    act_parts = call(
        act_kernel,
        2 * tokens * half * cut,
        [jax.ShapeDtypeStruct((part, cut), BF16)] * line,
        [SMEM, VMEM, VMEM, ANY],
        [pltpu.VMEM((tokens, width), BF16), pltpu.VMEM((half, cut), BF16)],
    )(where, local, far, first)
    act_part = sum(piece.astype(F32) for piece in send(act_parts)).astype(BF16)

    far_odd, far_even = call(far_kernel, 4 * rows * width**2, [slope, slope], [SMEM] + [VMEM] * 4)(
        where, weight, partner, far, partner_far
    )
    pair = jax.ShapeDtypeStruct((2 * rows, width), BF16)
    own_dh, give_dh, own_cot, give_cot = call(
        layers_kernel,
        8 * rows * width**2,
        [pair, pair, block, block],
        [SMEM] + [VMEM] * 9,
        [pltpu.VMEM((2 * rows, width), BF16)],
    )(where, weight, partner, near_odd, near_even, far_odd, far_even, near_up, far_up, cot_last)
    got_dh = lax.ppermute(give_dh, "core", SWAP)
    other_cot = lax.ppermute(give_cot, "core", SWAP)
    cot = jnp.stack([mine_of((own_cot, other_cot)), mine_of((other_cot, own_cot))])

    parts = call(
        grad_kernel,
        2 * tokens * half * (cut + width),
        [jax.ShapeDtypeStruct((part, 2 * cut + width), BF16)] * line,
        [SMEM] + [VMEM] * 5,
        [pltpu.VMEM((tokens, width), BF16)] * 2 + [pltpu.VMEM((half, cut + width), BF16)],
    )(where, local, far, own_dh, got_dh, act_part)
    got = send(parts)
    act_mine = jnp.stack([piece[:, cut + width:] for piece in got])
    act_other = lax.ppermute(act_mine, "side", SWAP)
    total = sum(piece[:, :cut + width].astype(F32) for piece in got).astype(BF16)
    got = send([total] * line)
    out_mine = jnp.stack([piece[:, :cut] for piece in got])
    grad_mine = jnp.stack([piece[:, cut:] for piece in got])
    out_other = lax.ppermute(out_mine, "side", SWAP)
    grad_other = lax.ppermute(grad_mine, "side", SWAP)

    def inverse(unroll, ours, theirs):
        return call(
            functools.partial(inverse_kernel, unroll, count),
            8 * width**3,
            jax.ShapeDtypeStruct((width, width), F32),
            [SMEM, VMEM, VMEM],
            [pltpu.VMEM((half, cut), F32)] * 2 + [pltpu.VMEM((width, width), F32)],
        )(where, ours, theirs)

    act_inv = inverse(True, act_mine, act_other)
    out_inv = inverse(False, out_mine, out_other)
    update = call(
        update_kernel,
        4 * width**3,
        jax.ShapeDtypeStruct((width, width), F32),
        [SMEM] + [VMEM] * 4,
        [pltpu.VMEM((width, width), BF16)],
    )(where, grad_mine, grad_other, act_inv, out_inv)
    return (cot[None], update[None])


def solution(mesh):
    sections, shards = mesh.devices.shape
    finer = Mesh(
        np.reshape(mesh.devices, (sections // 2, 2, shards // 2, 2)),
        ("row", "core", "line", "side"),
    )
    section, dp = ("row", "core"), ("line", "side")
    placed = (P(section, None, dp, None), P(section, None, None), P(None, dp, None))
    return jax.shard_map(
        body,
        mesh=finer,
        in_specs=placed,
        out_specs=(P(section, None, dp, None), P(section, None, None)),
        check_vma=False,
    )
```

```python
import functools

import jax
import jax.numpy as jnp
import numpy as np
from jax import lax
from jax.experimental import pallas as pl
from jax.experimental.pallas import tpu as pltpu
from jax.sharding import Mesh, PartitionSpec as P

BF16 = jnp.bfloat16
F32 = jnp.float32
SWAP = [(0, 1), (1, 0)]
SMEM = pl.BlockSpec(memory_space=pltpu.SMEM)
VMEM = pl.BlockSpec(memory_space=pltpu.VMEM)
ANY = pl.BlockSpec(memory_space=pl.ANY)


def silu_slope(pre):
    sig = jax.nn.sigmoid(pre)
    return sig * (1.0 + pre * (1.0 - sig))


def slope_of(inputs, matrix):
    return silu_slope(jnp.dot(inputs, matrix, preferred_element_type=F32))


def layer(upstream, slope, matrix):
    dh = (upstream.astype(F32) * slope).astype(BF16)
    back = lax.dot_general(dh, matrix, (((1,), (1,)), ((), ())), preferred_element_type=F32)
    return dh, (upstream.astype(F32) + back).astype(BF16)


def by_core(core, run, own, partner):
    @pl.when(core == 1)
    def _():
        run(own, partner)

    @pl.when(core == 0)
    def _():
        run(partner, own)


def load_kernel(where, weight, local, cot_last, weight_copy, slope, cot):
    core = where[2]
    weight_copy[...] = weight[...]
    cot[...] = cot_last[core]
    slope[...] = slope_of(local[core], weight_copy[...])


def first_kernel(where, own, partner, slope_own, local, cot_last, slope_partner, inputs, down, cross):
    inputs[...] = local[where[2]]
    upstream = cot_last[...]
    slope_partner[...] = slope_of(inputs[...], partner[...])

    def run(odd, even):
        cot = layer(upstream, odd[1][...], odd[0][...])[1]
        down[...] = layer(cot, even[1][...], even[0][...])[1]

    by_core(where[2], run, (own, slope_own), (partner, slope_partner))
    cross[...] = jnp.where(where[3] == 0, upstream, down[...])


def far_kernel(where, own, partner, far, partner_far, slope_own, slope_partner):
    slope_own[...] = slope_of(far[where[2]], own[...])
    slope_partner[...] = slope_of(partner_far[...], partner[...])


def layers_kernel(
    where, own, partner, near_own, near_partner, far_own, far_partner, near, far, cot_last,
    own_dh, give_dh, own_cot, give_cot, upstream,
):
    rows = near.shape[0]
    top = where[3] == where[4] - 1
    upstream[:rows] = jnp.where(top, cot_last[...], near[...])
    upstream[rows:] = far[...]

    def step(incoming, matrix, near_slope, far_slope, dh_out, cot_out):
        slope = jnp.concatenate([near_slope[...], far_slope[...]])
        dh, cot = layer(incoming, slope, matrix[...])
        dh_out[...] = dh
        cot_out[...] = cot[:rows]
        return cot

    def run(odd, even):
        step(step(upstream[...], *odd), *even)

    by_core(
        where[2],
        run,
        (own, near_own, far_own, own_dh, own_cot),
        (partner, near_partner, far_partner, give_dh, give_cot),
    )


def moment(left, right):
    return lax.dot_general(left, right, (((0,), (0,)), ((), ())), preferred_element_type=F32)


def split(value):
    high = value.astype(BF16)
    return high, (value - high.astype(F32)).astype(BF16)


def product(left, right, dims=((1,), (0,))):
    def dot(a, b):
        return lax.dot_general(a, b, (dims, ((), ())), preferred_element_type=F32)

    total = dot(left[0], right[0])
    if len(right) > 1:
        total += dot(left[0], right[1])
    if len(left) > 1:
        total += dot(left[1], right[0])
    return total


def call(kernel, flops, out_shape, in_specs, scratch=()):
    return pl.pallas_call(
        kernel,
        out_shape=out_shape,
        in_specs=in_specs,
        out_specs=jax.tree.map(lambda _: VMEM, out_shape),
        scratch_shapes=list(scratch),
        cost_estimate=pl.CostEstimate(flops=flops, bytes_accessed=1 << 20, transcendentals=0),
        compiler_params=pltpu.CompilerParams(vmem_limit_bytes=32 << 20),
    )


def blocks_of(tokens, side):
    half = tokens.shape[1] // 2
    quarter = half // 2
    own = pl.multiple_of(side * half, half)
    other = pl.multiple_of(half - side * half, half)
    mine = tokens[:, pl.ds(own, half)]
    upper = moment(mine[:, :quarter], mine)
    near = tokens[:, pl.ds(other, quarter)]
    lower = moment(mine[:, quarter:], jnp.concatenate([mine[:, quarter:], near], axis=1))
    left = tokens[:, pl.ds(pl.multiple_of(own + side * quarter, quarter), quarter)]
    right = tokens[:, pl.ds(pl.multiple_of(other + side * quarter, quarter), quarter)]
    return mine, jnp.concatenate([upper, lower]), moment(left, right)


def act_kernel(where, local, far, after, blocks, extra, tokens):
    micro, rows = local.shape[:2]
    for m in range(micro):
        tokens[m * rows:(m + 1) * rows] = local[m]
        tokens[(micro + m) * rows:(micro + m + 1) * rows] = far[m]
    _, main, corner = blocks_of(tokens, where[1])
    blocks[...] = main.astype(BF16)
    extra[...] = corner


def grad_kernel(where, local, far, dh_own, dh_got, act_blocks, act_extra, *refs):
    parts, (inputs, tokens, corners, whole) = refs[:-4], refs[-4:]
    line = len(parts)
    rows, width = local.shape[1:]
    core = where[2]
    inputs[:rows] = local[core]
    inputs[rows:2 * rows] = far[core]
    inputs[2 * rows:3 * rows] = local[1 - core]
    inputs[3 * rows:] = far[1 - core]
    tokens[:2 * rows] = dh_own[...]
    tokens[2 * rows:] = dh_got[...]
    half, quarter = width // 2, width // 4
    mine, main, corner = blocks_of(tokens, where[1])
    whole[:, :half] = act_blocks[...]
    whole[:, half:width] = main.astype(BF16)
    few = quarter // line
    for j in range(line):
        corners[2 * j * few:(2 * j + 1) * few] = act_extra[j * few:(j + 1) * few]
        corners[(2 * j + 1) * few:(2 * j + 2) * few] = corner[j * few:(j + 1) * few]
    whole[:, width:width + quarter] = corners[...].astype(BF16)
    whole[:, width + quarter:] = moment(mine, inputs[...]).astype(BF16)
    for step, part in enumerate(parts):
        count = part.shape[0]
        part[...] = whole[pl.ds(pl.multiple_of((where[0] ^ step) * count, count), count)]


def invert(total, count):
    row = lax.broadcasted_iota(jnp.int32, total.shape, 0)
    column = lax.broadcasted_iota(jnp.int32, total.shape, 1)
    eye = (row == column).astype(F32)
    ridge = 0.01
    mean = total[...].astype(F32) * (1.0 / count)
    full = mean + ridge * eye
    scale = lax.rsqrt(jnp.sum(full * full, keepdims=True))
    squared = product((total[...],), (total[...],)) * (1.0 / count) ** 2 + ridge * (mean + full)
    first = full * scale
    second = 2.0 * first - squared * (scale * scale)
    second_terms = split(second)
    last = 2.0 * (eye - second) + product(second_terms, second_terms)
    tail = 2.0 * last - product(second_terms, split(last))
    return split((2.0 * tail - product(split(first), split(tail))) * scale)


def inverse_kernel(count, where, mine, other, act_high, act_low, out_high, out_low, blocks, corners, act, out):
    line, rows = mine.shape[:2]
    few = rows // 2
    side = where[1]
    half = line * rows
    q = half // 2
    width = 2 * half
    for source, part in enumerate((mine, other)):
        for step in range(line):
            place = where[0] ^ step
            start = pl.multiple_of(place * rows, rows)
            blocks[source, pl.ds(start, rows)] = part[step, :, :width].astype(F32)
            corner = part[step, :, width:].astype(F32)
            start = pl.multiple_of(place * few, few)
            corners[source, 0, pl.ds(start, few)] = corner[:few]
            corners[source, 1, pl.ds(start, few)] = corner[few:]

    for which, total in enumerate((act, out)):
        first = which * half

        def put(row, column, value):
            total[row * q:(row + 1) * q, column * q:(column + 1) * q] = value.astype(BF16)

        def both(row, column, value):
            put(row, column, value)
            put(column, row, value.T)

        for source, at in enumerate((0, 2)):
            put(at, at, blocks[source, :q, first:first + q])
            both(at, at + 1, blocks[source, :q, first + q:first + half])
            put(at + 1, at + 1, blocks[source, q:, first:first + q])
            both(at + 1, (at + 2) % 4, blocks[source, q:, first + q:first + half])
        ours, theirs = corners[0, which], corners[1, which].T
        both(0, 2, jnp.where(side == 0, ours, theirs))
        both(1, 3, jnp.where(side == 0, theirs, ours))

    own = pl.multiple_of(side * half, half)
    away = pl.multiple_of(half - side * half, half)
    for result, term in zip((out_high, out_low), invert(out, count)):
        result[...] = term
    for result, term in zip((act_high, act_low), invert(act, count)):
        for i, a in enumerate((own, away)):
            for j, b in enumerate((own, away)):
                result[pl.ds(a, half), pl.ds(b, half)] = term[i * half:(i + 1) * half, j * half:(j + 1) * half]


def half_update(where, grad, act_inv, out_inv, rows_of, part):
    line, rows = grad.shape[:2]
    for step in range(line):
        start = pl.multiple_of((where[0] ^ step) * rows, rows)
        rows_of[pl.ds(start, rows)] = grad[step]
    half = line * rows
    left = product((rows_of[...],), tuple(term[...] for term in act_inv))
    right = tuple(term[part * half:(part + 1) * half] for term in out_inv)
    return product(split(left), right, ((0,), (0,)))


def own_kernel(where, grad, act_high, act_low, out_high, out_low, result, rows_of):
    result[...] = half_update(where, grad, (act_high, act_low), (out_high, out_low), rows_of, 0)


def update_kernel(where, grad, act_high, act_low, out_high, out_low, own, result, rows_of):
    term = half_update(where, grad, (act_high, act_low), (out_high, out_low), rows_of, 1)
    half = term.shape[1] // 2
    result[:, pl.ds(pl.multiple_of(where[1] * half, half), half)] = own[:, :half] + term[:, :half]
    result[:, pl.ds(pl.multiple_of(half - where[1] * half, half), half)] = own[:, half:] + term[:, half:]


def send(parts):
    line = len(parts)
    got = {0: parts[0]}
    for step in sorted(range(1, line), key=lambda k: (-(k & (line // 2)), k)):
        got[step] = lax.ppermute(parts[step], "line", [(i, i ^ step) for i in range(line)])
    return [got[step] for step in range(line)]


def body(acts, weights, cot_last):
    pairs = lax.axis_size("row")
    line = lax.axis_size("line")
    row = lax.axis_index("row")
    core = lax.axis_index("core")
    side = lax.axis_index("side")
    weight = weights[0]
    local = acts[0]
    micro, rows, width = local.shape
    count = micro * rows * line * 2
    odd = core == 1
    where = jnp.stack([lax.axis_index("line"), side, core, row, pairs]).astype(jnp.int32)

    def mine_of(pair):
        return jnp.where(odd, pair[1], pair[0])

    partner = lax.ppermute(weight, "core", SWAP)
    partner_local = lax.ppermute(local, "core", SWAP)
    far = lax.ppermute(local, "side", SWAP)
    block = jax.ShapeDtypeStruct((rows, width), BF16)
    slope = jax.ShapeDtypeStruct((rows, width), F32)
    square = jax.ShapeDtypeStruct((width, width), BF16)
    own, near_own, last = call(
        load_kernel, 2 * rows * width**2, [square, slope, block], [SMEM] + [VMEM] * 3
    )(where, weight, local, cot_last)
    near_partner, partner_x, down, cross = call(
        first_kernel, 6 * rows * width**2, [slope, block, block, block], [SMEM] + [VMEM] * 5
    )(where, own, partner, near_own, partner_local, last)
    partner_far = lax.ppermute(partner_x, "side", SWAP)
    first = down
    for turn in range(1, pairs):
        straight = [(r, r - 1) for r in range(1, pairs)]
        diagonal = [(2 * r + s, 2 * ((r - 1) % pairs) + 1 - s) for r in range(pairs) for s in range(2)]
        upstream = lax.ppermute(down, "row", straight)
        crossing = lax.ppermute(cross, ("row", "side"), diagonal)
        here = row == pairs - 1 - turn
        if turn == 1:
            near_up, far_up = upstream, crossing
        else:
            near_up = jnp.where(here, upstream, near_up)
            far_up = jnp.where(here, crossing, far_up)
        if turn < pairs - 1:
            cot = layer(upstream, mine_of((near_partner, near_own)), mine_of((partner, own)))[1]
            down = layer(cot, mine_of((near_own, near_partner)), mine_of((own, partner)))[1]
            cross = jnp.where(row == 0, last, down)

    tokens = 2 * micro * rows
    half, quarter = width // 2, width // 4
    act_blocks, act_extra = call(
        act_kernel,
        2 * tokens * half * width,
        [jax.ShapeDtypeStruct((half, half), BF16), jax.ShapeDtypeStruct((quarter, quarter), F32)],
        [SMEM, VMEM, VMEM, ANY],
        [pltpu.VMEM((tokens, width), BF16)],
    )(where, local, far, first)

    far_own, far_partner = call(
        far_kernel, 4 * rows * width**2, [slope, slope], [SMEM] + [VMEM] * 4
    )(where, own, partner, far, partner_far)
    pair = jax.ShapeDtypeStruct((2 * rows, width), BF16)
    own_dh, give_dh, own_cot, give_cot = call(
        layers_kernel,
        8 * rows * width**2,
        [pair, pair, block, block],
        [SMEM] + [VMEM] * 9,
        [pltpu.VMEM((2 * rows, width), BF16)],
    )(where, own, partner, near_own, near_partner, far_own, far_partner, near_up, far_up, last)
    got_dh = lax.ppermute(give_dh, "core", SWAP)
    other_cot = lax.ppermute(give_cot, "core", SWAP)
    cot = jnp.stack([mine_of((own_cot, other_cot)), mine_of((other_cot, own_cot))])

    factors = width + quarter
    parts = call(
        grad_kernel,
        4 * tokens * half * width,
        [jax.ShapeDtypeStruct((half // line, factors + width), BF16)] * line,
        [SMEM] + [VMEM] * 6,
        [
            pltpu.VMEM((tokens, width), BF16),
            pltpu.VMEM((tokens, width), BF16),
            pltpu.VMEM((half, quarter), F32),
            pltpu.VMEM((half, factors + width), BF16),
        ],
    )(where, local, far, own_dh, got_dh, act_blocks, act_extra)
    total = sum(piece.astype(F32) for piece in send(parts)).astype(BF16)
    factors_mine = jnp.stack(send([total[:, :factors]] * line))
    factors_other = lax.ppermute(factors_mine, "side", SWAP)
    grad_mine = jnp.stack(send([total[:, factors:]] * line))
    grad_other = lax.ppermute(grad_mine, "side", SWAP)
    terms = call(
        functools.partial(inverse_kernel, count),
        40 * width**3,
        [square] * 4,
        [SMEM, VMEM, VMEM],
        [
            pltpu.VMEM((2, half, width), F32),
            pltpu.VMEM((2, 2, quarter, quarter), F32),
            pltpu.VMEM((width, width), BF16),
            pltpu.VMEM((width, width), BF16),
        ],
    )(where, factors_mine, factors_other)
    whole = jax.ShapeDtypeStruct((width, width), F32)
    rows_of = [pltpu.VMEM((half, width), BF16)]
    own_term = call(own_kernel, 5 * width**3, whole, [SMEM] + [VMEM] * 5, rows_of)(where, grad_mine, *terms)
    update = call(update_kernel, 5 * width**3, whole, [SMEM] + [VMEM] * 6, rows_of)(
        where, grad_other, *terms, own_term
    )
    return (cot[None], update[None])


def solution(mesh):
    sections, shards = mesh.devices.shape
    finer = Mesh(
        np.reshape(mesh.devices, (sections // 2, 2, shards // 2, 2)),
        ("row", "core", "line", "side"),
    )
    section, dp = ("row", "core"), ("line", "side")
    placed = (P(section, None, dp, None), P(section, None, None), P(None, dp, None))
    return jax.shard_map(
        body,
        mesh=finer,
        in_specs=placed,
        out_specs=(P(section, None, dp, None), P(section, None, None)),
        check_vma=False,
    )
```

```python
import functools

import jax
import jax.numpy as jnp
import numpy as np
from jax import lax
from jax.experimental import pallas as pl
from jax.experimental.pallas import tpu as pltpu
from jax.sharding import Mesh, PartitionSpec as P

BF16 = jnp.bfloat16
F32 = jnp.float32
SWAP = [(0, 1), (1, 0)]
SMEM = pl.BlockSpec(memory_space=pltpu.SMEM)
VMEM = pl.BlockSpec(memory_space=pltpu.VMEM)
ANY = pl.BlockSpec(memory_space=pl.ANY)
GROUP = 4


def silu_slope(pre):
    sig = jax.nn.sigmoid(pre)
    return sig * (1.0 + pre * (1.0 - sig))


def slope_of(inputs, matrix):
    return silu_slope(jnp.dot(inputs, matrix, preferred_element_type=F32))


def layer(upstream, slope, matrix):
    dh = (upstream.astype(F32) * slope).astype(BF16)
    back = lax.dot_general(dh, matrix, (((1,), (1,)), ((), ())), preferred_element_type=F32)
    return dh, (upstream.astype(F32) + back).astype(BF16)


def by_core(core, run, own, partner):
    @pl.when(core == 1)
    def _():
        run(own, partner)

    @pl.when(core == 0)
    def _():
        run(partner, own)


def moment(left, right):
    return lax.dot_general(left, right, (((0,), (0,)), ((), ())), preferred_element_type=F32)


def split(value):
    high = value.astype(BF16)
    return high, (value - high.astype(F32)).astype(BF16)


def product(left, right, dims=((1,), (0,))):
    def dot(a, b):
        return lax.dot_general(a, b, (dims, ((), ())), preferred_element_type=F32)

    total = dot(left[0], right[0])
    if len(right) > 1:
        total += dot(left[0], right[1])
    if len(left) > 1:
        total += dot(left[1], right[0])
    return total


def call(kernel, flops, out_shape, in_specs, scratch=()):
    return pl.pallas_call(
        kernel,
        out_shape=jax.tree.map(lambda v: jax.ShapeDtypeStruct(v.shape, v.dtype), out_shape),
        in_specs=in_specs,
        out_specs=jax.tree.map(lambda _: VMEM, out_shape),
        scratch_shapes=list(scratch),
        cost_estimate=pl.CostEstimate(flops=flops, bytes_accessed=1 << 20, transcendentals=0),
        compiler_params=pltpu.CompilerParams(vmem_limit_bytes=32 << 20),
    )


def load_kernel(where, weight, local, cot_last, weight_copy, local_copy, slope, cot, done):
    core = where[0]
    copies = [
        pltpu.make_async_copy(source, target, done.at[i])
        for i, (source, target) in enumerate(
            ((weight, weight_copy), (local, local_copy), (cot_last.at[core], cot))
        )
    ]
    for copy in copies:
        copy.start()
    for copy in copies:
        copy.wait()
    slope[...] = slope_of(local_copy[core], weight_copy[...])


def first_kernel(where, own, partner, slope_own, local, upstream, slope_partner, down):
    slope_partner[...] = slope_of(local[where[0]], partner[...])

    def run(odd, even):
        cot = layer(upstream[...], odd[1][...], odd[0][...])[1]
        down[...] = layer(cot, even[1][...], even[0][...])[1]

    by_core(where[0], run, (own, slope_own), (partner, slope_partner))


def odd_kernel(where, own, partner, slope_own, slope_partner, arrived, last, dh, cot):
    upstream = jnp.where(where[2] == 1, last[...], arrived[...])

    def run(odd, even):
        dh[...], cot[...] = layer(upstream, odd[1][...], odd[0][...])

    by_core(where[0], run, (own, slope_own), (partner, slope_partner))


def even_kernel(
    where, own, partner, slope_own, slope_partner, dh, cot, after, own_dh, give_dh, own_cot, give_cot
):
    def run(odd, even):
        odd[2][...], odd[3][...] = dh[...], cot[...]
        even[2][...], even[3][...] = layer(cot[...], even[1][...], even[0][...])

    by_core(
        where[0], run, (own, slope_own, own_dh, own_cot), (partner, slope_partner, give_dh, give_cot)
    )


def put_factor(tokens, whole):
    width = tokens.shape[1]
    size = width // GROUP
    half = size // 2
    columns = [tokens[:, u * size:(u + 1) * size] for u in range(GROUP)]
    for u in range(GROUP):
        pair = jnp.concatenate([columns[u], columns[(u + 1) % GROUP]], axis=1)
        main = moment(columns[u], pair).astype(BF16)
        whole[u, :, :2 * size] = main[:half]
        whole[u, :, 2 * size:4 * size] = main[half:]
    for u in range(2):
        corner = moment(columns[u], columns[u + 2]).astype(BF16)
        whole[u, :, 4 * size:5 * size] = corner[:half]
        whole[u + 2, :, 4 * size:5 * size] = corner[half:]


def act_kernel(where, local, after, *refs):
    parts, (tokens, whole) = refs[:GROUP], refs[GROUP:]
    micro, rows = local.shape[:2]
    for m in range(micro):
        tokens[m * rows:(m + 1) * rows] = local[m]
    put_factor(tokens, whole)
    for step, part in enumerate(parts):
        part[...] = whole[where[1] ^ step]


def add_kernel(left, right, after, result):
    result[...] = (left[...].astype(F32) + right[...].astype(F32)).astype(BF16)


def begin_kernel(left, right, result):
    result[...] = left[...].astype(F32) + right[...].astype(F32)


def sum_kernel(*refs):
    pieces, result = refs[:GROUP], refs[-1]
    result[...] = sum(piece[...].astype(F32) for piece in pieces).astype(BF16)


def grad_kernel(where, local, dh_own, dh_got, *refs):
    parts, (inputs, tokens, whole) = refs[:GROUP], refs[GROUP:]
    rows, width = local.shape[1:]
    inputs[:rows] = local[where[0]]
    inputs[rows:] = local[1 - where[0]]
    tokens[:rows] = dh_own[...]
    tokens[rows:] = dh_got[...]
    put_factor(tokens, whole)
    size = width // GROUP
    half = size // 2
    for u in range(GROUP):
        grad = moment(tokens[:, u * size:(u + 1) * size], inputs[...]).astype(BF16)
        whole[u, :, 5 * size:5 * size + width] = grad[:half]
        whole[u, :, 5 * size + width:] = grad[half:]
    for step, part in enumerate(parts):
        part[...] = whole[where[1] ^ step]


def invert(total, count):
    row = lax.broadcasted_iota(jnp.int32, total.shape, 0)
    column = lax.broadcasted_iota(jnp.int32, total.shape, 1)
    eye = (row == column).astype(F32)
    ridge = 0.01
    mean = total[...].astype(F32) * (1.0 / count)
    full = mean + ridge * eye
    scale = lax.rsqrt(jnp.sum(full * full, keepdims=True))
    squared = product((total[...],), (total[...],)) * (1.0 / count) ** 2 + ridge * (mean + full)
    first = full * scale
    second = 2.0 * first - squared * (scale * scale)
    second_terms = split(second)
    last = 2.0 * (eye - second) + product(second_terms, second_terms)
    tail = 2.0 * last - product(second_terms, split(last))
    return split((2.0 * tail - product(split(first), split(tail))) * scale)

def inverse_kernel(count, where, *refs):
    pieces, (high, low, blocks, total) = refs[:GROUP], refs[GROUP:]
    for step, piece in enumerate(pieces):
        blocks[where[1] ^ step] = piece[...].astype(F32)
    size = total.shape[0] // GROUP

    def both(row, column, value):
        total[row * size:(row + 1) * size, column * size:(column + 1) * size] = value.astype(BF16)
        if row != column:
            total[column * size:(column + 1) * size, row * size:(row + 1) * size] = value.T.astype(BF16)

    for u in range(GROUP):
        main = jnp.concatenate([blocks[u, :, :2 * size], blocks[u, :, 2 * size:4 * size]])
        both(u, u, main[:, :size])
        both(u, (u + 1) % GROUP, main[:, size:])
    for u in range(2):
        both(u, u + 2, jnp.concatenate([blocks[u, :, 4 * size:], blocks[u + 2, :, 4 * size:]]))
    for result, term in zip((high, low), invert(total, count)):
        result[...] = term


def update_kernel(where, act_high, act_low, out_high, out_low, *refs):
    pieces, (result, grad) = refs[:GROUP], refs[GROUP:]
    half, twice = pieces[0].shape
    width = twice // 2
    for step, piece in enumerate(pieces):
        start = pl.multiple_of((where[1] ^ step) * 2 * half, 2 * half)
        grad[pl.ds(start, half)] = piece[:, :width]
        grad[pl.ds(start + half, half)] = piece[:, width:]
    left = product((grad[...],), (act_high[...], act_low[...]))
    result[...] = product(split(left), (out_high[...], out_low[...]), ((0,), (0,)))


def send(parts):
    got = {0: parts[0]}
    for step in (3, 1, 2):
        got[step] = lax.ppermute(parts[step], ("near", "side"), [(i, i ^ step) for i in range(GROUP)])
    return [got[step] for step in range(GROUP)]


def exchange(value, after=None):
    step = 1
    while step < lax.axis_size("far"):
        route = [(i, i ^ step) for i in range(lax.axis_size("far"))]
        got = lax.ppermute(value, "far", route)
        if after is None:
            value = (value.astype(F32) + got.astype(F32)).astype(BF16)
        else:
            value = call(add_kernel, 0, value, [VMEM, VMEM, ANY])(value, got, after)
        step *= 2
    return value


def body(acts, weights, cot_last):
    pairs = lax.axis_size("row")
    row = lax.axis_index("row")
    core = lax.axis_index("core")
    weight = weights[0]
    local = acts[0]
    micro, rows, width = local.shape
    tokens = micro * rows
    count = tokens * GROUP * lax.axis_size("far")
    odd = core == 1
    top = row == pairs - 1
    where = jnp.stack([core, lax.axis_index(("near", "side")), top.astype(jnp.int32)]).astype(jnp.int32)

    def mine_of(pair):
        return jnp.where(odd, pair[1], pair[0])

    def array(*shape, dtype=BF16):
        return jax.ShapeDtypeStruct(shape, dtype)

    partner = lax.ppermute(weight, "core", SWAP)
    partner_local = lax.ppermute(local, "core", SWAP)
    block = array(rows, width)
    slope = array(rows, width, dtype=F32)
    own, kept, slope_own, last = call(
        load_kernel,
        2 * rows * width**2,
        [array(width, width), array(micro, rows, width), slope, block],
        [SMEM] + [ANY] * 3,
        [pltpu.SemaphoreType.DMA((3,))],
    )(where, weight, local, cot_last)
    slope_partner, down = call(first_kernel, 6 * rows * width**2, [slope, block], [SMEM] + [VMEM] * 5)(
        where, own, partner, slope_own, partner_local, last
    )
    first = down
    for turn in range(1, pairs):
        upstream = lax.ppermute(down, "row", [(r, r - 1) for r in range(1, pairs)])
        arrived = upstream if turn == 1 else jnp.where(row == pairs - 1 - turn, upstream, arrived)
        if turn < pairs - 1:
            cot = layer(upstream, mine_of((slope_partner, slope_own)), mine_of((partner, own)))[1]
            down = layer(cot, mine_of((slope_own, slope_partner)), mine_of((own, partner)))[1]

    size = width // GROUP
    factor = 5 * size
    act_parts = call(
        act_kernel,
        2 * tokens * width**2,
        [array(size // 2, factor)] * GROUP,
        [SMEM, VMEM, ANY],
        [pltpu.VMEM((tokens, width), BF16), pltpu.VMEM((GROUP, size // 2, factor), BF16)],
    )(where, kept, first)
    act_pieces = send(act_parts)

    dh_odd, cot_odd = call(odd_kernel, 64 * rows * width**2, [block] * 2, [SMEM] + [VMEM] * 6)(
        where, own, partner, slope_own, slope_partner, arrived, last
    )
    act_part = call(sum_kernel, 0, array(size // 2, factor), [VMEM] * GROUP + [ANY])(*act_pieces, cot_odd)
    own_dh, give_dh, own_cot, give_cot = call(
        even_kernel, 4 * rows * width**2, [block] * 4, [SMEM] + [VMEM] * 6 + [ANY]
    )(where, own, partner, slope_own, slope_partner, dh_odd, cot_odd, act_part)
    got_dh = lax.ppermute(give_dh, "core", SWAP)
    other_cot = lax.ppermute(give_cot, "core", SWAP)
    cot = jnp.stack([mine_of((own_cot, other_cot)), mine_of((other_cot, own_cot))])

    parts = call(
        grad_kernel,
        4 * tokens * width**2,
        [array(size // 2, factor + 2 * width)] * GROUP,
        [SMEM] + [VMEM] * 3,
        [pltpu.VMEM((tokens, width), BF16)] * 2
        + [pltpu.VMEM((GROUP, size // 2, factor + 2 * width), BF16)],
    )(where, kept, own_dh, got_dh)
    pieces = send(parts)
    begun = call(
        begin_kernel, 0, array(*parts[0].shape, dtype=F32), [VMEM] * 2
    )(pieces[0], pieces[3])
    total = (begun + pieces[1].astype(F32) + pieces[2].astype(F32)).astype(BF16)
    act = send([exchange(act_part, begun)] * GROUP)
    def inverse(pieces):
        return call(
            functools.partial(inverse_kernel, count),
            20 * width**3,
            [array(width, width)] * 2,
            [SMEM] + [VMEM] * GROUP,
            [pltpu.VMEM((GROUP, size // 2, factor), F32), pltpu.VMEM((width, width), BF16)],
        )(where, *pieces)

    act_inv = inverse(act)
    total = exchange(total, act_inv[0])
    out = send([total[:, :factor]] * GROUP)
    grad = send([total[:, factor:]] * GROUP)
    update = call(
        update_kernel,
        10 * width**3,
        array(width, width, dtype=F32),
        [SMEM] + [VMEM] * (4 + GROUP),
        [pltpu.VMEM((width, width), BF16)],
    )(where, *act_inv, *inverse(out), *grad)
    return (cot[None], update[None])


def solution(mesh):
    sections, shards = mesh.devices.shape
    finer = Mesh(
        np.reshape(mesh.devices, (sections // 2, 2, shards // GROUP, 2, 2)),
        ("row", "core", "far", "near", "side"),
    )
    section, dp = ("row", "core"), ("far", "near", "side")
    placed = (P(section, None, dp, None), P(section, None, None), P(None, dp, None))
    return jax.shard_map(
        body,
        mesh=finer,
        in_specs=placed,
        out_specs=(P(section, None, dp, None), P(section, None, None)),
        check_vma=False,
    )
```

```python
import functools

import jax
import jax.numpy as jnp
import numpy as np
from jax import lax
from jax.experimental import pallas as pl
from jax.experimental.pallas import tpu as pltpu
from jax.sharding import Mesh, PartitionSpec as P

BF16 = jnp.bfloat16
F32 = jnp.float32
SWAP = [(0, 1), (1, 0)]
SMEM = pl.BlockSpec(memory_space=pltpu.SMEM)
VMEM = pl.BlockSpec(memory_space=pltpu.VMEM)
ANY = pl.BlockSpec(memory_space=pl.ANY)
HBM = pl.BlockSpec(memory_space=pltpu.HBM)
GROUP = 4


def silu_slope(pre):
    sig = jax.nn.sigmoid(pre)
    return sig * (1.0 + pre * (1.0 - sig))


def slope_of(inputs, matrix):
    return silu_slope(jnp.dot(inputs, matrix, preferred_element_type=F32))


def layer(upstream, slope, matrix):
    dh = (upstream.astype(F32) * slope).astype(BF16)
    back = lax.dot_general(dh, matrix, (((1,), (1,)), ((), ())), preferred_element_type=F32)
    return dh, (upstream.astype(F32) + back).astype(BF16)


def by_core(core, run, own, partner):
    @pl.when(core == 1)
    def _():
        run(own, partner)

    @pl.when(core == 0)
    def _():
        run(partner, own)


def moment(left, right):
    return lax.dot_general(left, right, (((0,), (0,)), ((), ())), preferred_element_type=F32)


def split(value):
    high = value.astype(BF16)
    return high, (value - high.astype(F32)).astype(BF16)


def product(left, right, dims=((1,), (0,))):
    def dot(a, b):
        return lax.dot_general(a, b, (dims, ((), ())), preferred_element_type=F32)

    total = dot(left[0], right[0])
    if len(right) > 1:
        total += dot(left[0], right[1])
    if len(left) > 1:
        total += dot(left[1], right[0])
    return total


def call(kernel, flops, out_shape, in_specs, scratch=(), out_spec=VMEM):
    return pl.pallas_call(
        kernel,
        out_shape=jax.tree.map(lambda v: jax.ShapeDtypeStruct(v.shape, v.dtype), out_shape),
        in_specs=in_specs,
        out_specs=jax.tree.map(lambda _: out_spec, out_shape),
        scratch_shapes=list(scratch),
        cost_estimate=pl.CostEstimate(flops=flops, bytes_accessed=1 << 20, transcendentals=0),
        compiler_params=pltpu.CompilerParams(vmem_limit_bytes=32 << 20),
    )


def load_kernel(where, weight, local, cot_last, weight_copy, local_copy, slope, cot, done):
    core = where[0]
    copies = [
        pltpu.make_async_copy(source, target, done.at[i])
        for i, (source, target) in enumerate(
            ((weight, weight_copy), (local, local_copy), (cot_last.at[core], cot))
        )
    ]
    for copy in copies:
        copy.start()
    for copy in copies:
        copy.wait()
    slope[...] = slope_of(local_copy[core], weight_copy[...])


def first_kernel(where, own, partner, slope_own, local, upstream, slope_partner, down):
    slope_partner[...] = slope_of(local[where[0]], partner[...])

    def run(odd, even):
        cot = layer(upstream[...], odd[1][...], odd[0][...])[1]
        down[...] = layer(cot, even[1][...], even[0][...])[1]

    by_core(where[0], run, (own, slope_own), (partner, slope_partner))


def odd_kernel(where, own, partner, slope_own, slope_partner, arrived, last, dh, cot):
    upstream = jnp.where(where[2] == 1, last[...], arrived[...])

    def run(odd, even):
        dh[...], cot[...] = layer(upstream, odd[1][...], odd[0][...])

    by_core(where[0], run, (own, slope_own), (partner, slope_partner))


def sum_kernel(*refs):
    pieces, result = refs[:GROUP], refs[-1]
    result[...] = sum(piece[...].astype(F32) for piece in pieces).astype(BF16)


def even_kernel(
    where, own, partner, slope_own, slope_partner, dh, cot, after, own_dh, give_dh, own_cot, give_cot
):
    def run(odd, even):
        odd[2][...], odd[3][...] = dh[...], cot[...]
        even[2][...], even[3][...] = layer(cot[...], even[1][...], even[0][...])

    by_core(
        where[0], run, (own, slope_own, own_dh, own_cot), (partner, slope_partner, give_dh, give_cot)
    )


def cot_kernel(where, own_cot, other_cot, result):
    result[where[0]] = own_cot[...]
    result[1 - where[0]] = other_cot[...]


def put_factor(tokens, whole):
    width = tokens.shape[1]
    size = width // GROUP
    half = size // 2
    columns = [tokens[:, u * size:(u + 1) * size] for u in range(GROUP)]
    for u in range(GROUP):
        pair = jnp.concatenate([columns[u], columns[(u + 1) % GROUP]], axis=1)
        main = moment(columns[u], pair).astype(BF16)
        whole[u, :, :2 * size] = main[:half]
        whole[u, :, 2 * size:4 * size] = main[half:]
    for u in range(2):
        corner = moment(columns[u], columns[u + 2]).astype(BF16)
        whole[u, :, 4 * size:5 * size] = corner[:half]
        whole[u + 2, :, 4 * size:5 * size] = corner[half:]


def act_kernel(where, local, after, *refs):
    parts, (tokens, whole) = refs[:GROUP], refs[GROUP:]
    micro, rows = local.shape[:2]
    for m in range(micro):
        tokens[m * rows:(m + 1) * rows] = local[m]
    put_factor(tokens, whole)
    for step, part in enumerate(parts):
        part[...] = whole[where[1] ^ step]


def add_kernel(left, right, *refs):
    refs[-1][...] = (left[...].astype(F32) + right[...].astype(F32)).astype(BF16)


def begin_kernel(left, right, after, result):
    result[...] = left[...].astype(F32) + right[...].astype(F32)


def grad_kernel(where, local, dh_own, dh_got, act_sum, *refs):
    parts, (act_part, inputs, tokens, whole) = refs[:GROUP], refs[GROUP:]
    act_part[...] = act_sum[...]
    rows, width = local.shape[1:]
    inputs[:rows] = local[where[0]]
    inputs[rows:] = local[1 - where[0]]
    tokens[:rows] = dh_own[...]
    tokens[rows:] = dh_got[...]
    put_factor(tokens, whole)
    size = width // GROUP
    half = size // 2
    for u in range(GROUP):
        grad = moment(inputs[:, u * size:(u + 1) * size], tokens[...]).astype(BF16)
        whole[u, :, 5 * size:5 * size + width] = grad[:half]
        whole[u, :, 5 * size + width:] = grad[half:]
    for step, part in enumerate(parts):
        part[...] = whole[where[1] ^ step]


def invert(total, count):
    row = lax.broadcasted_iota(jnp.int32, total.shape, 0)
    column = lax.broadcasted_iota(jnp.int32, total.shape, 1)
    eye = (row == column).astype(F32)
    ridge = 0.01
    mean = total[...].astype(F32) * (1.0 / count)
    full = mean + ridge * eye
    scale = lax.rsqrt(jnp.sum(full * full, keepdims=True))
    squared = product((total[...],), (total[...],)) * (1.0 / count) ** 2 + ridge * (mean + full)
    second = (2.0 * scale) * full - squared * (scale * scale)
    second_terms = split(second)
    last = 2.0 * (eye - second) + product(second_terms, second_terms)
    tail = 2.0 * last - product(second_terms, split(last))
    inner = product((total[...],), split(tail)) * (scale * (1.0 / count))
    return split(((2.0 - ridge * scale) * tail - inner) * scale)

def inverse_kernel(count, where, *refs):
    pieces, (high, low, blocks, total) = refs[:GROUP], refs[GROUP:]
    for step, piece in enumerate(pieces):
        blocks[where[1] ^ step] = piece[...].astype(F32)
    size = total.shape[0] // GROUP

    def both(row, column, value):
        total[row * size:(row + 1) * size, column * size:(column + 1) * size] = value.astype(BF16)
        if row != column:
            total[column * size:(column + 1) * size, row * size:(row + 1) * size] = value.T.astype(BF16)

    for u in range(GROUP):
        main = jnp.concatenate([blocks[u, :, :2 * size], blocks[u, :, 2 * size:4 * size]])
        both(u, u, main[:, :size])
        both(u, (u + 1) % GROUP, main[:, size:])
    for u in range(2):
        both(u, u + 2, jnp.concatenate([blocks[u, :, 4 * size:], blocks[u + 2, :, 4 * size:]]))
    for result, term in zip((high, low), invert(total, count)):
        result[...] = term


def update_kernel(where, act_high, act_low, out_high, out_low, *refs):
    pieces, (result, grad, update, done) = refs[:GROUP], refs[GROUP:]
    half, twice = pieces[0].shape
    width = twice // 2
    for step, piece in enumerate(pieces):
        start = pl.multiple_of((where[1] ^ step) * 2 * half, 2 * half)
        grad[pl.ds(start, half)] = piece[:, :width]
        grad[pl.ds(start + half, half)] = piece[:, width:]
    copies = []
    for u in range(GROUP):
        rows = pl.ds(u * 2 * half, 2 * half)
        left = product((act_high[rows], act_low[rows]), (grad[...],))
        update[rows] = product(split(left), (out_high[...], out_low[...]))
        copies.append(pltpu.make_async_copy(update.at[rows], result.at[rows], done.at[u]))
        copies[-1].start()
    for copy in copies:
        copy.wait()


def send(parts):
    got = {0: parts[0]}
    for step in (3, 1, 2):
        got[step] = lax.ppermute(parts[step], ("near", "side"), [(i, i ^ step) for i in range(GROUP)])
    return [got[step] for step in range(GROUP)]


def exchange(value, after=None):
    step = 1
    while step < lax.axis_size("far"):
        route = [(i, i ^ step) for i in range(lax.axis_size("far"))]
        got = lax.ppermute(value, "far", route)
        if after is None:
            value = (value.astype(F32) + got.astype(F32)).astype(BF16)
        else:
            value = call(add_kernel, 0, value, [VMEM] * 2 + [ANY] * len(after))(value, got, *after)
        step *= 2
    return value


def body(acts, weights, cot_last):
    pairs = lax.axis_size("row")
    row = lax.axis_index("row")
    core = lax.axis_index("core")
    weight = weights[0]
    local = acts[0]
    micro, rows, width = local.shape
    tokens = micro * rows
    count = tokens * GROUP * lax.axis_size("far")
    odd = core == 1
    top = row == pairs - 1
    where = jnp.stack([core, lax.axis_index(("near", "side")), top.astype(jnp.int32)]).astype(jnp.int32)

    def mine_of(pair):
        return jnp.where(odd, pair[1], pair[0])

    def array(*shape, dtype=BF16):
        return jax.ShapeDtypeStruct(shape, dtype)

    partner = lax.ppermute(weight, "core", SWAP)
    partner_local = lax.ppermute(local, "core", SWAP)
    block = array(rows, width)
    slope = array(rows, width, dtype=F32)
    own, kept, slope_own, last = call(
        load_kernel,
        2 * rows * width**2,
        [array(width, width), array(micro, rows, width), slope, block],
        [SMEM] + [HBM] * 3,
        [pltpu.SemaphoreType.DMA((3,))],
    )(where, weight, local, cot_last)
    slope_partner, down = call(first_kernel, 6 * rows * width**2, [slope, block], [SMEM] + [VMEM] * 5)(
        where, own, partner, slope_own, partner_local, last
    )
    first = down
    for turn in range(1, pairs):
        upstream = lax.ppermute(down, "row", [(r, r - 1) for r in range(1, pairs)])
        arrived = upstream if turn == 1 else jnp.where(row == pairs - 1 - turn, upstream, arrived)
        if turn < pairs - 1:
            cot = layer(upstream, mine_of((slope_partner, slope_own)), mine_of((partner, own)))[1]
            down = layer(cot, mine_of((slope_own, slope_partner)), mine_of((own, partner)))[1]

    size = width // GROUP
    factor = 5 * size
    act_parts = call(
        act_kernel,
        2 * tokens * width**2,
        [array(size // 2, factor)] * GROUP,
        [SMEM, VMEM, ANY],
        [pltpu.VMEM((tokens, width), BF16), pltpu.VMEM((GROUP, size // 2, factor), BF16)],
    )(where, kept, first)
    act_pieces = send(act_parts)

    dh_odd, cot_odd = call(odd_kernel, 64 * rows * width**2, [block] * 2, [SMEM] + [VMEM] * 6)(
        where, own, partner, slope_own, slope_partner, arrived, last
    )
    act_sum = call(sum_kernel, 0, array(size // 2, factor), [VMEM] * GROUP + [ANY])(
        *(act_pieces[step] for step in (0, 3, 1, 2)), cot_odd
    )
    own_dh, give_dh, own_cot, give_cot = call(
        even_kernel, 4 * rows * width**2, [block] * 4, [SMEM] + [VMEM] * 6 + [ANY]
    )(where, own, partner, slope_own, slope_partner, dh_odd, cot_odd, act_sum)
    got_dh = lax.ppermute(give_dh, "core", SWAP)
    other_cot = lax.ppermute(give_cot, "core", SWAP)
    cot = call(cot_kernel, 0, array(micro, rows, width), [SMEM, VMEM, VMEM])(where, own_cot, other_cot)

    *parts, act_part = call(
        grad_kernel,
        4 * tokens * width**2,
        [array(size // 2, factor + 2 * width)] * GROUP + [array(size // 2, factor)],
        [SMEM] + [VMEM] * 4,
        [pltpu.VMEM((tokens, width), BF16)] * 2
        + [pltpu.VMEM((GROUP, size // 2, factor + 2 * width), BF16)],
    )(where, kept, own_dh, got_dh, act_sum)
    pieces = send(parts)
    begun = call(begin_kernel, 0, array(*parts[0].shape, dtype=F32), [VMEM] * 2 + [ANY])(
        pieces[0], pieces[3], cot
    )
    total = (begun + pieces[1].astype(F32) + pieces[2].astype(F32)).astype(BF16)
    act = send([exchange(act_part, (begun,))] * GROUP)

    def inverse(pieces):
        return call(
            functools.partial(inverse_kernel, count),
            20 * width**3,
            [array(width, width)] * 2,
            [SMEM] + [VMEM] * GROUP,
            [pltpu.VMEM((GROUP, size // 2, factor), F32), pltpu.VMEM((width, width), BF16)],
        )(where, *pieces)

    act_inv = inverse(act)
    total = exchange(total, (act_inv[0],))
    out = send([total[:, :factor]] * GROUP)
    grad = send([total[:, factor:]] * GROUP)
    update = call(
        update_kernel,
        10 * width**3,
        array(width, width, dtype=F32),
        [SMEM] + [VMEM] * (4 + GROUP),
        [
            pltpu.VMEM((width, width), BF16),
            pltpu.VMEM((width, width), F32),
            pltpu.SemaphoreType.DMA((GROUP,)),
        ],
        HBM,
    )(where, *act_inv, *inverse(out), *grad)
    return (cot[None], update[None])


def solution(mesh):
    sections, shards = mesh.devices.shape
    finer = Mesh(
        np.reshape(mesh.devices, (sections // 2, 2, shards // GROUP, 2, 2)),
        ("row", "core", "far", "near", "side"),
    )
    section, dp = ("row", "core"), ("far", "near", "side")
    placed = (P(section, None, dp, None), P(section, None, None), P(None, dp, None))
    return jax.shard_map(
        body,
        mesh=finer,
        in_specs=placed,
        out_specs=(P(section, None, dp, None), P(section, None, None)),
        check_vma=False,
    )
```

```python
import functools

import jax
import jax.numpy as jnp
import numpy as np
from jax import lax
from jax.experimental import pallas as pl
from jax.experimental.pallas import tpu as pltpu
from jax.sharding import Mesh, PartitionSpec as P

BF16 = jnp.bfloat16
F32 = jnp.float32
SWAP = [(0, 1), (1, 0)]
SMEM = pl.BlockSpec(memory_space=pltpu.SMEM)
VMEM = pl.BlockSpec(memory_space=pltpu.VMEM)
ANY = pl.BlockSpec(memory_space=pl.ANY)
HBM = pl.BlockSpec(memory_space=pltpu.HBM)
GROUP = 4


def silu_slope(pre):
    sig = jax.nn.sigmoid(pre)
    return sig * (1.0 + pre * (1.0 - sig))


def slope_of(inputs, matrix):
    return silu_slope(jnp.dot(inputs, matrix, preferred_element_type=F32))


def layer(upstream, slope, matrix):
    dh = (upstream.astype(F32) * slope).astype(BF16)
    back = lax.dot_general(dh, matrix, (((1,), (1,)), ((), ())), preferred_element_type=F32)
    return dh, (upstream.astype(F32) + back).astype(BF16)


def by_core(core, run, own, partner):
    @pl.when(core == 1)
    def _():
        run(own, partner)

    @pl.when(core == 0)
    def _():
        run(partner, own)


def moment(left, right):
    return lax.dot_general(left, right, (((0,), (0,)), ((), ())), preferred_element_type=F32)


def split(value):
    high = value.astype(BF16)
    return high, (value - high.astype(F32)).astype(BF16)


def product(left, right, dims=((1,), (0,))):
    def dot(a, b):
        return lax.dot_general(a, b, (dims, ((), ())), preferred_element_type=F32)

    total = dot(left[0], right[0])
    if len(right) > 1:
        total += dot(left[0], right[1])
    if len(left) > 1:
        total += dot(left[1], right[0])
    return total


def call(kernel, flops, out_shape, in_specs, scratch=(), out_spec=VMEM):
    return pl.pallas_call(
        kernel,
        out_shape=jax.tree.map(lambda v: jax.ShapeDtypeStruct(v.shape, v.dtype), out_shape),
        in_specs=in_specs,
        out_specs=jax.tree.map(lambda _: out_spec, out_shape),
        scratch_shapes=list(scratch),
        cost_estimate=pl.CostEstimate(flops=flops, bytes_accessed=1 << 20, transcendentals=0),
        compiler_params=pltpu.CompilerParams(vmem_limit_bytes=32 << 20),
    )


def first_kernel(
    where, weight, local, cot_last, partner, partner_local,
    own, kept, last, slope_own, slope_partner, down,
):
    core = where[0]
    last[...] = cot_last[core]
    slope_own[...] = slope_of(local[core], weight[...])
    slope_partner[...] = slope_of(partner_local[core], partner[...])

    def run(odd, even):
        cot = layer(last[...], odd[1][...], odd[0][...])[1]
        down[...] = layer(cot, even[1][...], even[0][...])[1]

    by_core(core, run, (weight, slope_own), (partner, slope_partner))
    own[...] = weight[...]
    kept[...] = local[...]


def odd_kernel(where, own, partner, slope_own, slope_partner, arrived, last, dh, cot):
    upstream = jnp.where(where[2] == 1, last[...], arrived[...])

    def run(odd, even):
        dh[...], cot[...] = layer(upstream, odd[1][...], odd[0][...])

    by_core(where[0], run, (own, slope_own), (partner, slope_partner))


def sum_kernel(*refs):
    pieces, result = refs[:GROUP], refs[-1]
    result[...] = sum(piece[...].astype(F32) for piece in pieces).astype(BF16)


def even_kernel(
    where, own, partner, slope_own, slope_partner, dh, cot, after, own_dh, give_dh, own_cot, give_cot
):
    def run(odd, even):
        odd[2][...], odd[3][...] = dh[...], cot[...]
        even[2][...], even[3][...] = layer(cot[...], even[1][...], even[0][...])

    by_core(
        where[0], run, (own, slope_own, own_dh, own_cot), (partner, slope_partner, give_dh, give_cot)
    )


def cot_kernel(where, own_cot, other_cot, after, result):
    result[where[0]] = own_cot[...]
    result[1 - where[0]] = other_cot[...]


def put_factor(tokens, whole):
    width = tokens.shape[1]
    size = width // GROUP
    half = size // 2
    columns = [tokens[:, u * size:(u + 1) * size] for u in range(GROUP)]
    for u in range(GROUP):
        pair = jnp.concatenate([columns[u], columns[(u + 1) % GROUP]], axis=1)
        main = moment(columns[u], pair).astype(BF16)
        whole[u, :, :2 * size] = main[:half]
        whole[u, :, 2 * size:4 * size] = main[half:]
    for u in range(2):
        corner = moment(columns[u], columns[u + 2]).astype(BF16)
        whole[u, :, 4 * size:5 * size] = corner[:half]
        whole[u + 2, :, 4 * size:5 * size] = corner[half:]


def act_kernel(where, local, after, *refs):
    parts, (tokens, whole) = refs[:GROUP], refs[GROUP:]
    micro, rows = local.shape[:2]
    for m in range(micro):
        tokens[m * rows:(m + 1) * rows] = local[m]
    put_factor(tokens, whole)
    for step, part in enumerate(parts):
        part[...] = whole[where[1] ^ step]


def add_kernel(left, right, *refs):
    refs[-1][...] = (left[...].astype(F32) + right[...].astype(F32)).astype(BF16)


def begin_kernel(left, right, act, result, act_copy):
    act_copy[...] = act[...]
    result[...] = left[...].astype(F32) + right[...].astype(F32)


def grad_kernel(where, local, dh_own, dh_got, *refs):
    parts, (inputs, tokens, whole) = refs[:GROUP], refs[GROUP:]
    rows, width = local.shape[1:]
    inputs[:rows] = local[where[0]]
    inputs[rows:] = local[1 - where[0]]
    tokens[:rows] = dh_own[...]
    tokens[rows:] = dh_got[...]
    put_factor(tokens, whole)
    size = width // GROUP
    half = size // 2
    for u in range(GROUP):
        grad = moment(inputs[:, u * size:(u + 1) * size], tokens[...]).astype(BF16)
        whole[u, :, 5 * size:5 * size + width] = grad[:half]
        whole[u, :, 5 * size + width:] = grad[half:]
    for step, part in enumerate(parts):
        part[...] = whole[where[1] ^ step]


def invert(total, count):
    row = lax.broadcasted_iota(jnp.int32, total.shape, 0)
    column = lax.broadcasted_iota(jnp.int32, total.shape, 1)
    eye = (row == column).astype(F32)
    ridge = 0.01
    mean = total[...].astype(F32) * (1.0 / count)
    full = mean + ridge * eye
    scale = lax.rsqrt(jnp.sum(full * full, keepdims=True))
    squared = product((total[...],), (total[...],)) * (1.0 / count) ** 2 + ridge * (mean + full)
    second = (2.0 * scale) * full - squared * (scale * scale)
    second_terms = split(second)
    last = 2.0 * (eye - second) + product(second_terms, second_terms)
    tail = 2.0 * last - product(second_terms, split(last))
    inner = product((total[...],), split(tail)) * (scale * (1.0 / count))
    return split(((2.0 - ridge * scale) * tail - inner) * scale)

def inverse_kernel(count, where, *refs):
    pieces, (high, low, blocks, total) = refs[:GROUP], refs[GROUP:]
    for step, piece in enumerate(pieces):
        blocks[where[1] ^ step] = piece[...].astype(F32)
    size = total.shape[0] // GROUP

    def both(row, column, value):
        total[row * size:(row + 1) * size, column * size:(column + 1) * size] = value.astype(BF16)
        if row != column:
            total[column * size:(column + 1) * size, row * size:(row + 1) * size] = value.T.astype(BF16)

    for u in range(GROUP):
        main = jnp.concatenate([blocks[u, :, :2 * size], blocks[u, :, 2 * size:4 * size]])
        both(u, u, main[:, :size])
        both(u, (u + 1) % GROUP, main[:, size:])
    for u in range(2):
        both(u, u + 2, jnp.concatenate([blocks[u, :, 4 * size:], blocks[u + 2, :, 4 * size:]]))
    for result, term in zip((high, low), invert(total, count)):
        result[...] = term


def update_kernel(where, act_high, act_low, out_high, out_low, *refs):
    pieces, (result, grad, update, done) = refs[:GROUP], refs[GROUP:]
    half, twice = pieces[0].shape
    width = twice // 2
    for step, piece in enumerate(pieces):
        start = pl.multiple_of((where[1] ^ step) * 2 * half, 2 * half)
        grad[pl.ds(start, half)] = piece[:, :width]
        grad[pl.ds(start + half, half)] = piece[:, width:]
    left = product((act_high[...], act_low[...]), (grad[...],))
    copies = []
    for part in range(2):
        rows = pl.ds(part * 4 * half, 4 * half)
        update[rows] = product(split(left[part * 4 * half:(part + 1) * 4 * half]), (out_high[...], out_low[...]))
        copies.append(pltpu.make_async_copy(update.at[rows], result.at[rows], done.at[part]))
        copies[-1].start()
    for copy in copies:
        copy.wait()


def send(parts):
    got = {0: parts[0]}
    for step in (3, 1, 2):
        got[step] = lax.ppermute(parts[step], ("near", "side"), [(i, i ^ step) for i in range(GROUP)])
    return [got[step] for step in range(GROUP)]


def exchange(value, after=(), flops=0):
    step = 1
    while step < lax.axis_size("far"):
        route = [(i, i ^ step) for i in range(lax.axis_size("far"))]
        got = lax.ppermute(value, "far", route)
        value = call(add_kernel, flops, value, [VMEM] * 2 + [ANY] * len(after))(value, got, *after)
        step *= 2
    return value


def body(acts, weights, cot_last):
    pairs = lax.axis_size("row")
    row = lax.axis_index("row")
    core = lax.axis_index("core")
    weight = weights[0]
    local = acts[0]
    micro, rows, width = local.shape
    tokens = micro * rows
    count = tokens * GROUP * lax.axis_size("far")
    odd = core == 1
    top = row == pairs - 1
    where = jnp.stack([core, lax.axis_index(("near", "side")), top.astype(jnp.int32)]).astype(jnp.int32)

    def mine_of(pair):
        return jnp.where(odd, pair[1], pair[0])

    def array(*shape, dtype=BF16):
        return jax.ShapeDtypeStruct(shape, dtype)

    partner = lax.ppermute(weight, "core", SWAP)
    partner_local = lax.ppermute(local, "core", SWAP)
    block = array(rows, width)
    slope = array(rows, width, dtype=F32)
    own, kept, last, slope_own, slope_partner, down = call(
        first_kernel,
        8 * rows * width**2,
        [array(width, width), array(micro, rows, width), block, slope, slope, block],
        [SMEM] + [VMEM] * 5,
    )(where, weight, local, cot_last, partner, partner_local)
    first = down
    for turn in range(1, pairs):
        upstream = lax.ppermute(down, "row", [(r, r - 1) for r in range(1, pairs)])
        arrived = upstream if turn == 1 else jnp.where(row == pairs - 1 - turn, upstream, arrived)
        if turn < pairs - 1:
            cot = layer(upstream, mine_of((slope_partner, slope_own)), mine_of((partner, own)))[1]
            down = layer(cot, mine_of((slope_own, slope_partner)), mine_of((own, partner)))[1]

    size = width // GROUP
    factor = 5 * size
    act_parts = call(
        act_kernel,
        2 * tokens * width**2,
        [array(size // 2, factor)] * GROUP,
        [SMEM, VMEM, ANY],
        [pltpu.VMEM((tokens, width), BF16), pltpu.VMEM((GROUP, size // 2, factor), BF16)],
    )(where, kept, first)
    act_pieces = send(act_parts)

    dh_odd, cot_odd = call(odd_kernel, 64 * rows * width**2, [block] * 2, [SMEM] + [VMEM] * 6)(
        where, own, partner, slope_own, slope_partner, arrived, last
    )
    act_sum = call(sum_kernel, 0, array(size // 2, factor), [VMEM] * GROUP + [ANY])(
        *(act_pieces[step] for step in (0, 3, 1, 2)), cot_odd
    )
    own_dh, give_dh, own_cot, give_cot = call(
        even_kernel, 4 * rows * width**2, [block] * 4, [SMEM] + [VMEM] * 6 + [ANY]
    )(where, own, partner, slope_own, slope_partner, dh_odd, cot_odd, act_sum)
    got_dh = lax.ppermute(give_dh, "core", SWAP)
    other_cot = lax.ppermute(give_cot, "core", SWAP)

    parts = call(
        grad_kernel,
        4 * tokens * width**2,
        [array(size // 2, factor + 2 * width)] * GROUP,
        [SMEM] + [VMEM] * 3,
        [pltpu.VMEM((tokens, width), BF16)] * 2
        + [pltpu.VMEM((GROUP, size // 2, factor + 2 * width), BF16)],
    )(where, kept, own_dh, got_dh)
    pieces = send(parts)
    begun, act_part = call(
        begin_kernel,
        0,
        [array(*parts[0].shape, dtype=F32), array(size // 2, factor)],
        [VMEM] * 3,
    )(pieces[0], pieces[3], exchange(act_sum, flops=24 * width**3))
    total = (begun + pieces[1].astype(F32) + pieces[2].astype(F32)).astype(BF16)
    cot = call(cot_kernel, 0, array(micro, rows, width), [SMEM, VMEM, VMEM, ANY])(
        where, own_cot, other_cot, total
    )
    act = send([act_part] * GROUP)

    def inverse(pieces):
        return call(
            functools.partial(inverse_kernel, count),
            20 * width**3,
            [array(width, width)] * 2,
            [SMEM] + [VMEM] * GROUP,
            [pltpu.VMEM((GROUP, size // 2, factor), F32), pltpu.VMEM((width, width), BF16)],
        )(where, *pieces)

    act_inv = inverse(act)
    total = exchange(total, (act_inv[0], cot))
    out = send([total[:, :factor]] * GROUP)
    grad = send([total[:, factor:]] * GROUP)
    update = call(
        update_kernel,
        10 * width**3,
        array(width, width, dtype=F32),
        [SMEM] + [VMEM] * (4 + GROUP),
        [
            pltpu.VMEM((width, width), BF16),
            pltpu.VMEM((width, width), F32),
            pltpu.SemaphoreType.DMA((2,)),
        ],
        HBM,
    )(where, *act_inv, *inverse(out), *grad)
    return (cot[None], update[None])


def solution(mesh):
    sections, shards = mesh.devices.shape
    finer = Mesh(
        np.reshape(mesh.devices, (sections // 2, 2, shards // GROUP, 2, 2)),
        ("row", "core", "far", "near", "side"),
    )
    section, dp = ("row", "core"), ("far", "near", "side")
    placed = (P(section, None, dp, None), P(section, None, None), P(None, dp, None))
    return jax.shard_map(
        body,
        mesh=finer,
        in_specs=placed,
        out_specs=(P(section, None, dp, None), P(section, None, None)),
        check_vma=False,
    )
```

```python
import functools

import jax
import jax.numpy as jnp
import numpy as np
from jax import lax
from jax.experimental import pallas as pl
from jax.experimental.pallas import tpu as pltpu
from jax.sharding import Mesh, PartitionSpec as P

BF16 = jnp.bfloat16
F32 = jnp.float32
SWAP = [(0, 1), (1, 0)]
SMEM = pl.BlockSpec(memory_space=pltpu.SMEM)
VMEM = pl.BlockSpec(memory_space=pltpu.VMEM)
ANY = pl.BlockSpec(memory_space=pl.ANY)
HBM = pl.BlockSpec(memory_space=pltpu.HBM)
GROUP = 4


def silu_slope(pre):
    sig = jax.nn.sigmoid(pre)
    return sig * (1.0 + pre * (1.0 - sig))


def slope_of(inputs, matrix):
    return silu_slope(jnp.dot(inputs, matrix, preferred_element_type=F32))


def layer(upstream, slope, matrix):
    dh = (upstream.astype(F32) * slope).astype(BF16)
    back = lax.dot_general(dh, matrix, (((1,), (1,)), ((), ())), preferred_element_type=F32)
    return dh, (upstream.astype(F32) + back).astype(BF16)


def by_core(core, run, own, partner):
    @pl.when(core == 1)
    def _():
        run(own, partner)

    @pl.when(core == 0)
    def _():
        run(partner, own)


def moment(left, right):
    return lax.dot_general(left, right, (((0,), (0,)), ((), ())), preferred_element_type=F32)


def split(value):
    high = value.astype(BF16)
    return high, (value - high.astype(F32)).astype(BF16)


def product(left, right, dims=((1,), (0,))):
    def dot(a, b):
        return lax.dot_general(a, b, (dims, ((), ())), preferred_element_type=F32)

    total = dot(left[0], right[0])
    if len(right) > 1:
        total += dot(left[0], right[1])
    if len(left) > 1:
        total += dot(left[1], right[0])
    return total


def call(kernel, flops, out_shape, in_specs, scratch=(), out_spec=VMEM):
    return pl.pallas_call(
        kernel,
        out_shape=jax.tree.map(lambda v: jax.ShapeDtypeStruct(v.shape, v.dtype), out_shape),
        in_specs=in_specs,
        out_specs=jax.tree.map(lambda _: out_spec, out_shape),
        scratch_shapes=list(scratch),
        cost_estimate=pl.CostEstimate(flops=flops, bytes_accessed=1 << 20, transcendentals=0),
        compiler_params=pltpu.CompilerParams(vmem_limit_bytes=32 << 20),
    )


def first_kernel(
    where, weight, local, cot_last, partner, partner_local,
    own, kept, last, slope_own, slope_partner, down,
):
    core = where[0]
    last[...] = cot_last[core]
    slope_own[...] = slope_of(local[core], weight[...])
    slope_partner[...] = slope_of(partner_local[core], partner[...])

    def run(odd, even):
        cot = layer(last[...], odd[1][...], odd[0][...])[1]
        down[...] = layer(cot, even[1][...], even[0][...])[1]

    by_core(core, run, (weight, slope_own), (partner, slope_partner))
    own[...] = weight[...]
    kept[...] = local[...]


def odd_kernel(where, own, partner, slope_own, slope_partner, arrived, last, dh, cot):
    upstream = jnp.where(where[2] == 1, last[...], arrived[...])

    def run(odd, even):
        dh[...], cot[...] = layer(upstream, odd[1][...], odd[0][...])

    by_core(where[0], run, (own, slope_own), (partner, slope_partner))


def sum_kernel(*refs):
    pieces, result = refs[:GROUP], refs[-1]
    result[...] = sum(piece[...].astype(F32) for piece in pieces).astype(BF16)


def even_kernel(
    where, own, partner, slope_own, slope_partner, dh, cot, after, own_dh, give_dh, own_cot, give_cot
):
    def run(odd, even):
        odd[2][...], odd[3][...] = dh[...], cot[...]
        even[2][...], even[3][...] = layer(cot[...], even[1][...], even[0][...])

    by_core(
        where[0], run, (own, slope_own, own_dh, own_cot), (partner, slope_partner, give_dh, give_cot)
    )


def cot_kernel(where, own_cot, other_cot, result):
    result[where[0]] = own_cot[...]
    result[1 - where[0]] = other_cot[...]


def put_factor(tokens, whole):
    width = tokens.shape[1]
    size = width // GROUP
    half = size // 2
    columns = [tokens[:, u * size:(u + 1) * size] for u in range(GROUP)]
    for u in range(GROUP):
        pair = jnp.concatenate([columns[u], columns[(u + 1) % GROUP]], axis=1)
        main = moment(columns[u], pair).astype(BF16)
        whole[u, :, :2 * size] = main[:half]
        whole[u, :, 2 * size:4 * size] = main[half:]
    for u in range(2):
        corner = moment(columns[u], columns[u + 2]).astype(BF16)
        whole[u, :, 4 * size:5 * size] = corner[:half]
        whole[u + 2, :, 4 * size:5 * size] = corner[half:]


def act_kernel(where, local, after, *refs):
    parts, (tokens, whole) = refs[:GROUP], refs[GROUP:]
    micro, rows = local.shape[:2]
    for m in range(micro):
        tokens[m * rows:(m + 1) * rows] = local[m]
    put_factor(tokens, whole)
    for step, part in enumerate(parts):
        part[...] = whole[where[1] ^ step]


def add_kernel(left, right, *refs):
    refs[-1][...] = (left[...].astype(F32) + right[...].astype(F32)).astype(BF16)


def begin_kernel(left, right, act, after, result, act_copy):
    act_copy[...] = act[...]
    result[...] = left[...].astype(F32) + right[...].astype(F32)


def grad_kernel(where, local, dh_own, dh_got, *refs):
    parts, (inputs, tokens, whole) = refs[:GROUP], refs[GROUP:]
    rows, width = local.shape[1:]
    inputs[:rows] = local[where[0]]
    inputs[rows:] = local[1 - where[0]]
    tokens[:rows] = dh_own[...]
    tokens[rows:] = dh_got[...]
    put_factor(tokens, whole)
    size = width // GROUP
    half = size // 2
    for u in range(GROUP):
        grad = moment(inputs[:, u * size:(u + 1) * size], tokens[...]).astype(BF16)
        whole[u, :, 5 * size:5 * size + width] = grad[:half]
        whole[u, :, 5 * size + width:] = grad[half:]
    for step, part in enumerate(parts):
        part[...] = whole[where[1] ^ step]


def invert(total, count):
    row = lax.broadcasted_iota(jnp.int32, total.shape, 0)
    column = lax.broadcasted_iota(jnp.int32, total.shape, 1)
    eye = (row == column).astype(F32)
    ridge = 0.01
    mean = total[...].astype(F32) * (1.0 / count)
    full = mean + ridge * eye
    scale = lax.rsqrt(jnp.sum(full * full, keepdims=True))
    squared = product((total[...],), (total[...],)) * (1.0 / count) ** 2 + ridge * (mean + full)
    second = (2.0 * scale) * full - squared * (scale * scale)
    second_terms = split(second)
    last = 2.0 * (eye - second) + product(second_terms, second_terms)
    tail = 2.0 * last - product(second_terms, split(last))
    inner = product((total[...],), split(tail)) * (scale * (1.0 / count))
    return split(((2.0 - ridge * scale) * tail - inner) * scale)

def inverse_kernel(count, where, *refs):
    pieces, (high, low, blocks, total) = refs[:GROUP], refs[GROUP:]
    for step, piece in enumerate(pieces):
        blocks[where[1] ^ step] = piece[...].astype(F32)
    size = total.shape[0] // GROUP

    def both(row, column, value):
        total[row * size:(row + 1) * size, column * size:(column + 1) * size] = value.astype(BF16)
        if row != column:
            total[column * size:(column + 1) * size, row * size:(row + 1) * size] = value.T.astype(BF16)

    for u in range(GROUP):
        main = jnp.concatenate([blocks[u, :, :2 * size], blocks[u, :, 2 * size:4 * size]])
        both(u, u, main[:, :size])
        both(u, (u + 1) % GROUP, main[:, size:])
    for u in range(2):
        both(u, u + 2, jnp.concatenate([blocks[u, :, 4 * size:], blocks[u + 2, :, 4 * size:]]))
    for result, term in zip((high, low), invert(total, count)):
        result[...] = term


def update_kernel(where, act_high, act_low, out_high, out_low, *refs):
    pieces, (result, grad, update, done) = refs[:GROUP], refs[GROUP:]
    half, twice = pieces[0].shape
    width = twice // 2
    for step, piece in enumerate(pieces):
        start = pl.multiple_of((where[1] ^ step) * 2 * half, 2 * half)
        grad[pl.ds(start, half)] = piece[:, :width]
        grad[pl.ds(start + half, half)] = piece[:, width:]
    left = product((act_high[...], act_low[...]), (grad[...],))
    copies = []
    for part in range(2):
        rows = pl.ds(part * 4 * half, 4 * half)
        update[rows] = product(split(left[part * 4 * half:(part + 1) * 4 * half]), (out_high[...], out_low[...]))
        copies.append(pltpu.make_async_copy(update.at[rows], result.at[rows], done.at[part]))
        copies[-1].start()
    for copy in copies:
        copy.wait()


def send(parts):
    got = {0: parts[0]}
    for step in (3, 1, 2):
        got[step] = lax.ppermute(parts[step], ("near", "side"), [(i, i ^ step) for i in range(GROUP)])
    return [got[step] for step in range(GROUP)]


def exchange(value, after=(), flops=0):
    step = 1
    while step < lax.axis_size("far"):
        route = [(i, i ^ step) for i in range(lax.axis_size("far"))]
        got = lax.ppermute(value, "far", route)
        value = call(add_kernel, flops, value, [VMEM] * 2 + [ANY] * len(after))(value, got, *after)
        step *= 2
    return value


def body(acts, weights, cot_last):
    pairs = lax.axis_size("row")
    row = lax.axis_index("row")
    core = lax.axis_index("core")
    weight = weights[0]
    local = acts[0]
    micro, rows, width = local.shape
    tokens = micro * rows
    count = tokens * GROUP * lax.axis_size("far")
    odd = core == 1
    top = row == pairs - 1
    where = jnp.stack([core, lax.axis_index(("near", "side")), top.astype(jnp.int32)]).astype(jnp.int32)

    def mine_of(pair):
        return jnp.where(odd, pair[1], pair[0])

    def array(*shape, dtype=BF16):
        return jax.ShapeDtypeStruct(shape, dtype)

    def near_copy(value):
        return jnp.where(core > 1, jnp.zeros_like(value), value)

    partner = lax.ppermute(weight, "core", SWAP)
    partner_local = lax.ppermute(local, "core", SWAP)
    block = array(rows, width)
    slope = array(rows, width, dtype=F32)
    own, kept, last, slope_own, slope_partner, down = call(
        first_kernel,
        8 * rows * width**2,
        [array(width, width), array(micro, rows, width), block, slope, slope, block],
        [SMEM] + [VMEM] * 5,
    )(where, near_copy(weight), near_copy(local), near_copy(cot_last), partner, partner_local)
    first = down
    for turn in range(1, pairs):
        upstream = lax.ppermute(down, "row", [(r, r - 1) for r in range(1, pairs)])
        arrived = upstream if turn == 1 else jnp.where(row == pairs - 1 - turn, upstream, arrived)
        if turn < pairs - 1:
            cot = layer(upstream, mine_of((slope_partner, slope_own)), mine_of((partner, own)))[1]
            down = layer(cot, mine_of((slope_own, slope_partner)), mine_of((own, partner)))[1]

    size = width // GROUP
    factor = 5 * size
    act_parts = call(
        act_kernel,
        2 * tokens * width**2,
        [array(size // 2, factor)] * GROUP,
        [SMEM, VMEM, ANY],
        [pltpu.VMEM((tokens, width), BF16), pltpu.VMEM((GROUP, size // 2, factor), BF16)],
    )(where, kept, first)
    act_pieces = send(act_parts)

    dh_odd, cot_odd = call(odd_kernel, 64 * rows * width**2, [block] * 2, [SMEM] + [VMEM] * 6)(
        where, own, partner, slope_own, slope_partner, arrived, last
    )
    act_sum = call(sum_kernel, 0, array(size // 2, factor), [VMEM] * GROUP + [ANY])(
        *(act_pieces[step] for step in (0, 3, 1, 2)), cot_odd
    )
    own_dh, give_dh, own_cot, give_cot = call(
        even_kernel, 4 * rows * width**2, [block] * 4, [SMEM] + [VMEM] * 6 + [ANY]
    )(where, own, partner, slope_own, slope_partner, dh_odd, cot_odd, act_sum)
    got_dh = lax.ppermute(give_dh, "core", SWAP)
    other_cot = lax.ppermute(give_cot, "core", SWAP)

    parts = call(
        grad_kernel,
        4 * tokens * width**2,
        [array(size // 2, factor + 2 * width)] * GROUP,
        [SMEM] + [VMEM] * 3,
        [pltpu.VMEM((tokens, width), BF16)] * 2
        + [pltpu.VMEM((GROUP, size // 2, factor + 2 * width), BF16)],
    )(where, kept, own_dh, got_dh)
    cot = call(cot_kernel, 0, array(micro, rows, width), [SMEM, VMEM, VMEM])(where, own_cot, other_cot)
    pieces = send(parts)
    begun, act_part = call(
        begin_kernel,
        0,
        [array(*parts[0].shape, dtype=F32), array(size // 2, factor)],
        [VMEM] * 3 + [ANY],
    )(pieces[0], pieces[3], exchange(act_sum, flops=24 * width**3), cot)
    total = (begun + pieces[1].astype(F32) + pieces[2].astype(F32)).astype(BF16)
    act = send([act_part] * GROUP)

    def inverse(pieces, flops):
        return call(
            functools.partial(inverse_kernel, count),
            flops,
            [array(width, width)] * 2,
            [SMEM] + [VMEM] * GROUP,
            [pltpu.VMEM((GROUP, size // 2, factor), F32), pltpu.VMEM((width, width), BF16)],
        )(where, *pieces)

    act_inv = inverse(act, 0)
    total = exchange(total, (act_inv[0],))
    out = send([total[:, :factor]] * GROUP)
    grad = send([total[:, factor:]] * GROUP)
    update = call(
        update_kernel,
        10 * width**3,
        array(width, width, dtype=F32),
        [SMEM] + [VMEM] * (4 + GROUP),
        [
            pltpu.VMEM((width, width), BF16),
            pltpu.VMEM((width, width), F32),
            pltpu.SemaphoreType.DMA((2,)),
        ],
        HBM,
    )(where, *act_inv, *inverse(out, 20 * width**3), *grad)
    return (cot[None], update[None])


def solution(mesh):
    sections, shards = mesh.devices.shape
    finer = Mesh(
        np.reshape(mesh.devices, (sections // 2, 2, shards // GROUP, 2, 2)),
        ("row", "core", "far", "near", "side"),
    )
    section, dp = ("row", "core"), ("far", "near", "side")
    placed = (P(section, None, dp, None), P(section, None, None), P(None, dp, None))
    return jax.shard_map(
        body,
        mesh=finer,
        in_specs=placed,
        out_specs=(P(section, None, dp, None), P(section, None, None)),
        check_vma=False,
    )
```

```python
import functools

import jax
import jax.numpy as jnp
import numpy as np
from jax import lax
from jax.experimental import pallas as pl
from jax.experimental.pallas import tpu as pltpu
from jax.sharding import Mesh, PartitionSpec as P

BF16 = jnp.bfloat16
F32 = jnp.float32
SWAP = [(0, 1), (1, 0)]
SMEM = pl.BlockSpec(memory_space=pltpu.SMEM)
VMEM = pl.BlockSpec(memory_space=pltpu.VMEM)
ANY = pl.BlockSpec(memory_space=pl.ANY)
HBM = pl.BlockSpec(memory_space=pltpu.HBM)
GROUP = 4


def silu_slope(pre):
    sig = jax.nn.sigmoid(pre)
    return sig * (1.0 + pre * (1.0 - sig))


def slope_of(inputs, matrix):
    return silu_slope(jnp.dot(inputs, matrix, preferred_element_type=F32))


def layer(upstream, slope, matrix):
    dh = (upstream.astype(F32) * slope).astype(BF16)
    back = lax.dot_general(dh, matrix, (((1,), (1,)), ((), ())), preferred_element_type=F32)
    return dh, (upstream.astype(F32) + back).astype(BF16)


def by_core(core, run, own, partner):
    @pl.when(core == 1)
    def _():
        run(own, partner)

    @pl.when(core == 0)
    def _():
        run(partner, own)


def moment(left, right):
    return lax.dot_general(left, right, (((0,), (0,)), ((), ())), preferred_element_type=F32)


def split(value):
    high = value.astype(BF16)
    return high, (value - high.astype(F32)).astype(BF16)


def product(left, right, dims=((1,), (0,))):
    def dot(a, b):
        return lax.dot_general(a, b, (dims, ((), ())), preferred_element_type=F32)

    total = dot(left[0], right[0])
    if len(right) > 1:
        total += dot(left[0], right[1])
    if len(left) > 1:
        total += dot(left[1], right[0])
    return total


def call(kernel, flops, out_shape, in_specs, scratch=(), out_spec=VMEM):
    return pl.pallas_call(
        kernel,
        out_shape=jax.tree.map(lambda v: jax.ShapeDtypeStruct(v.shape, v.dtype), out_shape),
        in_specs=in_specs,
        out_specs=jax.tree.map(lambda _: out_spec, out_shape),
        scratch_shapes=list(scratch),
        cost_estimate=pl.CostEstimate(flops=flops, bytes_accessed=1 << 20, transcendentals=0),
        compiler_params=pltpu.CompilerParams(vmem_limit_bytes=32 << 20),
    )


def first_kernel(
    where, weight, local, cot_last, partner, partner_local,
    own, kept, last, slope_own, slope_partner, down,
):
    core = where[0]
    last[...] = cot_last[core]
    slope_own[...] = slope_of(local[core], weight[...])
    slope_partner[...] = slope_of(partner_local[core], partner[...])

    def run(odd, even):
        cot = layer(last[...], odd[1][...], odd[0][...])[1]
        down[...] = layer(cot, even[1][...], even[0][...])[1]

    by_core(core, run, (weight, slope_own), (partner, slope_partner))
    own[...] = weight[...]
    kept[...] = local[...]


def odd_kernel(where, own, partner, slope_own, slope_partner, arrived, last, dh, cot):
    upstream = jnp.where(where[2] == 1, last[...], arrived[...])

    def run(odd, even):
        dh[...], cot[...] = layer(upstream, odd[1][...], odd[0][...])

    by_core(where[0], run, (own, slope_own), (partner, slope_partner))


def sum_kernel(*refs):
    pieces, result = refs[:GROUP], refs[-1]
    result[...] = sum(piece[...].astype(F32) for piece in pieces).astype(BF16)


def even_kernel(where, own, partner, slope_own, slope_partner, dh, cot, own_dh, give_dh, own_cot, give_cot):
    def run(odd, even):
        odd[2][...], odd[3][...] = dh[...], cot[...]
        even[2][...], even[3][...] = layer(cot[...], even[1][...], even[0][...])

    by_core(
        where[0], run, (own, slope_own, own_dh, own_cot), (partner, slope_partner, give_dh, give_cot)
    )


def cot_kernel(where, own_cot, other_cot, result):
    result[where[0]] = own_cot[...]
    result[1 - where[0]] = other_cot[...]


def put_factor(tokens, whole):
    width = tokens.shape[1]
    size = width // GROUP
    half = size // 2
    columns = [tokens[:, u * size:(u + 1) * size] for u in range(GROUP)]
    for u in range(GROUP):
        pair = jnp.concatenate([columns[u], columns[(u + 1) % GROUP]], axis=1)
        main = moment(columns[u], pair).astype(BF16)
        whole[u, :, :2 * size] = main[:half]
        whole[u, :, 2 * size:4 * size] = main[half:]
    for u in range(2):
        corner = moment(columns[u], columns[u + 2]).astype(BF16)
        whole[u, :, 4 * size:5 * size] = corner[:half]
        whole[u + 2, :, 4 * size:5 * size] = corner[half:]


def act_kernel(where, local, after, *refs):
    parts, (tokens, whole) = refs[:GROUP], refs[GROUP:]
    micro, rows = local.shape[:2]
    for m in range(micro):
        tokens[m * rows:(m + 1) * rows] = local[m]
    put_factor(tokens, whole)
    for step, part in enumerate(parts):
        part[...] = whole[where[1] ^ step]


def add_kernel(left, right, *refs):
    refs[-1][...] = (left[...].astype(F32) + right[...].astype(F32)).astype(BF16)


def begin_kernel(left, right, act, after, result, act_copy):
    act_copy[...] = act[...]
    result[...] = left[...].astype(F32) + right[...].astype(F32)


def grad_kernel(where, local, dh_own, dh_got, after, *refs):
    parts, (inputs, tokens, whole) = refs[:GROUP], refs[GROUP:]
    rows, width = local.shape[1:]
    inputs[:rows] = local[where[0]]
    inputs[rows:] = local[1 - where[0]]
    tokens[:rows] = dh_own[...]
    tokens[rows:] = dh_got[...]
    put_factor(tokens, whole)
    size = width // GROUP
    half = size // 2
    for u in range(GROUP):
        grad = moment(inputs[:, u * size:(u + 1) * size], tokens[...]).astype(BF16)
        whole[u, :, 5 * size:5 * size + width] = grad[:half]
        whole[u, :, 5 * size + width:] = grad[half:]
    for step, part in enumerate(parts):
        part[...] = whole[where[1] ^ step]


def invert(total, count):
    row = lax.broadcasted_iota(jnp.int32, total.shape, 0)
    column = lax.broadcasted_iota(jnp.int32, total.shape, 1)
    eye = (row == column).astype(F32)
    ridge = 0.01
    mean = total[...].astype(F32) * (1.0 / count)
    full = mean + ridge * eye
    scale = lax.rsqrt(jnp.sum(full * full, keepdims=True))
    squared = product((total[...],), (total[...],)) * (1.0 / count) ** 2 + ridge * (mean + full)
    second = (2.0 * scale) * full - squared * (scale * scale)
    second_terms = split(second)
    last = 2.0 * (eye - second) + product(second_terms, second_terms)
    tail = 2.0 * last - product(second_terms, split(last))
    inner = product((total[...],), split(tail)) * (scale * (1.0 / count))
    return split(((2.0 - ridge * scale) * tail - inner) * scale)

def inverse_kernel(count, where, *refs):
    pieces, (high, low, blocks, total) = refs[:GROUP], refs[GROUP:]
    for step, piece in enumerate(pieces):
        blocks[where[1] ^ step] = piece[...].astype(F32)
    size = total.shape[0] // GROUP

    def both(row, column, value):
        total[row * size:(row + 1) * size, column * size:(column + 1) * size] = value.astype(BF16)
        if row != column:
            total[column * size:(column + 1) * size, row * size:(row + 1) * size] = value.T.astype(BF16)

    for u in range(GROUP):
        main = jnp.concatenate([blocks[u, :, :2 * size], blocks[u, :, 2 * size:4 * size]])
        both(u, u, main[:, :size])
        both(u, (u + 1) % GROUP, main[:, size:])
    for u in range(2):
        both(u, u + 2, jnp.concatenate([blocks[u, :, 4 * size:], blocks[u + 2, :, 4 * size:]]))
    for result, term in zip((high, low), invert(total, count)):
        result[...] = term


def update_kernel(where, act_high, act_low, out_high, out_low, *refs):
    pieces, (result, grad, update, done) = refs[:GROUP], refs[GROUP:]
    half, twice = pieces[0].shape
    width = twice // 2
    for step, piece in enumerate(pieces):
        start = pl.multiple_of((where[1] ^ step) * 2 * half, 2 * half)
        grad[pl.ds(start, half)] = piece[:, :width]
        grad[pl.ds(start + half, half)] = piece[:, width:]
    left = product((act_high[...], act_low[...]), (grad[...],))
    copies = []
    for part in range(2):
        rows = pl.ds(part * 4 * half, 4 * half)
        update[rows] = product(split(left[part * 4 * half:(part + 1) * 4 * half]), (out_high[...], out_low[...]))
        copies.append(pltpu.make_async_copy(update.at[rows], result.at[rows], done.at[part]))
        copies[-1].start()
    for copy in copies:
        copy.wait()


def send(parts):
    got = {0: parts[0]}
    for step in (3, 1, 2):
        got[step] = lax.ppermute(parts[step], ("near", "side"), [(i, i ^ step) for i in range(GROUP)])
    return [got[step] for step in range(GROUP)]


def exchange(value, after=(), flops=0):
    step = 1
    while step < lax.axis_size("far"):
        route = [(i, i ^ step) for i in range(lax.axis_size("far"))]
        got = lax.ppermute(value, "far", route)
        value = call(add_kernel, flops, value, [VMEM] * 2 + [ANY] * len(after))(value, got, *after)
        step *= 2
    return value


def body(acts, weights, cot_last):
    pairs = lax.axis_size("row")
    row = lax.axis_index("row")
    core = lax.axis_index("core")
    weight = weights[0]
    local = acts[0]
    micro, rows, width = local.shape
    tokens = micro * rows
    count = tokens * GROUP * lax.axis_size("far")
    odd = core == 1
    top = row == pairs - 1
    where = jnp.stack([core, lax.axis_index(("near", "side")), top.astype(jnp.int32)]).astype(jnp.int32)

    def mine_of(pair):
        return jnp.where(odd, pair[1], pair[0])

    def array(*shape, dtype=BF16):
        return jax.ShapeDtypeStruct(shape, dtype)

    def near_copy(value):
        return jnp.where(core > 1, jnp.zeros_like(value), value)

    partner = lax.ppermute(weight, "core", SWAP)
    partner_local = lax.ppermute(local, "core", SWAP)
    block = array(rows, width)
    slope = array(rows, width, dtype=F32)
    own, kept, last, slope_own, slope_partner, down = call(
        first_kernel,
        8 * rows * width**2,
        [array(width, width), array(micro, rows, width), block, slope, slope, block],
        [SMEM] + [VMEM] * 5,
    )(where, near_copy(weight), near_copy(local), near_copy(cot_last), partner, partner_local)
    first = down
    for turn in range(1, pairs):
        upstream = lax.ppermute(down, "row", [(r, r - 1) for r in range(1, pairs)])
        arrived = upstream if turn == 1 else jnp.where(row == pairs - 1 - turn, upstream, arrived)
        if turn < pairs - 1:
            cot = layer(upstream, mine_of((slope_partner, slope_own)), mine_of((partner, own)))[1]
            down = layer(cot, mine_of((slope_own, slope_partner)), mine_of((own, partner)))[1]

    size = width // GROUP
    factor = 5 * size
    act_parts = call(
        act_kernel,
        2 * tokens * width**2,
        [array(size // 2, factor)] * GROUP,
        [SMEM, VMEM, ANY],
        [pltpu.VMEM((tokens, width), BF16), pltpu.VMEM((GROUP, size // 2, factor), BF16)],
    )(where, kept, first)
    act_pieces = send(act_parts)

    dh_odd, cot_odd = call(odd_kernel, 64 * rows * width**2, [block] * 2, [SMEM] + [VMEM] * 6)(
        where, own, partner, slope_own, slope_partner, arrived, last
    )
    own_dh, give_dh, own_cot, give_cot = call(
        even_kernel, 4 * rows * width**2, [block] * 4, [SMEM] + [VMEM] * 6
    )(where, own, partner, slope_own, slope_partner, dh_odd, cot_odd)
    act_sum = call(sum_kernel, 0, array(size // 2, factor), [VMEM] * GROUP + [ANY])(
        *(act_pieces[step] for step in (0, 3, 1, 2)), own_dh
    )
    got_dh = lax.ppermute(give_dh, "core", SWAP)
    other_cot = lax.ppermute(give_cot, "core", SWAP)

    parts = call(
        grad_kernel,
        4 * tokens * width**2,
        [array(size // 2, factor + 2 * width)] * GROUP,
        [SMEM] + [VMEM] * 3 + [ANY],
        [pltpu.VMEM((tokens, width), BF16)] * 2
        + [pltpu.VMEM((GROUP, size // 2, factor + 2 * width), BF16)],
    )(where, kept, own_dh, got_dh, act_sum)
    cot = call(cot_kernel, 0, array(micro, rows, width), [SMEM, VMEM, VMEM])(where, own_cot, other_cot)
    pieces = send(parts)
    begun, act_part = call(
        begin_kernel,
        0,
        [array(*parts[0].shape, dtype=F32), array(size // 2, factor)],
        [VMEM] * 3 + [ANY],
    )(pieces[0], pieces[3], exchange(act_sum, flops=24 * width**3), cot)
    total = (begun + pieces[1].astype(F32) + pieces[2].astype(F32)).astype(BF16)
    act = send([act_part] * GROUP)

    def inverse(pieces, flops):
        return call(
            functools.partial(inverse_kernel, count),
            flops,
            [array(width, width)] * 2,
            [SMEM] + [VMEM] * GROUP,
            [pltpu.VMEM((GROUP, size // 2, factor), F32), pltpu.VMEM((width, width), BF16)],
        )(where, *pieces)

    act_inv = inverse(act, 0)
    out = send([exchange(total[:, :factor])] * GROUP)
    grad = send([exchange(total[:, factor:], (act_inv[0], *out))] * GROUP)
    update = call(
        update_kernel,
        10 * width**3,
        array(width, width, dtype=F32),
        [SMEM] + [VMEM] * (4 + GROUP),
        [
            pltpu.VMEM((width, width), BF16),
            pltpu.VMEM((width, width), F32),
            pltpu.SemaphoreType.DMA((2,)),
        ],
        HBM,
    )(where, *act_inv, *inverse(out, 20 * width**3), *grad)
    return (cot[None], update[None])


def solution(mesh):
    sections, shards = mesh.devices.shape
    finer = Mesh(
        np.reshape(mesh.devices, (sections // 2, 2, shards // GROUP, 2, 2)),
        ("row", "core", "far", "near", "side"),
    )
    section, dp = ("row", "core"), ("far", "near", "side")
    placed = (P(section, None, dp, None), P(section, None, None), P(None, dp, None))
    return jax.shard_map(
        body,
        mesh=finer,
        in_specs=placed,
        out_specs=(P(section, None, dp, None), P(section, None, None)),
        check_vma=False,
    )
```

```python
import functools

import jax
import jax.numpy as jnp
import numpy as np
from jax import lax
from jax.experimental import pallas as pl
from jax.experimental.pallas import tpu as pltpu
from jax.sharding import Mesh, PartitionSpec as P

BF16 = jnp.bfloat16
F32 = jnp.float32
SWAP = [(0, 1), (1, 0)]
SMEM = pl.BlockSpec(memory_space=pltpu.SMEM)
VMEM = pl.BlockSpec(memory_space=pltpu.VMEM)
ANY = pl.BlockSpec(memory_space=pl.ANY)
HBM = pl.BlockSpec(memory_space=pltpu.HBM)
GROUP = 4


def silu_slope(pre):
    sig = jax.nn.sigmoid(pre)
    return sig * (1.0 + pre * (1.0 - sig))


def slope_of(inputs, matrix):
    return silu_slope(jnp.dot(inputs, matrix, preferred_element_type=F32))


def layer(upstream, slope, matrix):
    dh = (upstream.astype(F32) * slope).astype(BF16)
    back = lax.dot_general(dh, matrix, (((1,), (1,)), ((), ())), preferred_element_type=F32)
    return dh, (upstream.astype(F32) + back).astype(BF16)


def by_core(core, run, own, partner):
    @pl.when(core == 1)
    def _():
        run(own, partner)

    @pl.when(core == 0)
    def _():
        run(partner, own)


def moment(left, right):
    return lax.dot_general(left, right, (((0,), (0,)), ((), ())), preferred_element_type=F32)


def split(value):
    high = value.astype(BF16)
    return high, (value - high.astype(F32)).astype(BF16)


def product(left, right, dims=((1,), (0,))):
    def dot(a, b):
        return lax.dot_general(a, b, (dims, ((), ())), preferred_element_type=F32)

    total = dot(left[0], right[0])
    if len(right) > 1:
        total += dot(left[0], right[1])
    if len(left) > 1:
        total += dot(left[1], right[0])
    return total


def call(kernel, flops, out_shape, in_specs, scratch=(), out_spec=VMEM):
    return pl.pallas_call(
        kernel,
        out_shape=jax.tree.map(lambda v: jax.ShapeDtypeStruct(v.shape, v.dtype), out_shape),
        in_specs=in_specs,
        out_specs=jax.tree.map(lambda _: out_spec, out_shape),
        scratch_shapes=list(scratch),
        cost_estimate=pl.CostEstimate(flops=flops, bytes_accessed=1 << 20, transcendentals=0),
        compiler_params=pltpu.CompilerParams(vmem_limit_bytes=32 << 20),
    )


def first_kernel(
    where, weight, local, cot_last, partner, partner_local,
    own, kept, last, slope_own, slope_partner, down,
):
    core = where[0]
    last[...] = cot_last[core]
    slope_own[...] = slope_of(local[core], weight[...])
    slope_partner[...] = slope_of(partner_local[core], partner[...])

    def run(odd, even):
        cot = layer(last[...], odd[1][...], odd[0][...])[1]
        down[...] = layer(cot, even[1][...], even[0][...])[1]

    by_core(core, run, (weight, slope_own), (partner, slope_partner))
    own[...] = weight[...]
    kept[...] = local[...]


def sum_kernel(*refs):
    result = refs[-1]
    result[...] = sum(piece[...].astype(F32) for piece in refs[:GROUP]).astype(BF16)


def pass_kernel(*refs):
    refs[-2][...] = sum(piece[...].astype(F32) for piece in refs[:GROUP]).astype(BF16)
    refs[-1][...] = refs[GROUP][...]


def layers_kernel(
    where, own, partner, slope_own, slope_partner, arrived, last, own_dh, give_dh, own_cot, give_cot
):
    upstream = jnp.where(where[2] == 1, last[...], arrived[...])

    def run(odd, even):
        dh, cot = layer(upstream, odd[1][...], odd[0][...])
        odd[2][...], odd[3][...] = dh, cot
        even[2][...], even[3][...] = layer(cot, even[1][...], even[0][...])

    by_core(
        where[0], run, (own, slope_own, own_dh, own_cot), (partner, slope_partner, give_dh, give_cot)
    )


def cot_kernel(where, own_cot, other_cot, result):
    result[where[0]] = own_cot[...]
    result[1 - where[0]] = other_cot[...]


def put_factor(tokens, whole):
    width = tokens.shape[1]
    size = width // GROUP
    half = size // 2
    columns = [tokens[:, u * size:(u + 1) * size] for u in range(GROUP)]
    for u in range(GROUP):
        pair = jnp.concatenate([columns[u], columns[(u + 1) % GROUP]], axis=1)
        main = moment(columns[u], pair).astype(BF16)
        whole[u, :, :2 * size] = main[:half]
        whole[u, :, 2 * size:4 * size] = main[half:]
    for u in range(2):
        corner = moment(columns[u], columns[u + 2]).astype(BF16)
        whole[u, :, 4 * size:5 * size] = corner[:half]
        whole[u + 2, :, 4 * size:5 * size] = corner[half:]


def act_kernel(where, local, after, *refs):
    parts, (tokens, whole) = refs[:GROUP], refs[GROUP:]
    micro, rows = local.shape[:2]
    for m in range(micro):
        tokens[m * rows:(m + 1) * rows] = local[m]
    put_factor(tokens, whole)
    for step, part in enumerate(parts):
        part[...] = whole[where[1] ^ step]


def add_kernel(left, right, *refs):
    refs[-1][...] = (left[...].astype(F32) + right[...].astype(F32)).astype(BF16)


def grad_kernel(where, local, dh_own, dh_got, after, *refs):
    factors, grads, (inputs, tokens, whole, rest) = refs[:GROUP], refs[GROUP:2 * GROUP], refs[2 * GROUP:]
    rows, width = local.shape[1:]
    inputs[:rows] = local[where[0]]
    inputs[rows:] = local[1 - where[0]]
    tokens[:rows] = dh_own[...]
    tokens[rows:] = dh_got[...]
    put_factor(tokens, whole)
    size = width // GROUP
    half = size // 2
    for u in range(GROUP):
        grad = moment(inputs[:, u * size:(u + 1) * size], tokens[...]).astype(BF16)
        rest[u, :, :width] = grad[:half]
        rest[u, :, width:] = grad[half:]
    for step in range(GROUP):
        factors[step][...] = whole[where[1] ^ step]
        grads[step][...] = rest[where[1] ^ step]


def invert(total, count):
    row = lax.broadcasted_iota(jnp.int32, total.shape, 0)
    column = lax.broadcasted_iota(jnp.int32, total.shape, 1)
    eye = (row == column).astype(F32)
    ridge = 0.01
    mean = total[...].astype(F32) * (1.0 / count)
    full = mean + ridge * eye
    scale = lax.rsqrt(jnp.sum(full * full, keepdims=True))
    squared = product((total[...],), (total[...],)) * (1.0 / count) ** 2 + ridge * (mean + full)
    second = (2.0 * scale) * full - squared * (scale * scale)
    second_terms = split(second)
    last = 2.0 * (eye - second) + product(second_terms, second_terms)
    tail = 2.0 * last - product(second_terms, split(last))
    inner = product((total[...],), split(tail)) * (scale * (1.0 / count))
    return split(((2.0 - ridge * scale) * tail - inner) * scale)

def inverse_kernel(count, where, *refs):
    pieces, (high, low, blocks, total) = refs[:GROUP], refs[GROUP:]
    for step, piece in enumerate(pieces):
        blocks[where[1] ^ step] = piece[...].astype(F32)
    size = total.shape[0] // GROUP

    def both(row, column, value):
        total[row * size:(row + 1) * size, column * size:(column + 1) * size] = value.astype(BF16)
        if row != column:
            total[column * size:(column + 1) * size, row * size:(row + 1) * size] = value.T.astype(BF16)

    for u in range(GROUP):
        main = jnp.concatenate([blocks[u, :, :2 * size], blocks[u, :, 2 * size:4 * size]])
        both(u, u, main[:, :size])
        both(u, (u + 1) % GROUP, main[:, size:])
    for u in range(2):
        both(u, u + 2, jnp.concatenate([blocks[u, :, 4 * size:], blocks[u + 2, :, 4 * size:]]))
    for result, term in zip((high, low), invert(total, count)):
        result[...] = term


def update_kernel(where, act_high, act_low, out_high, out_low, *refs):
    pieces, (result, grad, update, done) = refs[:GROUP], refs[GROUP:]
    half, twice = pieces[0].shape
    width = twice // 2
    for step, piece in enumerate(pieces):
        start = pl.multiple_of((where[1] ^ step) * 2 * half, 2 * half)
        grad[pl.ds(start, half)] = piece[:, :width]
        grad[pl.ds(start + half, half)] = piece[:, width:]
    left = product((act_high[...], act_low[...]), (grad[...],))
    copies = []
    for part in range(2):
        rows = pl.ds(part * 4 * half, 4 * half)
        update[rows] = product(split(left[part * 4 * half:(part + 1) * 4 * half]), (out_high[...], out_low[...]))
        copies.append(pltpu.make_async_copy(update.at[rows], result.at[rows], done.at[part]))
        copies[-1].start()
    for copy in copies:
        copy.wait()


def send(parts):
    got = {0: parts[0]}
    for step in (3, 1, 2):
        got[step] = lax.ppermute(parts[step], ("near", "side"), [(i, i ^ step) for i in range(GROUP)])
    return [got[step] for step in range(GROUP)]


def exchange(value, after=(), flops=0):
    step = 1
    while step < lax.axis_size("far"):
        route = [(i, i ^ step) for i in range(lax.axis_size("far"))]
        got = lax.ppermute(value, "far", route)
        value = call(add_kernel, flops, value, [VMEM] * 2 + [ANY] * len(after))(value, got, *after)
        step *= 2
    return value


def body(acts, weights, cot_last):
    pairs = lax.axis_size("row")
    row = lax.axis_index("row")
    core = lax.axis_index("core")
    weight = weights[0]
    local = acts[0]
    micro, rows, width = local.shape
    tokens = micro * rows
    count = tokens * GROUP * lax.axis_size("far")
    odd = core == 1
    top = row == pairs - 1
    where = jnp.stack([core, lax.axis_index(("near", "side")), top.astype(jnp.int32)]).astype(jnp.int32)

    def mine_of(pair):
        return jnp.where(odd, pair[1], pair[0])

    def array(*shape, dtype=BF16):
        return jax.ShapeDtypeStruct(shape, dtype)

    def near_copy(value):
        return jnp.where(core > 1, jnp.zeros_like(value), value)

    partner = lax.ppermute(weight, "core", SWAP)
    partner_local = lax.ppermute(local, "core", SWAP)
    block = array(rows, width)
    slope = array(rows, width, dtype=F32)
    own, kept, last, slope_own, slope_partner, down = call(
        first_kernel,
        8 * rows * width**2,
        [array(width, width), array(micro, rows, width), block, slope, slope, block],
        [SMEM] + [VMEM] * 5,
    )(where, near_copy(weight), near_copy(local), near_copy(cot_last), partner, partner_local)
    first = down
    for turn in range(1, pairs):
        upstream = lax.ppermute(down, "row", [(r, r - 1) for r in range(1, pairs)])
        arrived = upstream if turn == 1 else jnp.where(row == pairs - 1 - turn, upstream, arrived)
        if turn < pairs - 1:
            cot = layer(upstream, mine_of((slope_partner, slope_own)), mine_of((partner, own)))[1]
            down = layer(cot, mine_of((slope_own, slope_partner)), mine_of((own, partner)))[1]

    size = width // GROUP
    factor = 5 * size
    act_parts = call(
        act_kernel,
        2 * tokens * width**2,
        [array(size // 2, factor)] * GROUP,
        [SMEM, VMEM, ANY],
        [pltpu.VMEM((tokens, width), BF16), pltpu.VMEM((GROUP, size // 2, factor), BF16)],
    )(where, kept, first)
    act_pieces = send(act_parts)

    own_dh, give_dh, own_cot, give_cot = call(
        layers_kernel, 64 * rows * width**2, [block] * 4, [SMEM] + [VMEM] * 6
    )(where, own, partner, slope_own, slope_partner, arrived, last)
    act_sum = call(sum_kernel, 24 * width**3, array(size // 2, factor), [VMEM] * GROUP + [ANY])(
        *(act_pieces[step] for step in (0, 3, 1, 2)), own_dh
    )
    got_dh = lax.ppermute(give_dh, "core", SWAP)
    other_cot = lax.ppermute(give_cot, "core", SWAP)

    parts = call(
        grad_kernel,
        4 * tokens * width**2,
        [array(size // 2, factor)] * GROUP + [array(size // 2, 2 * width)] * GROUP,
        [SMEM] + [VMEM] * 3 + [ANY],
        [pltpu.VMEM((tokens, width), BF16)] * 2
        + [pltpu.VMEM((GROUP, size // 2, factor), BF16), pltpu.VMEM((GROUP, size // 2, 2 * width), BF16)],
    )(where, kept, own_dh, got_dh, act_sum)
    cot = call(cot_kernel, 0, array(micro, rows, width), [SMEM, VMEM, VMEM])(where, own_cot, other_cot)

    def summed(pieces):
        shape = array(*pieces[0].shape)
        return call(sum_kernel, 0, shape, [VMEM] * GROUP)(*(pieces[step] for step in (0, 3, 1, 2)))

    pieces = send(parts[:GROUP])
    factors, act_part = call(
        pass_kernel, 0, [array(size // 2, factor)] * 2, [VMEM] * (GROUP + 1) + [ANY]
    )(*(pieces[step] for step in (0, 3, 1, 2)), exchange(act_sum, flops=16 * width**3), cot)
    out = send([exchange(factors)] * GROUP)
    act = send([act_part] * GROUP)
    total = summed(send(parts[GROUP:]))

    def inverse(pieces, flops):
        return call(
            functools.partial(inverse_kernel, count),
            flops,
            [array(width, width)] * 2,
            [SMEM] + [VMEM] * GROUP,
            [pltpu.VMEM((GROUP, size // 2, factor), F32), pltpu.VMEM((width, width), BF16)],
        )(where, *pieces)

    act_inv = inverse(act, 0)
    grad = send([exchange(total, (act_inv[0], *out))] * GROUP)
    update = call(
        update_kernel,
        10 * width**3,
        array(width, width, dtype=F32),
        [SMEM] + [VMEM] * (4 + GROUP),
        [
            pltpu.VMEM((width, width), BF16),
            pltpu.VMEM((width, width), F32),
            pltpu.SemaphoreType.DMA((2,)),
        ],
        HBM,
    )(where, *act_inv, *inverse(out, 20 * width**3), *grad)
    return (cot[None], update[None])


def solution(mesh):
    sections, shards = mesh.devices.shape
    finer = Mesh(
        np.reshape(mesh.devices, (sections // 2, 2, shards // GROUP, 2, 2)),
        ("row", "core", "far", "near", "side"),
    )
    section, dp = ("row", "core"), ("far", "near", "side")
    placed = (P(section, None, dp, None), P(section, None, None), P(None, dp, None))
    return jax.shard_map(
        body,
        mesh=finer,
        in_specs=placed,
        out_specs=(P(section, None, dp, None), P(section, None, None)),
        check_vma=False,
    )
```

```python
import functools

import jax
import jax.numpy as jnp
import numpy as np
from jax import lax
from jax.experimental import pallas as pl
from jax.experimental.pallas import tpu as pltpu
from jax.sharding import Mesh, PartitionSpec as P

BF16 = jnp.bfloat16
F32 = jnp.float32
SWAP = [(0, 1), (1, 0)]
SMEM = pl.BlockSpec(memory_space=pltpu.SMEM)
VMEM = pl.BlockSpec(memory_space=pltpu.VMEM)
ANY = pl.BlockSpec(memory_space=pl.ANY)
HBM = pl.BlockSpec(memory_space=pltpu.HBM)
GROUP = 4


def silu_slope(pre):
    sig = jax.nn.sigmoid(pre)
    return sig * (1.0 + pre * (1.0 - sig))


def slope_of(inputs, matrix):
    return silu_slope(jnp.dot(inputs, matrix, preferred_element_type=F32))


def layer(upstream, slope, matrix):
    dh = (upstream.astype(F32) * slope).astype(BF16)
    back = lax.dot_general(dh, matrix, (((1,), (1,)), ((), ())), preferred_element_type=F32)
    return dh, (upstream.astype(F32) + back).astype(BF16)


def by_core(core, run, own, partner):
    @pl.when(core == 1)
    def _():
        run(own, partner)

    @pl.when(core == 0)
    def _():
        run(partner, own)


def moment(left, right):
    return lax.dot_general(left, right, (((0,), (0,)), ((), ())), preferred_element_type=F32)


def split(value):
    high = value.astype(BF16)
    return high, (value - high.astype(F32)).astype(BF16)


def dot(left, right):
    return jnp.dot(left.astype(BF16), right.astype(BF16), preferred_element_type=F32)


def call(kernel, flops, out_shape, in_specs, scratch=(), out_spec=VMEM):
    return pl.pallas_call(
        kernel,
        out_shape=jax.tree.map(lambda v: jax.ShapeDtypeStruct(v.shape, v.dtype), out_shape),
        in_specs=in_specs,
        out_specs=jax.tree.map(lambda _: out_spec, out_shape),
        scratch_shapes=list(scratch),
        cost_estimate=pl.CostEstimate(flops=flops, bytes_accessed=1 << 20, transcendentals=0),
        compiler_params=pltpu.CompilerParams(vmem_limit_bytes=32 << 20),
    )


def first_kernel(
    where, weight, local, cot_last, partner, partner_local,
    own, kept, last, slope_own, slope_partner, down,
):
    core = where[0]
    last[...] = cot_last[core]
    slope_own[...] = slope_of(local[core], weight[...])
    slope_partner[...] = slope_of(partner_local[core], partner[...])

    def run(odd, even):
        cot = layer(last[...], odd[1][...], odd[0][...])[1]
        down[...] = layer(cot, even[1][...], even[0][...])[1]

    by_core(core, run, (weight, slope_own), (partner, slope_partner))
    own[...] = weight[...]
    kept[...] = local[...]


def sum_kernel(*refs):
    result = refs[-1]
    result[...] = sum(piece[...].astype(F32) for piece in refs[:GROUP]).astype(BF16)


def pass_kernel(*refs):
    refs[-2][...] = sum(piece[...].astype(F32) for piece in refs[:GROUP]).astype(BF16)
    refs[-1][...] = refs[GROUP][...]


def layers_kernel(
    where, own, partner, slope_own, slope_partner, arrived, last, own_dh, give_dh, own_cot, give_cot
):
    upstream = jnp.where(where[2] == 1, last[...], arrived[...])

    def run(odd, even):
        dh, cot = layer(upstream, odd[1][...], odd[0][...])
        odd[2][...], odd[3][...] = dh, cot
        even[2][...], even[3][...] = layer(cot, even[1][...], even[0][...])

    by_core(
        where[0], run, (own, slope_own, own_dh, own_cot), (partner, slope_partner, give_dh, give_cot)
    )


def put_factor(tokens, whole):
    width = tokens.shape[1]
    size = width // GROUP
    half = size // 2
    columns = [tokens[:, u * size:(u + 1) * size] for u in range(GROUP)]
    for u in range(GROUP):
        pair = jnp.concatenate([columns[u], columns[(u + 1) % GROUP]], axis=1)
        main = moment(columns[u], pair).astype(BF16)
        whole[u, :, :2 * size] = main[:half]
        whole[u, :, 2 * size:4 * size] = main[half:]
    for u in range(2):
        corner = moment(columns[u], columns[u + 2]).astype(BF16)
        whole[u, :, 4 * size:5 * size] = corner[:half]
        whole[u + 2, :, 4 * size:5 * size] = corner[half:]


def act_kernel(where, local, after, *refs):
    parts, (tokens, whole) = refs[:GROUP], refs[GROUP:]
    micro, rows = local.shape[:2]
    for m in range(micro):
        tokens[m * rows:(m + 1) * rows] = local[m]
    put_factor(tokens, whole)
    for step, part in enumerate(parts):
        part[...] = whole[where[1] ^ step]


def add_kernel(left, right, *refs):
    refs[-1][...] = (left[...].astype(F32) + right[...].astype(F32)).astype(BF16)


def grad_kernel(where, local, dh_own, dh_got, after, *refs):
    factors, grads, (inputs, tokens, whole, rest) = refs[:GROUP], refs[GROUP:2 * GROUP], refs[2 * GROUP:]
    rows, width = local.shape[1:]
    inputs[:rows] = local[where[0]]
    inputs[rows:] = local[1 - where[0]]
    tokens[:rows] = dh_own[...]
    tokens[rows:] = dh_got[...]
    put_factor(tokens, whole)
    size = width // GROUP
    half = size // 2
    for u in range(GROUP):
        grad = moment(inputs[:, u * size:(u + 1) * size], tokens[...]).astype(BF16)
        rest[u, :, :width] = grad[:half]
        rest[u, :, width:] = grad[half:]
    for step in range(GROUP):
        factors[step][...] = whole[where[1] ^ step]
        grads[step][...] = rest[where[1] ^ step]


def invert(total, count):
    row = lax.broadcasted_iota(jnp.int32, total.shape, 0)
    column = lax.broadcasted_iota(jnp.int32, total.shape, 1)
    eye = (row == column).astype(F32)
    ridge = 0.01
    mean = total[...].astype(F32) * (1.0 / count)
    full = mean + ridge * eye
    scale = lax.rsqrt(jnp.sum(full * full, keepdims=True))
    squared = dot(total[...], total[...]) * (1.0 / count) ** 2 + ridge * (mean + full)
    second = (2.0 * scale) * full - squared * (scale * scale)
    last = 2.0 * (eye - second) + dot(second, second)
    tail = 2.0 * last - dot(second, last)
    inner = dot(total[...], tail) * (scale * (1.0 / count))
    return split(((2.0 - ridge * scale) * tail - inner) * scale)


def inverse_kernel(count, where, *refs):
    pieces, (high, low, blocks, total) = refs[:GROUP], refs[GROUP:]
    for step, piece in enumerate(pieces):
        blocks[where[1] ^ step] = piece[...]
    size = total.shape[0] // GROUP

    def both(row, column, value):
        total[row * size:(row + 1) * size, column * size:(column + 1) * size] = value
        if row != column:
            turned = value.astype(F32).T.astype(BF16)
            total[column * size:(column + 1) * size, row * size:(row + 1) * size] = turned

    for u in range(GROUP):
        main = jnp.concatenate([blocks[u, :, :2 * size], blocks[u, :, 2 * size:4 * size]])
        both(u, u, main[:, :size])
        both(u, (u + 1) % GROUP, main[:, size:])
    for u in range(2):
        both(u, u + 2, jnp.concatenate([blocks[u, :, 4 * size:], blocks[u + 2, :, 4 * size:]]))
    for result, term in zip((high, low), invert(total, count)):
        result[...] = term


def update_kernel(where, act_high, act_low, out_high, out_low, own_cot, other_cot, *refs):
    pieces, (result, cot, grad, update, done) = refs[:GROUP], refs[GROUP:]
    copies = [
        pltpu.make_async_copy(own_cot, cot.at[where[0]], done.at[0]),
        pltpu.make_async_copy(other_cot, cot.at[1 - where[0]], done.at[1]),
    ]
    for copy in copies:
        copy.start()
    half, twice = pieces[0].shape
    width = twice // 2
    for step, piece in enumerate(pieces):
        start = pl.multiple_of((where[1] ^ step) * 2 * half, 2 * half)
        grad[pl.ds(start, half)] = piece[:, :width]
        grad[pl.ds(start + half, half)] = piece[:, width:]
    left = (dot(act_high[...], grad[...]) + dot(act_low[...], grad[...])).astype(BF16)
    for part in range(2):
        rows = slice(part * width // 2, (part + 1) * width // 2)
        update[rows] = dot(left[rows], out_high[...]) + dot(left[rows], out_low[...])
        copies.append(pltpu.make_async_copy(update.at[rows], result.at[rows], done.at[2 + part]))
        copies[-1].start()
    for copy in copies:
        copy.wait()


def send(parts):
    got = {0: parts[0]}
    for step in (3, 1, 2):
        got[step] = lax.ppermute(parts[step], ("near", "side"), [(i, i ^ step) for i in range(GROUP)])
    return [got[step] for step in range(GROUP)]


def exchange(value, after=(), flops=0):
    step = 1
    while step < lax.axis_size("far"):
        route = [(i, i ^ step) for i in range(lax.axis_size("far"))]
        got = lax.ppermute(value, "far", route)
        value = call(add_kernel, flops, value, [VMEM] * 2 + [ANY] * len(after))(value, got, *after)
        step *= 2
    return value


def body(acts, weights, cot_last):
    pairs = lax.axis_size("row")
    row = lax.axis_index("row")
    core = lax.axis_index("core")
    weight = weights[0]
    local = acts[0]
    micro, rows, width = local.shape
    tokens = micro * rows
    count = tokens * GROUP * lax.axis_size("far")
    odd = core == 1
    top = row == pairs - 1
    where = jnp.stack([core, lax.axis_index(("near", "side")), top.astype(jnp.int32)]).astype(jnp.int32)

    def mine_of(pair):
        return jnp.where(odd, pair[1], pair[0])

    def array(*shape, dtype=BF16):
        return jax.ShapeDtypeStruct(shape, dtype)

    def near_copy(value):
        return jnp.where(core > 1, jnp.zeros_like(value), value)

    partner = lax.ppermute(weight, "core", SWAP)
    partner_local = lax.ppermute(local, "core", SWAP)
    block = array(rows, width)
    slope = array(rows, width, dtype=F32)
    own, kept, last, slope_own, slope_partner, down = call(
        first_kernel,
        8 * rows * width**2,
        [array(width, width), array(micro, rows, width), block, slope, slope, block],
        [SMEM] + [VMEM] * 5,
    )(where, near_copy(weight), near_copy(local), near_copy(cot_last), partner, partner_local)
    first = down
    for turn in range(1, pairs):
        upstream = lax.ppermute(down, "row", [(r, r - 1) for r in range(1, pairs)])
        arrived = upstream if turn == 1 else jnp.where(row == pairs - 1 - turn, upstream, arrived)
        if turn < pairs - 1:
            cot = layer(upstream, mine_of((slope_partner, slope_own)), mine_of((partner, own)))[1]
            down = layer(cot, mine_of((slope_own, slope_partner)), mine_of((own, partner)))[1]

    size = width // GROUP
    factor = 5 * size
    act_parts = call(
        act_kernel,
        2 * tokens * width**2,
        [array(size // 2, factor)] * GROUP,
        [SMEM, VMEM, ANY],
        [pltpu.VMEM((tokens, width), BF16), pltpu.VMEM((GROUP, size // 2, factor), BF16)],
    )(where, kept, first)
    act_pieces = send(act_parts)

    own_dh, give_dh, own_cot, give_cot = call(
        layers_kernel, 64 * rows * width**2, [block] * 4, [SMEM] + [VMEM] * 6
    )(where, own, partner, slope_own, slope_partner, arrived, last)
    act_sum = call(sum_kernel, 24 * width**3, array(size // 2, factor), [VMEM] * GROUP + [ANY])(
        *(act_pieces[step] for step in (0, 3, 1, 2)), own_dh
    )
    got_dh = lax.ppermute(give_dh, "core", SWAP)
    other_cot = lax.ppermute(give_cot, "core", SWAP)

    parts = call(
        grad_kernel,
        4 * tokens * width**2,
        [array(size // 2, factor)] * GROUP + [array(size // 2, 2 * width)] * GROUP,
        [SMEM] + [VMEM] * 3 + [ANY],
        [pltpu.VMEM((tokens, width), BF16)] * 2
        + [pltpu.VMEM((GROUP, size // 2, factor), BF16), pltpu.VMEM((GROUP, size // 2, 2 * width), BF16)],
    )(where, kept, own_dh, got_dh, act_sum)

    def summed(pieces):
        shape = array(*pieces[0].shape)
        return call(sum_kernel, 0, shape, [VMEM] * GROUP)(*(pieces[step] for step in (0, 3, 1, 2)))

    pieces = send(parts[:GROUP])
    factors, act_part = call(
        pass_kernel, 0, [array(size // 2, factor)] * 2, [VMEM] * (GROUP + 1)
    )(*(pieces[step] for step in (0, 3, 1, 2)), exchange(act_sum, flops=16 * width**3))
    out = send([exchange(factors)] * GROUP)
    act = send([act_part] * GROUP)
    total = summed(send(parts[GROUP:]))

    def inverse(pieces, flops):
        return call(
            functools.partial(inverse_kernel, count),
            flops,
            [array(width, width)] * 2,
            [SMEM] + [VMEM] * GROUP,
            [pltpu.VMEM((GROUP, size // 2, factor), BF16), pltpu.VMEM((width, width), BF16)],
        )(where, *pieces)

    act_inv = inverse(act, 0)
    grad = send([exchange(total, (act_inv[0], *out))] * GROUP)
    update, cot = call(
        update_kernel,
        10 * width**3,
        [array(width, width, dtype=F32), array(micro, rows, width)],
        [SMEM] + [VMEM] * (6 + GROUP),
        [
            pltpu.VMEM((width, width), BF16),
            pltpu.VMEM((width, width), F32),
            pltpu.SemaphoreType.DMA((4,)),
        ],
        HBM,
    )(where, *act_inv, *inverse(out, 20 * width**3), own_cot, other_cot, *grad)
    return (cot[None], update[None])


def solution(mesh):
    sections, shards = mesh.devices.shape
    finer = Mesh(
        np.reshape(mesh.devices, (sections // 2, 2, shards // GROUP, 2, 2)),
        ("row", "core", "far", "near", "side"),
    )
    section, dp = ("row", "core"), ("far", "near", "side")
    placed = (P(section, None, dp, None), P(section, None, None), P(None, dp, None))
    return jax.shard_map(
        body,
        mesh=finer,
        in_specs=placed,
        out_specs=(P(section, None, dp, None), P(section, None, None)),
        check_vma=False,
    )
```

```python
import functools

import jax
import jax.numpy as jnp
import numpy as np
from jax import lax
from jax.experimental import pallas as pl
from jax.experimental.pallas import tpu as pltpu
from jax.sharding import Mesh, PartitionSpec as P

BF16 = jnp.bfloat16
F32 = jnp.float32
SWAP = [(0, 1), (1, 0)]
SMEM = pl.BlockSpec(memory_space=pltpu.SMEM)
VMEM = pl.BlockSpec(memory_space=pltpu.VMEM)
ANY = pl.BlockSpec(memory_space=pl.ANY)
HBM = pl.BlockSpec(memory_space=pltpu.HBM)
GROUP = 4


def silu_slope(pre):
    sig = jax.nn.sigmoid(pre)
    return sig * (1.0 + pre * (1.0 - sig))


def slope_of(inputs, matrix):
    return silu_slope(jnp.dot(inputs, matrix, preferred_element_type=F32))


def layer(upstream, slope, matrix):
    dh = (upstream.astype(F32) * slope).astype(BF16)
    back = lax.dot_general(dh, matrix, (((1,), (1,)), ((), ())), preferred_element_type=F32)
    return dh, (upstream.astype(F32) + back).astype(BF16)


def by_core(core, run, own, partner):
    @pl.when(core == 1)
    def _():
        run(own, partner)

    @pl.when(core == 0)
    def _():
        run(partner, own)


def moment(left, right):
    return lax.dot_general(left, right, (((0,), (0,)), ((), ())), preferred_element_type=F32)


def split(value):
    high = value.astype(BF16)
    return high, (value - high.astype(F32)).astype(BF16)


def dot(left, right):
    return jnp.dot(left.astype(BF16), right.astype(BF16), preferred_element_type=F32)


def call(kernel, flops, out_shape, in_specs, scratch=(), out_spec=VMEM):
    return pl.pallas_call(
        kernel,
        out_shape=jax.tree.map(lambda v: jax.ShapeDtypeStruct(v.shape, v.dtype), out_shape),
        in_specs=in_specs,
        out_specs=jax.tree.map(lambda _: out_spec, out_shape),
        scratch_shapes=list(scratch),
        cost_estimate=pl.CostEstimate(flops=flops, bytes_accessed=1 << 20, transcendentals=0),
        compiler_params=pltpu.CompilerParams(vmem_limit_bytes=32 << 20),
    )


def near_kernel(where, weight, local, slope):
    slope[...] = slope_of(local[where[0]], weight[...])


def first_kernel(where, own, partner, slope_own, partner_local, cot_last, slope_partner, down):
    core = where[0]
    slope_partner[...] = slope_of(partner_local[core], partner[...])

    def run(odd, even):
        cot = layer(cot_last[core], odd[1][...], odd[0][...])[1]
        down[...] = layer(cot, even[1][...], even[0][...])[1]

    by_core(core, run, (own, slope_own), (partner, slope_partner))


def sum_kernel(*refs):
    result = refs[-1]
    result[...] = sum(piece[...].astype(F32) for piece in refs[:GROUP]).astype(BF16)


def pass_kernel(*refs):
    refs[-2][...] = sum(piece[...].astype(F32) for piece in refs[:GROUP]).astype(BF16)
    refs[-1][...] = refs[GROUP][...]


def layers_kernel(
    where, own, partner, slope_own, slope_partner, arrived, cot_last, own_dh, give_dh, own_cot, give_cot
):
    upstream = jnp.where(where[2] == 1, cot_last[where[0]], arrived[...])

    def run(odd, even):
        dh, cot = layer(upstream, odd[1][...], odd[0][...])
        odd[2][...], odd[3][...] = dh, cot
        even[2][...], even[3][...] = layer(cot, even[1][...], even[0][...])

    by_core(
        where[0], run, (own, slope_own, own_dh, own_cot), (partner, slope_partner, give_dh, give_cot)
    )


def put_factor(tokens, whole):
    width = tokens.shape[1]
    size = width // GROUP
    half = size // 2
    columns = [tokens[:, u * size:(u + 1) * size] for u in range(GROUP)]
    for u in range(GROUP):
        pair = jnp.concatenate([columns[u], columns[(u + 1) % GROUP]], axis=1)
        main = moment(columns[u], pair).astype(BF16)
        whole[u, :, :2 * size] = main[:half]
        whole[u, :, 2 * size:4 * size] = main[half:]
    for u in range(2):
        corner = moment(columns[u], columns[u + 2]).astype(BF16)
        whole[u, :, 4 * size:5 * size] = corner[:half]
        whole[u + 2, :, 4 * size:5 * size] = corner[half:]


def act_kernel(where, local, after, *refs):
    parts, (tokens, whole) = refs[:GROUP], refs[GROUP:]
    micro, rows = local.shape[:2]
    for m in range(micro):
        tokens[m * rows:(m + 1) * rows] = local[m]
    put_factor(tokens, whole)
    for step, part in enumerate(parts):
        part[...] = whole[where[1] ^ step]


def add_kernel(left, right, *refs):
    refs[-1][...] = (left[...].astype(F32) + right[...].astype(F32)).astype(BF16)


def grad_kernel(where, local, dh_own, dh_got, after, *refs):
    factors, grads, (inputs, tokens, whole, rest) = refs[:GROUP], refs[GROUP:2 * GROUP], refs[2 * GROUP:]
    rows, width = local.shape[1:]
    inputs[:rows] = local[where[0]]
    inputs[rows:] = local[1 - where[0]]
    tokens[:rows] = dh_own[...]
    tokens[rows:] = dh_got[...]
    put_factor(tokens, whole)
    size = width // GROUP
    half = size // 2
    for u in range(GROUP):
        grad = moment(inputs[:, u * size:(u + 1) * size], tokens[...]).astype(BF16)
        rest[u, :, :width] = grad[:half]
        rest[u, :, width:] = grad[half:]
    for step in range(GROUP):
        factors[step][...] = whole[where[1] ^ step]
        grads[step][...] = rest[where[1] ^ step]


def invert(total, count):
    row = lax.broadcasted_iota(jnp.int32, total.shape, 0)
    column = lax.broadcasted_iota(jnp.int32, total.shape, 1)
    eye = (row == column).astype(F32)
    ridge = 0.01
    mean = total[...].astype(F32) * (1.0 / count)
    full = mean + ridge * eye
    scale = lax.rsqrt(jnp.sum(full * full, keepdims=True))
    squared = dot(total[...], total[...]) * (1.0 / count) ** 2 + ridge * (mean + full)
    second = (2.0 * scale) * full - squared * (scale * scale)
    last = 2.0 * (eye - second) + dot(second, second)
    tail = 2.0 * last - dot(second, last)
    inner = dot(total[...], tail) * (scale * (1.0 / count))
    return split(((2.0 - ridge * scale) * tail - inner) * scale)


def inverse_kernel(count, where, *refs):
    pieces, (high, low, blocks, total) = refs[:GROUP], refs[GROUP:]
    for step, piece in enumerate(pieces):
        blocks[where[1] ^ step] = piece[...]
    size = total.shape[0] // GROUP

    def both(row, column, value):
        total[row * size:(row + 1) * size, column * size:(column + 1) * size] = value
        if row != column:
            turned = value.astype(F32).T.astype(BF16)
            total[column * size:(column + 1) * size, row * size:(row + 1) * size] = turned

    for u in range(GROUP):
        main = jnp.concatenate([blocks[u, :, :2 * size], blocks[u, :, 2 * size:4 * size]])
        both(u, u, main[:, :size])
        both(u, (u + 1) % GROUP, main[:, size:])
    for u in range(2):
        both(u, u + 2, jnp.concatenate([blocks[u, :, 4 * size:], blocks[u + 2, :, 4 * size:]]))
    for result, term in zip((high, low), invert(total, count)):
        result[...] = term


def update_kernel(where, act_high, act_low, out_high, out_low, own_cot, other_cot, *refs):
    pieces, (result, cot, grad, update, done) = refs[:GROUP], refs[GROUP:]
    copies = [
        pltpu.make_async_copy(own_cot, cot.at[where[0]], done.at[0]),
        pltpu.make_async_copy(other_cot, cot.at[1 - where[0]], done.at[1]),
    ]
    for copy in copies:
        copy.start()
    half, twice = pieces[0].shape
    width = twice // 2
    for step, piece in enumerate(pieces):
        start = pl.multiple_of((where[1] ^ step) * 2 * half, 2 * half)
        grad[pl.ds(start, half)] = piece[:, :width]
        grad[pl.ds(start + half, half)] = piece[:, width:]
    left = (dot(act_high[...], grad[...]) + dot(act_low[...], grad[...])).astype(BF16)
    for part in range(2):
        rows = slice(part * width // 2, (part + 1) * width // 2)
        update[rows] = dot(left[rows], out_high[...]) + dot(left[rows], out_low[...])
        copies.append(pltpu.make_async_copy(update.at[rows], result.at[rows], done.at[2 + part]))
        copies[-1].start()
    for copy in copies:
        copy.wait()


def send(parts):
    got = {0: parts[0]}
    for step in (3, 1, 2):
        got[step] = lax.ppermute(parts[step], ("near", "side"), [(i, i ^ step) for i in range(GROUP)])
    return [got[step] for step in range(GROUP)]


def exchange(value, after=(), flops=0):
    step = 1
    while step < lax.axis_size("far"):
        route = [(i, i ^ step) for i in range(lax.axis_size("far"))]
        got = lax.ppermute(value, "far", route)
        value = call(add_kernel, flops, value, [VMEM] * 2 + [ANY] * len(after))(value, got, *after)
        step *= 2
    return value


def body(acts, weights, cot_last):
    pairs = lax.axis_size("row")
    row = lax.axis_index("row")
    core = lax.axis_index("core")
    weight = weights[0]
    local = acts[0]
    micro, rows, width = local.shape
    tokens = micro * rows
    count = tokens * GROUP * lax.axis_size("far")
    odd = core == 1
    top = row == pairs - 1
    where = jnp.stack([core, lax.axis_index(("near", "side")), top.astype(jnp.int32)]).astype(jnp.int32)

    def mine_of(pair):
        return jnp.where(odd, pair[1], pair[0])

    def array(*shape, dtype=BF16):
        return jax.ShapeDtypeStruct(shape, dtype)

    def near_copy(value):
        return jnp.where(core > 1, jnp.zeros_like(value), value)

    partner = lax.ppermute(weight, "core", SWAP)
    partner_local = lax.ppermute(local, "core", SWAP)
    block = array(rows, width)
    slope = array(rows, width, dtype=F32)
    own, kept, last = near_copy(weight), near_copy(local), near_copy(cot_last)
    slope_own = call(near_kernel, 2 * rows * width**2, slope, [SMEM] + [VMEM] * 2)(where, own, kept)
    slope_partner, down = call(first_kernel, 6 * rows * width**2, [slope, block], [SMEM] + [VMEM] * 5)(
        where, own, partner, slope_own, partner_local, last
    )
    first = down
    for turn in range(1, pairs):
        upstream = lax.ppermute(down, "row", [(r, r - 1) for r in range(1, pairs)])
        arrived = upstream if turn == 1 else jnp.where(row == pairs - 1 - turn, upstream, arrived)
        if turn < pairs - 1:
            cot = layer(upstream, mine_of((slope_partner, slope_own)), mine_of((partner, own)))[1]
            down = layer(cot, mine_of((slope_own, slope_partner)), mine_of((own, partner)))[1]

    size = width // GROUP
    factor = 5 * size
    act_parts = call(
        act_kernel,
        2 * tokens * width**2,
        [array(size // 2, factor)] * GROUP,
        [SMEM, VMEM, ANY],
        [pltpu.VMEM((tokens, width), BF16), pltpu.VMEM((GROUP, size // 2, factor), BF16)],
    )(where, kept, first)
    act_pieces = send(act_parts)

    own_dh, give_dh, own_cot, give_cot = call(
        layers_kernel, 64 * rows * width**2, [block] * 4, [SMEM] + [VMEM] * 6
    )(where, own, partner, slope_own, slope_partner, arrived, last)
    act_sum = call(sum_kernel, 24 * width**3, array(size // 2, factor), [VMEM] * GROUP + [ANY])(
        *(act_pieces[step] for step in (0, 3, 1, 2)), own_dh
    )
    got_dh = lax.ppermute(give_dh, "core", SWAP)
    other_cot = lax.ppermute(give_cot, "core", SWAP)

    parts = call(
        grad_kernel,
        4 * tokens * width**2,
        [array(size // 2, factor)] * GROUP + [array(size // 2, 2 * width)] * GROUP,
        [SMEM] + [VMEM] * 3 + [ANY],
        [pltpu.VMEM((tokens, width), BF16)] * 2
        + [pltpu.VMEM((GROUP, size // 2, factor), BF16), pltpu.VMEM((GROUP, size // 2, 2 * width), BF16)],
    )(where, kept, own_dh, got_dh, act_sum)

    def summed(pieces):
        shape = array(*pieces[0].shape)
        return call(sum_kernel, 0, shape, [VMEM] * GROUP)(*(pieces[step] for step in (0, 3, 1, 2)))

    pieces = send(parts[:GROUP])
    factors, act_part = call(
        pass_kernel, 0, [array(size // 2, factor)] * 2, [VMEM] * (GROUP + 1)
    )(*(pieces[step] for step in (0, 3, 1, 2)), exchange(act_sum, flops=16 * width**3))
    out = send([exchange(factors)] * GROUP)
    act = send([act_part] * GROUP)
    total = summed(send(parts[GROUP:]))

    def inverse(pieces, flops):
        return call(
            functools.partial(inverse_kernel, count),
            flops,
            [array(width, width)] * 2,
            [SMEM] + [VMEM] * GROUP,
            [pltpu.VMEM((GROUP, size // 2, factor), BF16), pltpu.VMEM((width, width), BF16)],
        )(where, *pieces)

    act_inv = inverse(act, 0)
    grad = send([exchange(total, (act_inv[0], *out))] * GROUP)
    update, cot = call(
        update_kernel,
        10 * width**3,
        [array(width, width, dtype=F32), array(micro, rows, width)],
        [SMEM] + [VMEM] * (6 + GROUP),
        [
            pltpu.VMEM((width, width), BF16),
            pltpu.VMEM((width, width), F32),
            pltpu.SemaphoreType.DMA((4,)),
        ],
        HBM,
    )(where, *act_inv, *inverse(out, 20 * width**3), own_cot, other_cot, *grad)
    return (cot[None], update[None])


def solution(mesh):
    sections, shards = mesh.devices.shape
    finer = Mesh(
        np.reshape(mesh.devices, (sections // 2, 2, shards // GROUP, 2, 2)),
        ("row", "core", "far", "near", "side"),
    )
    section, dp = ("row", "core"), ("far", "near", "side")
    placed = (P(section, None, dp, None), P(section, None, None), P(None, dp, None))
    return jax.shard_map(
        body,
        mesh=finer,
        in_specs=placed,
        out_specs=(P(section, None, dp, None), P(section, None, None)),
        check_vma=False,
    )
```

```python
import functools

import jax
import jax.numpy as jnp
import numpy as np
from jax import lax
from jax.experimental import pallas as pl
from jax.experimental.pallas import tpu as pltpu
from jax.sharding import Mesh, PartitionSpec as P

BF16 = jnp.bfloat16
F32 = jnp.float32
SWAP = [(0, 1), (1, 0)]
VMEM = pl.BlockSpec(memory_space=pltpu.VMEM)
ANY = pl.BlockSpec(memory_space=pl.ANY)
HBM = pl.BlockSpec(memory_space=pltpu.HBM)
GROUP = 4


def silu_slope(pre):
    sig = jax.nn.sigmoid(pre)
    return sig * (1.0 + pre * (1.0 - sig))


def slope_of(inputs, matrix):
    return silu_slope(jnp.dot(inputs, matrix, preferred_element_type=F32))


def layer(upstream, slope, matrix):
    dh = (upstream.astype(F32) * slope).astype(BF16)
    back = lax.dot_general(dh, matrix, (((1,), (1,)), ((), ())), preferred_element_type=F32)
    return dh, (upstream.astype(F32) + back).astype(BF16)


def by_core(core, run, own, partner):
    @pl.when(core == 1)
    def _():
        run(own, partner)

    @pl.when(core == 0)
    def _():
        run(partner, own)


def moment(left, right):
    return lax.dot_general(left, right, (((0,), (0,)), ((), ())), preferred_element_type=F32)


def group_place():
    return 2 * lax.axis_index("near") + lax.axis_index("side")


def split(value):
    high = value.astype(BF16)
    return high, (value - high.astype(F32)).astype(BF16)


def dot(left, right):
    return jnp.dot(left.astype(BF16), right.astype(BF16), preferred_element_type=F32)


def call(kernel, flops, out_shape, in_specs, scratch=(), out_spec=VMEM):
    return pl.pallas_call(
        kernel,
        out_shape=jax.tree.map(lambda v: jax.ShapeDtypeStruct(v.shape, v.dtype), out_shape),
        in_specs=in_specs,
        out_specs=jax.tree.map(lambda _: out_spec, out_shape),
        scratch_shapes=list(scratch),
        cost_estimate=pl.CostEstimate(flops=flops, bytes_accessed=1 << 20, transcendentals=0),
        compiler_params=pltpu.CompilerParams(vmem_limit_bytes=32 << 20),
    )


def first_kernel(
    weight, local, cot_last, partner, partner_local,
    own, kept, last, slope_own, slope_partner, down,
):
    core = lax.axis_index("core")
    last[...] = cot_last[core]
    slope_own[...] = slope_of(local[core], weight[...])
    slope_partner[...] = slope_of(partner_local[core], partner[...])

    def run(odd, even):
        cot = layer(last[...], odd[1][...], odd[0][...])[1]
        down[...] = layer(cot, even[1][...], even[0][...])[1]

    by_core(core, run, (weight, slope_own), (partner, slope_partner))
    own[...] = weight[...]
    kept[...] = local[...]


def sum_kernel(*refs):
    result = refs[-1]
    result[...] = sum(piece[...].astype(F32) for piece in refs[:GROUP]).astype(BF16)


def pass_kernel(*refs):
    refs[-2][...] = sum(piece[...].astype(F32) for piece in refs[:GROUP]).astype(BF16)
    refs[-1][...] = refs[GROUP][...]


def layers_kernel(
    own, partner, slope_own, slope_partner, arrived, last, own_dh, give_dh, own_cot, give_cot
):
    upstream = jnp.where(lax.axis_index("row") == lax.axis_size("row") - 1, last[...], arrived[...])

    def run(odd, even):
        dh, cot = layer(upstream, odd[1][...], odd[0][...])
        odd[2][...], odd[3][...] = dh, cot
        even[2][...], even[3][...] = layer(cot, even[1][...], even[0][...])

    by_core(
        lax.axis_index("core"), run, (own, slope_own, own_dh, own_cot), (partner, slope_partner, give_dh, give_cot)
    )


def put_factor(tokens, whole):
    width = tokens.shape[1]
    size = width // GROUP
    half = size // 2
    columns = [tokens[:, u * size:(u + 1) * size] for u in range(GROUP)]
    for u in range(GROUP):
        pair = jnp.concatenate([columns[u], columns[(u + 1) % GROUP]], axis=1)
        main = moment(columns[u], pair).astype(BF16)
        whole[u, :, :2 * size] = main[:half]
        whole[u, :, 2 * size:4 * size] = main[half:]
    for u in range(2):
        corner = moment(columns[u], columns[u + 2]).astype(BF16)
        whole[u, :, 4 * size:5 * size] = corner[:half]
        whole[u + 2, :, 4 * size:5 * size] = corner[half:]


def act_kernel(local, after, *refs):
    parts, (tokens, whole) = refs[:GROUP], refs[GROUP:]
    micro, rows = local.shape[:2]
    for m in range(micro):
        tokens[m * rows:(m + 1) * rows] = local[m]
    put_factor(tokens, whole)
    for step, part in enumerate(parts):
        part[...] = whole[group_place() ^ step]


def add_kernel(left, right, *refs):
    refs[-1][...] = (left[...].astype(F32) + right[...].astype(F32)).astype(BF16)


def grad_kernel(local, dh_own, dh_got, after, *refs):
    factors, grads, (inputs, tokens, whole, rest) = refs[:GROUP], refs[GROUP:2 * GROUP], refs[2 * GROUP:]
    rows, width = local.shape[1:]
    inputs[:rows] = local[lax.axis_index("core")]
    inputs[rows:] = local[1 - lax.axis_index("core")]
    tokens[:rows] = dh_own[...]
    tokens[rows:] = dh_got[...]
    put_factor(tokens, whole)
    size = width // GROUP
    half = size // 2
    for u in range(GROUP):
        grad = moment(inputs[:, u * size:(u + 1) * size], tokens[...]).astype(BF16)
        rest[u, :, :width] = grad[:half]
        rest[u, :, width:] = grad[half:]
    for step in range(GROUP):
        factors[step][...] = whole[group_place() ^ step]
        grads[step][...] = rest[group_place() ^ step]


def invert(total, count):
    row = lax.broadcasted_iota(jnp.int32, total.shape, 0)
    column = lax.broadcasted_iota(jnp.int32, total.shape, 1)
    eye = (row == column).astype(F32)
    ridge = 0.01
    mean = total[...].astype(F32) * (1.0 / count)
    full = mean + ridge * eye
    scale = lax.rsqrt(jnp.sum(full * full, keepdims=True))
    squared = dot(total[...], total[...]) * (1.0 / count) ** 2 + ridge * (mean + full)
    second = (2.0 * scale) * full - squared * (scale * scale)
    last = 2.0 * (eye - second) + dot(second, second)
    tail = 2.0 * last - dot(second, last)
    inner = dot(total[...], tail) * (scale * (1.0 / count))
    return split(((2.0 - ridge * scale) * tail - inner) * scale)


def inverse_kernel(count, *refs):
    pieces, (high, low, blocks, total) = refs[:GROUP], refs[GROUP:]
    for step, piece in enumerate(pieces):
        blocks[group_place() ^ step] = piece[...]
    size = total.shape[0] // GROUP

    def both(row, column, value):
        total[row * size:(row + 1) * size, column * size:(column + 1) * size] = value
        if row != column:
            turned = value.astype(F32).T.astype(BF16)
            total[column * size:(column + 1) * size, row * size:(row + 1) * size] = turned

    for u in range(GROUP):
        main = jnp.concatenate([blocks[u, :, :2 * size], blocks[u, :, 2 * size:4 * size]])
        both(u, u, main[:, :size])
        both(u, (u + 1) % GROUP, main[:, size:])
    for u in range(2):
        both(u, u + 2, jnp.concatenate([blocks[u, :, 4 * size:], blocks[u + 2, :, 4 * size:]]))
    for result, term in zip((high, low), invert(total, count)):
        result[...] = term


def update_kernel(act_high, act_low, out_high, out_low, own_cot, other_cot, *refs):
    pieces, (result, cot, grad, update, done) = refs[:GROUP], refs[GROUP:]
    copies = [
        pltpu.make_async_copy(own_cot, cot.at[lax.axis_index("core")], done.at[0]),
        pltpu.make_async_copy(other_cot, cot.at[1 - lax.axis_index("core")], done.at[1]),
    ]
    for copy in copies:
        copy.start()
    half, twice = pieces[0].shape
    width = twice // 2
    for step, piece in enumerate(pieces):
        start = pl.multiple_of((group_place() ^ step) * 2 * half, 2 * half)
        grad[pl.ds(start, half)] = piece[:, :width]
        grad[pl.ds(start + half, half)] = piece[:, width:]
    left = (dot(act_high[...], grad[...]) + dot(act_low[...], grad[...])).astype(BF16)
    for part in range(2):
        rows = slice(part * width // 2, (part + 1) * width // 2)
        update[rows] = dot(left[rows], out_high[...]) + dot(left[rows], out_low[...])
        copies.append(pltpu.make_async_copy(update.at[rows], result.at[rows], done.at[2 + part]))
        copies[-1].start()
    for copy in copies:
        copy.wait()


def send(parts):
    got = {0: parts[0]}
    for step in (3, 1, 2):
        got[step] = lax.ppermute(parts[step], ("near", "side"), [(i, i ^ step) for i in range(GROUP)])
    return [got[step] for step in range(GROUP)]


def exchange(value, after=(), flops=0):
    step = 1
    while step < lax.axis_size("far"):
        route = [(i, i ^ step) for i in range(lax.axis_size("far"))]
        got = lax.ppermute(value, "far", route)
        value = call(add_kernel, flops, value, [VMEM] * 2 + [ANY] * len(after))(value, got, *after)
        step *= 2
    return value


def body(acts, weights, cot_last):
    pairs = lax.axis_size("row")
    row = lax.axis_index("row")
    core = lax.axis_index("core")
    weight = weights[0]
    local = acts[0]
    micro, rows, width = local.shape
    tokens = micro * rows
    count = tokens * GROUP * lax.axis_size("far")
    odd = core == 1

    def mine_of(pair):
        return jnp.where(odd, pair[1], pair[0])

    def array(*shape, dtype=BF16):
        return jax.ShapeDtypeStruct(shape, dtype)

    def near_copy(value):
        return jnp.where(core > 1, jnp.zeros_like(value), value)

    partner = lax.ppermute(weight, "core", SWAP)
    partner_local = lax.ppermute(local, "core", SWAP)
    block = array(rows, width)
    slope = array(rows, width, dtype=F32)
    own, kept, last, slope_own, slope_partner, down = call(
        first_kernel,
        8 * rows * width**2,
        [array(width, width), array(micro, rows, width), block, slope, slope, block],
        [VMEM] * 5,
    )(near_copy(weight), near_copy(local), near_copy(cot_last), partner, partner_local)
    first = down
    for turn in range(1, pairs):
        upstream = lax.ppermute(down, "row", [(r, r - 1) for r in range(1, pairs)])
        arrived = upstream if turn == 1 else jnp.where(row == pairs - 1 - turn, upstream, arrived)
        if turn < pairs - 1:
            cot = layer(upstream, mine_of((slope_partner, slope_own)), mine_of((partner, own)))[1]
            down = layer(cot, mine_of((slope_own, slope_partner)), mine_of((own, partner)))[1]

    size = width // GROUP
    factor = 5 * size
    act_parts = call(
        act_kernel,
        2 * tokens * width**2,
        [array(size // 2, factor)] * GROUP,
        [VMEM, ANY],
        [pltpu.VMEM((tokens, width), BF16), pltpu.VMEM((GROUP, size // 2, factor), BF16)],
    )(kept, first)
    act_pieces = send(act_parts)

    own_dh, give_dh, own_cot, give_cot = call(
        layers_kernel, 64 * rows * width**2, [block] * 4, [VMEM] * 6
    )(own, partner, slope_own, slope_partner, arrived, last)
    act_sum = call(sum_kernel, 24 * width**3, array(size // 2, factor), [VMEM] * GROUP + [ANY])(
        *(act_pieces[step] for step in (0, 3, 1, 2)), own_dh
    )
    got_dh = lax.ppermute(give_dh, "core", SWAP)
    other_cot = lax.ppermute(give_cot, "core", SWAP)

    parts = call(
        grad_kernel,
        4 * tokens * width**2,
        [array(size // 2, factor)] * GROUP + [array(size // 2, 2 * width)] * GROUP,
        [VMEM] * 3 + [ANY],
        [pltpu.VMEM((tokens, width), BF16)] * 2
        + [pltpu.VMEM((GROUP, size // 2, factor), BF16), pltpu.VMEM((GROUP, size // 2, 2 * width), BF16)],
    )(kept, own_dh, got_dh, act_sum)

    def summed(pieces):
        shape = array(*pieces[0].shape)
        return call(sum_kernel, 0, shape, [VMEM] * GROUP)(*(pieces[step] for step in (0, 3, 1, 2)))

    pieces = send(parts[:GROUP])
    factors, act_part = call(
        pass_kernel, 0, [array(size // 2, factor)] * 2, [VMEM] * (GROUP + 1)
    )(*(pieces[step] for step in (0, 3, 1, 2)), exchange(act_sum, flops=16 * width**3))
    out = send([exchange(factors)] * GROUP)
    act = send([act_part] * GROUP)
    total = summed(send(parts[GROUP:]))

    def inverse(pieces, flops):
        return call(
            functools.partial(inverse_kernel, count),
            flops,
            [array(width, width)] * 2,
            [VMEM] * GROUP,
            [pltpu.VMEM((GROUP, size // 2, factor), BF16), pltpu.VMEM((width, width), BF16)],
        )(*pieces)

    act_inv = inverse(act, 0)
    grad = send([exchange(total, (act_inv[0], *out))] * GROUP)
    update, cot = call(
        update_kernel,
        10 * width**3,
        [array(width, width, dtype=F32), array(micro, rows, width)],
        [VMEM] * (6 + GROUP),
        [
            pltpu.VMEM((width, width), BF16),
            pltpu.VMEM((width, width), F32),
            pltpu.SemaphoreType.DMA((4,)),
        ],
        HBM,
    )(*act_inv, *inverse(out, 20 * width**3), own_cot, other_cot, *grad)
    return (cot[None], update[None])


def solution(mesh):
    sections, shards = mesh.devices.shape
    finer = Mesh(
        np.reshape(mesh.devices, (sections // 2, 2, shards // GROUP, 2, 2)),
        ("row", "core", "far", "near", "side"),
    )
    section, dp = ("row", "core"), ("far", "near", "side")
    placed = (P(section, None, dp, None), P(section, None, None), P(None, dp, None))
    return jax.shard_map(
        body,
        mesh=finer,
        in_specs=placed,
        out_specs=(P(section, None, dp, None), P(section, None, None)),
        check_vma=False,
    )
```

```python
import functools

import jax
import jax.numpy as jnp
import numpy as np
from jax import lax
from jax.experimental import pallas as pl
from jax.experimental.pallas import tpu as pltpu
from jax.sharding import Mesh, PartitionSpec as P

BF16 = jnp.bfloat16
F32 = jnp.float32
SWAP = [(0, 1), (1, 0)]
VMEM = pl.BlockSpec(memory_space=pltpu.VMEM)
ANY = pl.BlockSpec(memory_space=pl.ANY)
HBM = pl.BlockSpec(memory_space=pltpu.HBM)
GROUP = 4


def silu_slope(pre):
    sig = jax.nn.sigmoid(pre)
    return sig * (1.0 + pre * (1.0 - sig))


def slope_of(inputs, matrix):
    return silu_slope(jnp.dot(inputs, matrix, preferred_element_type=F32))


def layer(upstream, slope, matrix):
    dh = (upstream.astype(F32) * slope).astype(BF16)
    back = lax.dot_general(dh, matrix, (((1,), (1,)), ((), ())), preferred_element_type=F32)
    return dh, (upstream.astype(F32) + back).astype(BF16)


def by_core(core, run, own, partner):
    @pl.when(core == 1)
    def _():
        run(own, partner)

    @pl.when(core == 0)
    def _():
        run(partner, own)


def moment(left, right):
    return lax.dot_general(left, right, (((0,), (0,)), ((), ())), preferred_element_type=F32)


def group_place():
    return 2 * lax.axis_index("near") + lax.axis_index("side")


def split(value):
    high = value.astype(BF16)
    return high, (value - high.astype(F32)).astype(BF16)


def dot(left, right):
    return jnp.dot(left.astype(BF16), right.astype(BF16), preferred_element_type=F32)


def call(kernel, flops, out_shape, in_specs, scratch=(), out_spec=VMEM):
    return pl.pallas_call(
        kernel,
        out_shape=jax.tree.map(lambda v: jax.ShapeDtypeStruct(v.shape, v.dtype), out_shape),
        in_specs=in_specs,
        out_specs=jax.tree.map(lambda _: out_spec, out_shape),
        scratch_shapes=list(scratch),
        cost_estimate=pl.CostEstimate(flops=flops, bytes_accessed=1 << 20, transcendentals=0),
        compiler_params=pltpu.CompilerParams(vmem_limit_bytes=32 << 20),
    )


def first_kernel(
    weight, local, cot_last, partner, partner_local,
    own, kept, last, slope_own, slope_partner, down,
):
    core = lax.axis_index("core")
    last[...] = cot_last[core]
    slope_own[...] = slope_of(local[core], weight[...])
    slope_partner[...] = slope_of(partner_local[core], partner[...])

    def run(odd, even):
        cot = layer(last[...], odd[1][...], odd[0][...])[1]
        down[...] = layer(cot, even[1][...], even[0][...])[1]

    by_core(core, run, (weight, slope_own), (partner, slope_partner))
    own[...] = weight[...]
    kept[...] = local[...]


def sum_kernel(*refs):
    result = refs[-1]
    result[...] = sum(piece[...].astype(F32) for piece in refs[:GROUP]).astype(BF16)


def pass_kernel(*refs):
    refs[-2][...] = sum(piece[...].astype(F32) for piece in refs[:GROUP]).astype(BF16)
    refs[-1][...] = refs[GROUP][...]


def layers_kernel(
    own, partner, slope_own, slope_partner, arrived, last, own_dh, give_dh, own_cot, give_cot
):
    upstream = jnp.where(lax.axis_index("row") == lax.axis_size("row") - 1, last[...], arrived[...])

    def run(odd, even):
        dh, cot = layer(upstream, odd[1][...], odd[0][...])
        odd[2][...], odd[3][...] = dh, cot
        even[2][...], even[3][...] = layer(cot, even[1][...], even[0][...])

    by_core(
        lax.axis_index("core"), run, (own, slope_own, own_dh, own_cot), (partner, slope_partner, give_dh, give_cot)
    )


def put_factor(tokens, whole):
    width = tokens.shape[1]
    size = width // GROUP
    half = size // 2
    columns = [tokens[:, u * size:(u + 1) * size] for u in range(GROUP)]
    for u in range(GROUP):
        pair = jnp.concatenate([columns[u], columns[(u + 1) % GROUP]], axis=1)
        main = moment(columns[u], pair).astype(BF16)
        whole[u, :, :2 * size] = main[:half]
        whole[u, :, 2 * size:4 * size] = main[half:]
    for u in range(2):
        corner = moment(columns[u], columns[u + 2]).astype(BF16)
        whole[u, :, 4 * size:5 * size] = corner[:half]
        whole[u + 2, :, 4 * size:5 * size] = corner[half:]


def act_kernel(local, after, *refs):
    parts, (tokens, whole) = refs[:GROUP], refs[GROUP:]
    micro, rows = local.shape[:2]
    for m in range(micro):
        tokens[m * rows:(m + 1) * rows] = local[m]
    put_factor(tokens, whole)
    for step, part in enumerate(parts):
        part[...] = whole[group_place() ^ step]


def add_kernel(left, right, *refs):
    refs[-1][...] = (left[...].astype(F32) + right[...].astype(F32)).astype(BF16)


def grad_kernel(local, dh_own, dh_got, after, *refs):
    factors, grads, (inputs, tokens, whole, rest) = refs[:GROUP], refs[GROUP:2 * GROUP], refs[2 * GROUP:]
    rows, width = local.shape[1:]
    inputs[:rows] = local[lax.axis_index("core")]
    inputs[rows:] = local[1 - lax.axis_index("core")]
    tokens[:rows] = dh_own[...]
    tokens[rows:] = dh_got[...]
    put_factor(tokens, whole)
    size = width // GROUP
    half = size // 2
    for u in range(GROUP):
        grad = moment(inputs[:, u * size:(u + 1) * size], tokens[...]).astype(BF16)
        rest[u, :, :width] = grad[:half]
        rest[u, :, width:] = grad[half:]
    for step in range(GROUP):
        factors[step][...] = whole[group_place() ^ step]
        grads[step][...] = rest[group_place() ^ step]


def invert(total, count):
    row = lax.broadcasted_iota(jnp.int32, total.shape, 0)
    column = lax.broadcasted_iota(jnp.int32, total.shape, 1)
    eye = (row == column).astype(F32)
    ridge = 0.01
    mean = total[...].astype(F32) * (1.0 / count)
    full = mean + ridge * eye
    scale = lax.rsqrt(jnp.sum(full * full, keepdims=True))
    squared = dot(total[...], total[...]) * (1.0 / count) ** 2 + ridge * (mean + full)
    second = (2.0 * scale) * full - squared * (scale * scale)
    last = 2.0 * (eye - second) + dot(second, second)
    tail = 2.0 * last - dot(second, last)
    inner = dot(total[...], tail) * (scale * (1.0 / count))
    return split(((2.0 - ridge * scale) * tail - inner) * scale)


def inverse_kernel(count, through, after, *refs):
    pieces, (high, low, through_copy, blocks, total) = refs[:GROUP], refs[GROUP:]
    through_copy[...] = through[...]
    for step, piece in enumerate(pieces):
        blocks[group_place() ^ step] = piece[...]
    size = total.shape[0] // GROUP

    def both(row, column, value):
        total[row * size:(row + 1) * size, column * size:(column + 1) * size] = value
        if row != column:
            turned = value.astype(F32).T.astype(BF16)
            total[column * size:(column + 1) * size, row * size:(row + 1) * size] = turned

    for u in range(GROUP):
        main = jnp.concatenate([blocks[u, :, :2 * size], blocks[u, :, 2 * size:4 * size]])
        both(u, u, main[:, :size])
        both(u, (u + 1) % GROUP, main[:, size:])
    for u in range(2):
        both(u, u + 2, jnp.concatenate([blocks[u, :, 4 * size:], blocks[u + 2, :, 4 * size:]]))
    for result, term in zip((high, low), invert(total, count)):
        result[...] = term


def update_kernel(act_high, act_low, out_high, out_low, own_cot, other_cot, *refs):
    pieces, (result, cot, grad, update, done) = refs[:GROUP], refs[GROUP:]
    copies = [
        pltpu.make_async_copy(own_cot, cot.at[lax.axis_index("core")], done.at[0]),
        pltpu.make_async_copy(other_cot, cot.at[1 - lax.axis_index("core")], done.at[1]),
    ]
    for copy in copies:
        copy.start()
    half, twice = pieces[0].shape
    width = twice // 2
    for step, piece in enumerate(pieces):
        start = pl.multiple_of((group_place() ^ step) * 2 * half, 2 * half)
        grad[pl.ds(start, half)] = piece[:, :width]
        grad[pl.ds(start + half, half)] = piece[:, width:]
    left = (dot(act_high[...], grad[...]) + dot(act_low[...], grad[...])).astype(BF16)
    for part in range(2):
        rows = slice(part * width // 2, (part + 1) * width // 2)
        update[rows] = dot(left[rows], out_high[...]) + dot(left[rows], out_low[...])
        copies.append(pltpu.make_async_copy(update.at[rows], result.at[rows], done.at[2 + part]))
        copies[-1].start()
    for copy in copies:
        copy.wait()


def send(parts):
    got = {0: parts[0]}
    for step in (3, 1, 2):
        got[step] = lax.ppermute(parts[step], ("near", "side"), [(i, i ^ step) for i in range(GROUP)])
    return [got[step] for step in range(GROUP)]


def exchange(value, after=(), flops=0):
    step = 1
    while step < lax.axis_size("far"):
        route = [(i, i ^ step) for i in range(lax.axis_size("far"))]
        got = lax.ppermute(value, "far", route)
        value = call(add_kernel, flops, value, [VMEM] * 2 + [ANY] * len(after))(value, got, *after)
        step *= 2
    return value


def body(acts, weights, cot_last):
    pairs = lax.axis_size("row")
    row = lax.axis_index("row")
    core = lax.axis_index("core")
    weight = weights[0]
    local = acts[0]
    micro, rows, width = local.shape
    tokens = micro * rows
    count = tokens * GROUP * lax.axis_size("far")
    odd = core == 1

    def mine_of(pair):
        return jnp.where(odd, pair[1], pair[0])

    def array(*shape, dtype=BF16):
        return jax.ShapeDtypeStruct(shape, dtype)

    def near_copy(value):
        return jnp.where(core > 1, jnp.zeros_like(value), value)

    partner = lax.ppermute(weight, "core", SWAP)
    partner_local = lax.ppermute(local, "core", SWAP)
    block = array(rows, width)
    slope = array(rows, width, dtype=F32)
    own, kept, last, slope_own, slope_partner, down = call(
        first_kernel,
        8 * rows * width**2,
        [array(width, width), array(micro, rows, width), block, slope, slope, block],
        [VMEM] * 5,
    )(near_copy(weight), near_copy(local), near_copy(cot_last), partner, partner_local)
    first = down
    for turn in range(1, pairs):
        upstream = lax.ppermute(down, "row", [(r, r - 1) for r in range(1, pairs)])
        arrived = upstream if turn == 1 else jnp.where(row == pairs - 1 - turn, upstream, arrived)
        if turn < pairs - 1:
            cot = layer(upstream, mine_of((slope_partner, slope_own)), mine_of((partner, own)))[1]
            down = layer(cot, mine_of((slope_own, slope_partner)), mine_of((own, partner)))[1]

    size = width // GROUP
    factor = 5 * size
    act_parts = call(
        act_kernel,
        2 * tokens * width**2,
        [array(size // 2, factor)] * GROUP,
        [VMEM, ANY],
        [pltpu.VMEM((tokens, width), BF16), pltpu.VMEM((GROUP, size // 2, factor), BF16)],
    )(kept, first)
    act_pieces = send(act_parts)

    own_dh, give_dh, own_cot, give_cot = call(
        layers_kernel, 64 * rows * width**2, [block] * 4, [VMEM] * 6
    )(own, partner, slope_own, slope_partner, arrived, last)
    act_sum = call(sum_kernel, 24 * width**3, array(size // 2, factor), [VMEM] * GROUP + [ANY])(
        *(act_pieces[step] for step in (0, 3, 1, 2)), own_dh
    )
    got_dh = lax.ppermute(give_dh, "core", SWAP)

    parts = call(
        grad_kernel,
        4 * tokens * width**2,
        [array(size // 2, factor)] * GROUP + [array(size // 2, 2 * width)] * GROUP,
        [VMEM] * 3 + [ANY],
        [pltpu.VMEM((tokens, width), BF16)] * 2
        + [pltpu.VMEM((GROUP, size // 2, factor), BF16), pltpu.VMEM((GROUP, size // 2, 2 * width), BF16)],
    )(kept, own_dh, got_dh, act_sum)

    pieces = send(parts[:GROUP])
    factors, act_part = call(
        pass_kernel, 0, [array(size // 2, factor)] * 2, [VMEM] * (GROUP + 1)
    )(*(pieces[step] for step in (0, 3, 1, 2)), exchange(act_sum, flops=16 * width**3))
    out = send([exchange(factors)] * GROUP)
    pieces = send(parts[GROUP:])
    total, act_part = call(
        pass_kernel, 0, [array(size // 2, 2 * width), array(size // 2, factor)], [VMEM] * (GROUP + 1)
    )(*(pieces[step] for step in (0, 3, 1, 2)), act_part)
    act = send([act_part] * GROUP)

    def inverse(pieces, through, after):
        return call(
            functools.partial(inverse_kernel, count),
            20 * width**3,
            [array(width, width)] * 2 + [array(*through.shape)],
            [VMEM, ANY] + [VMEM] * GROUP,
            [pltpu.VMEM((GROUP, size // 2, factor), BF16), pltpu.VMEM((width, width), BF16)],
        )(through, after, *pieces)

    total = exchange(total, (*out, act[1]))
    grad = send([total] * GROUP)
    *out_inv, give_cot = inverse(out, give_cot, total)
    *act_inv, _ = inverse(act, act_part, total)
    other_cot = lax.ppermute(give_cot, "core", SWAP)
    update, cot = call(
        update_kernel,
        10 * width**3,
        [array(width, width, dtype=F32), array(micro, rows, width)],
        [VMEM] * (6 + GROUP),
        [
            pltpu.VMEM((width, width), BF16),
            pltpu.VMEM((width, width), F32),
            pltpu.SemaphoreType.DMA((4,)),
        ],
        HBM,
    )(*act_inv, *out_inv, own_cot, other_cot, *grad)
    return (cot[None], update[None])


def solution(mesh):
    sections, shards = mesh.devices.shape
    finer = Mesh(
        np.reshape(mesh.devices, (sections // 2, 2, shards // GROUP, 2, 2)),
        ("row", "core", "far", "near", "side"),
    )
    section, dp = ("row", "core"), ("far", "near", "side")
    placed = (P(section, None, dp, None), P(section, None, None), P(None, dp, None))
    return jax.shard_map(
        body,
        mesh=finer,
        in_specs=placed,
        out_specs=(P(section, None, dp, None), P(section, None, None)),
        check_vma=False,
    )
```

```python
import functools

import jax
import jax.numpy as jnp
import numpy as np
from jax import lax
from jax.experimental import pallas as pl
from jax.experimental.pallas import tpu as pltpu
from jax.sharding import Mesh, PartitionSpec as P

BF16 = jnp.bfloat16
F32 = jnp.float32
SWAP = [(0, 1), (1, 0)]
VMEM = pl.BlockSpec(memory_space=pltpu.VMEM)
ANY = pl.BlockSpec(memory_space=pl.ANY)
HBM = pl.BlockSpec(memory_space=pltpu.HBM)
GROUP = 4


def silu_slope(pre):
    sig = jax.nn.sigmoid(pre)
    return sig * (1.0 + pre * (1.0 - sig))


def slope_of(inputs, matrix):
    return silu_slope(jnp.dot(inputs, matrix, preferred_element_type=F32))


def layer(upstream, slope, matrix):
    dh = (upstream.astype(F32) * slope).astype(BF16)
    back = lax.dot_general(dh, matrix, (((1,), (1,)), ((), ())), preferred_element_type=F32)
    return dh, (upstream.astype(F32) + back).astype(BF16)


def by_core(core, run, own, partner):
    @pl.when(core == 1)
    def _():
        run(own, partner)

    @pl.when(core == 0)
    def _():
        run(partner, own)


def moment(left, right):
    return lax.dot_general(left, right, (((0,), (0,)), ((), ())), preferred_element_type=F32)


def group_place():
    return 2 * lax.axis_index("near") + lax.axis_index("side")


def split(value):
    high = value.astype(BF16)
    return high, (value - high.astype(F32)).astype(BF16)


def dot(left, right):
    return jnp.dot(left.astype(BF16), right.astype(BF16), preferred_element_type=F32)


def call(kernel, flops, out_shape, in_specs, scratch=(), out_spec=VMEM):
    return pl.pallas_call(
        kernel,
        out_shape=jax.tree.map(lambda v: jax.ShapeDtypeStruct(v.shape, v.dtype), out_shape),
        in_specs=in_specs,
        out_specs=jax.tree.map(lambda _: out_spec, out_shape),
        scratch_shapes=list(scratch),
        cost_estimate=pl.CostEstimate(flops=flops, bytes_accessed=1 << 20, transcendentals=0),
        compiler_params=pltpu.CompilerParams(vmem_limit_bytes=32 << 20),
    )


def first_kernel(
    weight, local, cot_last, partner, partner_local,
    own, kept, last, slope_own, slope_partner, down,
):
    core = lax.axis_index("core")
    last[...] = cot_last[core]
    slope_own[...] = slope_of(local[core], weight[...])
    slope_partner[...] = slope_of(partner_local[core], partner[...])

    def run(odd, even):
        cot = layer(last[...], odd[1][...], odd[0][...])[1]
        down[...] = layer(cot, even[1][...], even[0][...])[1]

    by_core(core, run, (weight, slope_own), (partner, slope_partner))
    own[...] = weight[...]
    kept[...] = local[...]


def sum_kernel(*refs):
    result = refs[-1]
    result[...] = sum(piece[...].astype(F32) for piece in refs[:GROUP]).astype(BF16)


def pass_kernel(*refs):
    refs[-2][...] = sum(piece[...].astype(F32) for piece in refs[:GROUP]).astype(BF16)
    refs[-1][...] = refs[GROUP][...]


def layers_kernel(
    own, partner, slope_own, slope_partner, arrived, last, own_dh, give_dh, own_cot, give_cot
):
    upstream = jnp.where(lax.axis_index("row") == lax.axis_size("row") - 1, last[...], arrived[...])

    def run(odd, even):
        dh, cot = layer(upstream, odd[1][...], odd[0][...])
        odd[2][...], odd[3][...] = dh, cot
        even[2][...], even[3][...] = layer(cot, even[1][...], even[0][...])

    by_core(
        lax.axis_index("core"), run, (own, slope_own, own_dh, own_cot), (partner, slope_partner, give_dh, give_cot)
    )


def put_factor(tokens, whole):
    width = tokens.shape[1]
    size = width // GROUP
    half = size // 2
    columns = [tokens[:, u * size:(u + 1) * size] for u in range(GROUP)]
    for u in range(GROUP):
        pair = jnp.concatenate([columns[u], columns[(u + 1) % GROUP]], axis=1)
        main = moment(columns[u], pair).astype(BF16)
        whole[u, :, :2 * size] = main[:half]
        whole[u, :, 2 * size:4 * size] = main[half:]
    for u in range(2):
        corner = moment(columns[u], columns[u + 2]).astype(BF16)
        whole[u, :, 4 * size:5 * size] = corner[:half]
        whole[u + 2, :, 4 * size:5 * size] = corner[half:]


def act_kernel(local, after, *refs):
    parts, (tokens, whole) = refs[:GROUP], refs[GROUP:]
    micro, rows = local.shape[:2]
    for m in range(micro):
        tokens[m * rows:(m + 1) * rows] = local[m]
    put_factor(tokens, whole)
    for step, part in enumerate(parts):
        part[...] = whole[group_place() ^ step]


def add_kernel(left, right, *refs):
    refs[-1][...] = (left[...].astype(F32) + right[...].astype(F32)).astype(BF16)


def grad_kernel(local, dh_own, dh_got, after, *refs):
    factors, grads, (inputs, tokens, whole, rest) = refs[:GROUP], refs[GROUP:2 * GROUP], refs[2 * GROUP:]
    rows, width = local.shape[1:]
    inputs[:rows] = local[lax.axis_index("core")]
    inputs[rows:] = local[1 - lax.axis_index("core")]
    tokens[:rows] = dh_own[...]
    tokens[rows:] = dh_got[...]
    put_factor(tokens, whole)
    size = width // GROUP
    half = size // 2
    for u in range(GROUP):
        grad = moment(inputs[:, u * size:(u + 1) * size], tokens[...]).astype(BF16)
        rest[u, :, :width] = grad[:half]
        rest[u, :, width:] = grad[half:]
    for step in range(GROUP):
        factors[step][...] = whole[group_place() ^ step]
        grads[step][...] = rest[group_place() ^ step]


def invert(total, count):
    row = lax.broadcasted_iota(jnp.int32, total.shape, 0)
    column = lax.broadcasted_iota(jnp.int32, total.shape, 1)
    eye = (row == column).astype(F32)
    ridge = 0.01
    mean = total[...].astype(F32) * (1.0 / count)
    full = mean + ridge * eye
    scale = lax.rsqrt(jnp.sum(full * full, keepdims=True))
    squared = dot(total[...], total[...]) * (1.0 / count) ** 2 + ridge * (mean + full)
    second = (2.0 * scale) * full - squared * (scale * scale)
    last = 2.0 * (eye - second) + dot(second, second)
    tail = 2.0 * last - dot(second, last)
    inner = dot(total[...], tail) * (scale * (1.0 / count))
    return split(((2.0 - ridge * scale) * tail - inner) * scale)


def through_kernel(count, through, after, *refs):
    through_copy = refs[GROUP + 2]
    through_copy[...] = through[...]
    inverse_kernel(count, after, *refs[:GROUP + 2], *refs[GROUP + 3:])


def inverse_kernel(count, after, *refs):
    pieces, (high, low, blocks, total) = refs[:GROUP], refs[GROUP:]
    for step, piece in enumerate(pieces):
        blocks[group_place() ^ step] = piece[...]
    size = total.shape[0] // GROUP

    def both(row, column, value):
        total[row * size:(row + 1) * size, column * size:(column + 1) * size] = value
        if row != column:
            turned = value.astype(F32).T.astype(BF16)
            total[column * size:(column + 1) * size, row * size:(row + 1) * size] = turned

    for u in range(GROUP):
        main = jnp.concatenate([blocks[u, :, :2 * size], blocks[u, :, 2 * size:4 * size]])
        both(u, u, main[:, :size])
        both(u, (u + 1) % GROUP, main[:, size:])
    for u in range(2):
        both(u, u + 2, jnp.concatenate([blocks[u, :, 4 * size:], blocks[u + 2, :, 4 * size:]]))
    for result, term in zip((high, low), invert(total, count)):
        result[...] = term


def update_kernel(act_high, act_low, out_high, out_low, own_cot, other_cot, *refs):
    pieces, (result, cot, grad, update, done) = refs[:GROUP], refs[GROUP:]
    copies = [
        pltpu.make_async_copy(own_cot, cot.at[lax.axis_index("core")], done.at[0]),
        pltpu.make_async_copy(other_cot, cot.at[1 - lax.axis_index("core")], done.at[1]),
    ]
    for copy in copies:
        copy.start()
    half, twice = pieces[0].shape
    width = twice // 2
    for step, piece in enumerate(pieces):
        start = pl.multiple_of((group_place() ^ step) * 2 * half, 2 * half)
        grad[pl.ds(start, half)] = piece[:, :width]
        grad[pl.ds(start + half, half)] = piece[:, width:]
    left = (dot(act_high[...], grad[...]) + dot(act_low[...], grad[...])).astype(BF16)
    for part in range(2):
        rows = slice(part * width // 2, (part + 1) * width // 2)
        update[rows] = dot(left[rows], out_high[...]) + dot(left[rows], out_low[...])
        copies.append(pltpu.make_async_copy(update.at[rows], result.at[rows], done.at[2 + part]))
        copies[-1].start()
    for copy in copies:
        copy.wait()


def send(parts):
    got = {0: parts[0]}
    for step in (3, 1, 2):
        got[step] = lax.ppermute(parts[step], ("near", "side"), [(i, i ^ step) for i in range(GROUP)])
    return [got[step] for step in range(GROUP)]


def exchange(value, after=(), flops=0):
    step = 1
    while step < lax.axis_size("far"):
        route = [(i, i ^ step) for i in range(lax.axis_size("far"))]
        got = lax.ppermute(value, "far", route)
        value = call(add_kernel, flops, value, [VMEM] * 2 + [ANY] * len(after))(value, got, *after)
        step *= 2
    return value


def body(acts, weights, cot_last):
    pairs = lax.axis_size("row")
    row = lax.axis_index("row")
    core = lax.axis_index("core")
    weight = weights[0]
    local = acts[0]
    micro, rows, width = local.shape
    tokens = micro * rows
    count = tokens * GROUP * lax.axis_size("far")
    odd = core == 1

    def mine_of(pair):
        return jnp.where(odd, pair[1], pair[0])

    def array(*shape, dtype=BF16):
        return jax.ShapeDtypeStruct(shape, dtype)

    def near_copy(value):
        return jnp.where(core > 1, jnp.zeros_like(value), value)

    partner = lax.ppermute(weight, "core", SWAP)
    partner_local = lax.ppermute(local, "core", SWAP)
    block = array(rows, width)
    slope = array(rows, width, dtype=F32)
    own, kept, last, slope_own, slope_partner, down = call(
        first_kernel,
        8 * rows * width**2,
        [array(width, width), array(micro, rows, width), block, slope, slope, block],
        [VMEM] * 5,
    )(near_copy(weight), near_copy(local), near_copy(cot_last), partner, partner_local)
    first = down
    for turn in range(1, pairs):
        upstream = lax.ppermute(down, "row", [(r, r - 1) for r in range(1, pairs)])
        arrived = upstream if turn == 1 else jnp.where(row == pairs - 1 - turn, upstream, arrived)
        if turn < pairs - 1:
            cot = layer(upstream, mine_of((slope_partner, slope_own)), mine_of((partner, own)))[1]
            down = layer(cot, mine_of((slope_own, slope_partner)), mine_of((own, partner)))[1]

    size = width // GROUP
    factor = 5 * size
    act_parts = call(
        act_kernel,
        2 * tokens * width**2,
        [array(size // 2, factor)] * GROUP,
        [VMEM, ANY],
        [pltpu.VMEM((tokens, width), BF16), pltpu.VMEM((GROUP, size // 2, factor), BF16)],
    )(kept, first)
    act_pieces = send(act_parts)

    own_dh, give_dh, own_cot, give_cot = call(
        layers_kernel, 64 * rows * width**2, [block] * 4, [VMEM] * 6
    )(own, partner, slope_own, slope_partner, arrived, last)
    act_sum = call(sum_kernel, 24 * width**3, array(size // 2, factor), [VMEM] * GROUP + [ANY])(
        *(act_pieces[step] for step in (0, 3, 1, 2)), own_dh
    )
    got_dh = lax.ppermute(give_dh, "core", SWAP)

    parts = call(
        grad_kernel,
        4 * tokens * width**2,
        [array(size // 2, factor)] * GROUP + [array(size // 2, 2 * width)] * GROUP,
        [VMEM] * 3 + [ANY],
        [pltpu.VMEM((tokens, width), BF16)] * 2
        + [pltpu.VMEM((GROUP, size // 2, factor), BF16), pltpu.VMEM((GROUP, size // 2, 2 * width), BF16)],
    )(kept, own_dh, got_dh, act_sum)

    pieces = send(parts[:GROUP])
    factors, act_part = call(
        pass_kernel, 0, [array(size // 2, factor)] * 2, [VMEM] * (GROUP + 1)
    )(*(pieces[step] for step in (0, 3, 1, 2)), exchange(act_sum, flops=16 * width**3))
    out = send([exchange(factors)] * GROUP)
    pieces = send(parts[GROUP:])
    total, act_part = call(
        pass_kernel, 0, [array(size // 2, 2 * width), array(size // 2, factor)], [VMEM] * (GROUP + 1)
    )(*(pieces[step] for step in (0, 3, 1, 2)), act_part)
    act = send([act_part] * GROUP)

    def inverse(pieces, after, *through):
        return call(
            functools.partial(through_kernel if through else inverse_kernel, count),
            20 * width**3,
            [array(width, width)] * 2 + [array(*value.shape) for value in through],
            [VMEM] * len(through) + [ANY] + [VMEM] * GROUP,
            [pltpu.VMEM((GROUP, size // 2, factor), BF16), pltpu.VMEM((width, width), BF16)],
        )(*through, after, *pieces)

    total = exchange(total, (*out, act[1]))
    grad = send([total] * GROUP)
    *out_inv, give_cot = inverse(out, total, give_cot)
    act_inv = inverse(act, total)
    other_cot = lax.ppermute(give_cot, "core", SWAP)
    update, cot = call(
        update_kernel,
        10 * width**3,
        [array(width, width, dtype=F32), array(micro, rows, width)],
        [VMEM] * (6 + GROUP),
        [
            pltpu.VMEM((width, width), BF16),
            pltpu.VMEM((width, width), F32),
            pltpu.SemaphoreType.DMA((4,)),
        ],
        HBM,
    )(*act_inv, *out_inv, own_cot, other_cot, *grad)
    return (cot[None], update[None])


def solution(mesh):
    sections, shards = mesh.devices.shape
    finer = Mesh(
        np.reshape(mesh.devices, (sections // 2, 2, shards // GROUP, 2, 2)),
        ("row", "core", "far", "near", "side"),
    )
    section, dp = ("row", "core"), ("far", "near", "side")
    placed = (P(section, None, dp, None), P(section, None, None), P(None, dp, None))
    return jax.shard_map(
        body,
        mesh=finer,
        in_specs=placed,
        out_specs=(P(section, None, dp, None), P(section, None, None)),
        check_vma=False,
    )
```

```python
import functools

import jax
import jax.numpy as jnp
import numpy as np
from jax import lax
from jax.experimental import pallas as pl
from jax.experimental.pallas import tpu as pltpu
from jax.sharding import Mesh, PartitionSpec as P

BF16 = jnp.bfloat16
F32 = jnp.float32
SWAP = [(0, 1), (1, 0)]
VMEM = pl.BlockSpec(memory_space=pltpu.VMEM)
ANY = pl.BlockSpec(memory_space=pl.ANY)
HBM = pl.BlockSpec(memory_space=pltpu.HBM)
GROUP = 4


def silu_slope(pre):
    sig = jax.nn.sigmoid(pre)
    return sig * (1.0 + pre * (1.0 - sig))


def slope_of(inputs, matrix):
    return silu_slope(jnp.dot(inputs, matrix, preferred_element_type=F32))


def layer(upstream, slope, matrix):
    dh = (upstream.astype(F32) * slope).astype(BF16)
    back = lax.dot_general(dh, matrix, (((1,), (1,)), ((), ())), preferred_element_type=F32)
    return dh, (upstream.astype(F32) + back).astype(BF16)


def by_core(core, run, own, partner):
    @pl.when(core == 1)
    def _():
        run(own, partner)

    @pl.when(core == 0)
    def _():
        run(partner, own)


def moment(left, right):
    return lax.dot_general(left, right, (((0,), (0,)), ((), ())), preferred_element_type=F32)


def group_place():
    return 2 * lax.axis_index("near") + lax.axis_index("side")


def dot(left, right):
    return jnp.dot(left.astype(BF16), right.astype(BF16), preferred_element_type=F32)


def call(kernel, flops, out_shape, in_specs, scratch=(), out_spec=VMEM):
    return pl.pallas_call(
        kernel,
        out_shape=jax.tree.map(lambda v: jax.ShapeDtypeStruct(v.shape, v.dtype), out_shape),
        in_specs=in_specs,
        out_specs=jax.tree.map(lambda _: out_spec, out_shape),
        scratch_shapes=list(scratch),
        cost_estimate=pl.CostEstimate(flops=flops, bytes_accessed=1 << 20, transcendentals=0),
        compiler_params=pltpu.CompilerParams(vmem_limit_bytes=32 << 20),
    )


def first_kernel(
    weight, local, cot_last, partner, partner_local,
    own, kept, last, slope_own, slope_partner, down,
):
    core = lax.axis_index("core")
    last[...] = cot_last[core]
    slope_own[...] = slope_of(local[core], weight[...])
    slope_partner[...] = slope_of(partner_local[core], partner[...])

    def run(odd, even):
        cot = layer(last[...], odd[1][...], odd[0][...])[1]
        down[...] = layer(cot, even[1][...], even[0][...])[1]

    by_core(core, run, (weight, slope_own), (partner, slope_partner))
    own[...] = weight[...]
    kept[...] = local[...]


def sum_kernel(*refs):
    result = refs[-1]
    result[...] = sum(piece[...].astype(F32) for piece in refs[:GROUP]).astype(BF16)


def pass_kernel(*refs):
    refs[-2][...] = sum(piece[...].astype(F32) for piece in refs[:GROUP]).astype(BF16)
    refs[-1][...] = refs[GROUP][...]


def layers_kernel(
    own, partner, slope_own, slope_partner, arrived, last, own_dh, give_dh, own_cot, give_cot
):
    upstream = jnp.where(lax.axis_index("row") == lax.axis_size("row") - 1, last[...], arrived[...])

    def run(odd, even):
        dh, cot = layer(upstream, odd[1][...], odd[0][...])
        odd[2][...], odd[3][...] = dh, cot
        even[2][...], even[3][...] = layer(cot, even[1][...], even[0][...])

    by_core(
        lax.axis_index("core"), run, (own, slope_own, own_dh, own_cot), (partner, slope_partner, give_dh, give_cot)
    )


def put_factor(tokens, whole):
    width = tokens.shape[1]
    size = width // GROUP
    half = size // 2
    columns = [tokens[:, u * size:(u + 1) * size] for u in range(GROUP)]
    for u in range(GROUP):
        pair = jnp.concatenate([columns[u], columns[(u + 1) % GROUP]], axis=1)
        main = moment(columns[u], pair).astype(BF16)
        whole[u, :, :2 * size] = main[:half]
        whole[u, :, 2 * size:4 * size] = main[half:]
    for u in range(2):
        corner = moment(columns[u], columns[u + 2]).astype(BF16)
        whole[u, :, 4 * size:5 * size] = corner[:half]
        whole[u + 2, :, 4 * size:5 * size] = corner[half:]


def act_kernel(local, after, *refs):
    parts, (tokens, whole) = refs[:GROUP], refs[GROUP:]
    micro, rows = local.shape[:2]
    for m in range(micro):
        tokens[m * rows:(m + 1) * rows] = local[m]
    put_factor(tokens, whole)
    for step, part in enumerate(parts):
        part[...] = whole[group_place() ^ step]


def add_kernel(left, right, *refs):
    refs[-1][...] = (left[...].astype(F32) + right[...].astype(F32)).astype(BF16)


def grad_kernel(local, dh_own, dh_got, after, *refs):
    factors, grads, (inputs, tokens, whole, rest) = refs[:GROUP], refs[GROUP:2 * GROUP], refs[2 * GROUP:]
    rows, width = local.shape[1:]
    inputs[:rows] = local[lax.axis_index("core")]
    inputs[rows:] = local[1 - lax.axis_index("core")]
    tokens[:rows] = dh_own[...]
    tokens[rows:] = dh_got[...]
    put_factor(tokens, whole)
    size = width // GROUP
    half = size // 2
    for u in range(GROUP):
        grad = moment(inputs[:, u * size:(u + 1) * size], tokens[...]).astype(BF16)
        rest[u, :, :width] = grad[:half]
        rest[u, :, width:] = grad[half:]
    for step in range(GROUP):
        factors[step][...] = whole[group_place() ^ step]
        grads[step][...] = rest[group_place() ^ step]


def invert(total, count):
    row = lax.broadcasted_iota(jnp.int32, total.shape, 0)
    column = lax.broadcasted_iota(jnp.int32, total.shape, 1)
    eye = (row == column).astype(F32)
    ridge = 0.01
    mean = total[...].astype(F32) * (1.0 / count)
    full = mean + ridge * eye
    scale = lax.rsqrt(jnp.sum(full * full, keepdims=True))
    squared = dot(total[...], total[...]) * (1.0 / count) ** 2 + ridge * (mean + full)
    second = (2.0 * scale) * full - squared * (scale * scale)
    last = 2.0 * (eye - second) + dot(second, second)
    tail = 2.0 * last - dot(second, last)
    inner = dot(total[...], tail) * (scale * (1.0 / count))
    return (((2.0 - ridge * scale) * tail - inner) * scale).astype(BF16)


def through_kernel(count, through, after, *refs):
    through_copy = refs[GROUP + 1]
    through_copy[...] = through[...]
    inverse_kernel(count, after, *refs[:GROUP + 1], *refs[GROUP + 2:])


def inverse_kernel(count, after, *refs):
    pieces, (result, blocks, total) = refs[:GROUP], refs[GROUP:]
    for step, piece in enumerate(pieces):
        blocks[group_place() ^ step] = piece[...]
    size = total.shape[0] // GROUP

    def both(row, column, value):
        total[row * size:(row + 1) * size, column * size:(column + 1) * size] = value
        if row != column:
            turned = value.astype(F32).T.astype(BF16)
            total[column * size:(column + 1) * size, row * size:(row + 1) * size] = turned

    for u in range(GROUP):
        main = jnp.concatenate([blocks[u, :, :2 * size], blocks[u, :, 2 * size:4 * size]])
        both(u, u, main[:, :size])
        both(u, (u + 1) % GROUP, main[:, size:])
    for u in range(2):
        both(u, u + 2, jnp.concatenate([blocks[u, :, 4 * size:], blocks[u + 2, :, 4 * size:]]))
    result[...] = invert(total, count)


def update_kernel(act_inv, out_inv, own_cot, other_cot, *refs):
    pieces, (result, cot, grad, update, done) = refs[:GROUP], refs[GROUP:]
    copies = [
        pltpu.make_async_copy(own_cot, cot.at[lax.axis_index("core")], done.at[0]),
        pltpu.make_async_copy(other_cot, cot.at[1 - lax.axis_index("core")], done.at[1]),
    ]
    for copy in copies:
        copy.start()
    half, twice = pieces[0].shape
    width = twice // 2
    for step, piece in enumerate(pieces):
        start = pl.multiple_of((group_place() ^ step) * 2 * half, 2 * half)
        grad[pl.ds(start, half)] = piece[:, :width]
        grad[pl.ds(start + half, half)] = piece[:, width:]
    left = dot(act_inv[...], grad[...]).astype(BF16)
    for part in range(2):
        rows = slice(part * width // 2, (part + 1) * width // 2)
        update[rows] = dot(left[rows], out_inv[...])
        copies.append(pltpu.make_async_copy(update.at[rows], result.at[rows], done.at[2 + part]))
        copies[-1].start()
    for copy in copies:
        copy.wait()


def send(parts):
    got = {0: parts[0]}
    for step in (3, 1, 2):
        got[step] = lax.ppermute(parts[step], ("near", "side"), [(i, i ^ step) for i in range(GROUP)])
    return [got[step] for step in range(GROUP)]


def exchange(value, after=(), flops=0):
    step = 1
    while step < lax.axis_size("far"):
        route = [(i, i ^ step) for i in range(lax.axis_size("far"))]
        got = lax.ppermute(value, "far", route)
        value = call(add_kernel, flops, value, [VMEM] * 2 + [ANY] * len(after))(value, got, *after)
        step *= 2
    return value


def body(acts, weights, cot_last):
    pairs = lax.axis_size("row")
    row = lax.axis_index("row")
    core = lax.axis_index("core")
    weight = weights[0]
    local = acts[0]
    micro, rows, width = local.shape
    tokens = micro * rows
    count = tokens * GROUP * lax.axis_size("far")
    odd = core == 1

    def mine_of(pair):
        return jnp.where(odd, pair[1], pair[0])

    def array(*shape, dtype=BF16):
        return jax.ShapeDtypeStruct(shape, dtype)

    def near_copy(value):
        return jnp.where(core > 1, jnp.zeros_like(value), value)

    partner = lax.ppermute(weight, "core", SWAP)
    partner_local = lax.ppermute(local, "core", SWAP)
    block = array(rows, width)
    slope = array(rows, width, dtype=F32)
    own, kept, last, slope_own, slope_partner, down = call(
        first_kernel,
        8 * rows * width**2,
        [array(width, width), array(micro, rows, width), block, slope, slope, block],
        [VMEM] * 5,
    )(near_copy(weight), near_copy(local), near_copy(cot_last), partner, partner_local)
    first = down
    for turn in range(1, pairs):
        upstream = lax.ppermute(down, "row", [(r, r - 1) for r in range(1, pairs)])
        arrived = upstream if turn == 1 else jnp.where(row == pairs - 1 - turn, upstream, arrived)
        if turn < pairs - 1:
            cot = layer(upstream, mine_of((slope_partner, slope_own)), mine_of((partner, own)))[1]
            down = layer(cot, mine_of((slope_own, slope_partner)), mine_of((own, partner)))[1]

    size = width // GROUP
    factor = 5 * size
    act_parts = call(
        act_kernel,
        2 * tokens * width**2,
        [array(size // 2, factor)] * GROUP,
        [VMEM, ANY],
        [pltpu.VMEM((tokens, width), BF16), pltpu.VMEM((GROUP, size // 2, factor), BF16)],
    )(kept, first)
    act_pieces = send(act_parts)

    own_dh, give_dh, own_cot, give_cot = call(
        layers_kernel, 64 * rows * width**2, [block] * 4, [VMEM] * 6
    )(own, partner, slope_own, slope_partner, arrived, last)
    act_sum = call(sum_kernel, 24 * width**3, array(size // 2, factor), [VMEM] * GROUP + [ANY])(
        *(act_pieces[step] for step in (0, 3, 1, 2)), own_dh
    )
    got_dh = lax.ppermute(give_dh, "core", SWAP)

    parts = call(
        grad_kernel,
        4 * tokens * width**2,
        [array(size // 2, factor)] * GROUP + [array(size // 2, 2 * width)] * GROUP,
        [VMEM] * 3 + [ANY],
        [pltpu.VMEM((tokens, width), BF16)] * 2
        + [pltpu.VMEM((GROUP, size // 2, factor), BF16), pltpu.VMEM((GROUP, size // 2, 2 * width), BF16)],
    )(kept, own_dh, got_dh, act_sum)

    pieces = send(parts[:GROUP])
    factors, act_part = call(
        pass_kernel, 0, [array(size // 2, factor)] * 2, [VMEM] * (GROUP + 1)
    )(*(pieces[step] for step in (0, 3, 1, 2)), exchange(act_sum, flops=16 * width**3))
    out = send([exchange(factors)] * GROUP)
    pieces = send(parts[GROUP:])
    total, act_part = call(
        pass_kernel, 0, [array(size // 2, 2 * width), array(size // 2, factor)], [VMEM] * (GROUP + 1)
    )(*(pieces[step] for step in (0, 3, 1, 2)), act_part)
    act = send([act_part] * GROUP)

    def inverse(pieces, after, *through):
        return call(
            functools.partial(through_kernel if through else inverse_kernel, count),
            20 * width**3,
            [array(width, width)] + [array(*value.shape) for value in through],
            [VMEM] * len(through) + [ANY] + [VMEM] * GROUP,
            [pltpu.VMEM((GROUP, size // 2, factor), BF16), pltpu.VMEM((width, width), BF16)],
        )(*through, after, *pieces)

    total = exchange(total, (*out, act[1]))
    grad = send([total] * GROUP)
    out_inv, give_cot = inverse(out, total, give_cot)
    (act_inv,) = inverse(act, total)
    other_cot = lax.ppermute(give_cot, "core", SWAP)
    update, cot = call(
        update_kernel,
        10 * width**3,
        [array(width, width, dtype=F32), array(micro, rows, width)],
        [VMEM] * (4 + GROUP),
        [
            pltpu.VMEM((width, width), BF16),
            pltpu.VMEM((width, width), F32),
            pltpu.SemaphoreType.DMA((4,)),
        ],
        HBM,
    )(act_inv, out_inv, own_cot, other_cot, *grad)
    return (cot[None], update[None])


def solution(mesh):
    sections, shards = mesh.devices.shape
    finer = Mesh(
        np.reshape(mesh.devices, (sections // 2, 2, shards // GROUP, 2, 2)),
        ("row", "core", "far", "near", "side"),
    )
    section, dp = ("row", "core"), ("far", "near", "side")
    placed = (P(section, None, dp, None), P(section, None, None), P(None, dp, None))
    return jax.shard_map(
        body,
        mesh=finer,
        in_specs=placed,
        out_specs=(P(section, None, dp, None), P(section, None, None)),
        check_vma=False,
    )
```

```python
import functools

import jax
import jax.numpy as jnp
import numpy as np
from jax import lax
from jax.experimental import pallas as pl
from jax.experimental.pallas import tpu as pltpu
from jax.sharding import Mesh, PartitionSpec as P

BF16 = jnp.bfloat16
F32 = jnp.float32
SWAP = [(0, 1), (1, 0)]
VMEM = pl.BlockSpec(memory_space=pltpu.VMEM)
ANY = pl.BlockSpec(memory_space=pl.ANY)
HBM = pl.BlockSpec(memory_space=pltpu.HBM)
GROUP = 4


def silu_slope(pre):
    sig = jax.nn.sigmoid(pre)
    return sig * (1.0 + pre * (1.0 - sig))


def slope_of(inputs, matrix):
    return silu_slope(jnp.dot(inputs, matrix, preferred_element_type=F32))


def layer(upstream, slope, matrix):
    dh = (upstream.astype(F32) * slope).astype(BF16)
    back = lax.dot_general(dh, matrix, (((1,), (1,)), ((), ())), preferred_element_type=F32)
    return dh, (upstream.astype(F32) + back).astype(BF16)


def by_core(core, run, own, partner):
    @pl.when(core == 1)
    def _():
        run(own, partner)

    @pl.when(core == 0)
    def _():
        run(partner, own)


def moment(left, right):
    return lax.dot_general(left, right, (((0,), (0,)), ((), ())), preferred_element_type=F32)


def group_place():
    return 2 * lax.axis_index("near") + lax.axis_index("side")


def dot(left, right):
    return jnp.dot(left.astype(BF16), right.astype(BF16), preferred_element_type=F32)


def call(kernel, flops, out_shape, in_specs, scratch=(), out_spec=VMEM):
    return pl.pallas_call(
        kernel,
        out_shape=jax.tree.map(lambda v: jax.ShapeDtypeStruct(v.shape, v.dtype), out_shape),
        in_specs=in_specs,
        out_specs=jax.tree.map(lambda _: out_spec, out_shape),
        scratch_shapes=list(scratch),
        cost_estimate=pl.CostEstimate(flops=flops, bytes_accessed=1 << 20, transcendentals=0),
        compiler_params=pltpu.CompilerParams(vmem_limit_bytes=32 << 20),
    )


def first_kernel(
    weight, local, cot_last, partner, partner_local,
    own, kept, last, slope_own, slope_partner, down,
):
    core = lax.axis_index("core")
    last[...] = cot_last[core]
    slope_own[...] = slope_of(local[core], weight[...])
    slope_partner[...] = slope_of(partner_local[core], partner[...])

    def run(odd, even):
        cot = layer(last[...], odd[1][...], odd[0][...])[1]
        down[...] = layer(cot, even[1][...], even[0][...])[1]

    by_core(core, run, (weight, slope_own), (partner, slope_partner))
    own[...] = weight[...]
    kept[...] = local[...]


def sum_kernel(*refs):
    result = refs[-1]
    result[...] = sum(piece[...].astype(F32) for piece in refs[:GROUP]).astype(BF16)


def pass_kernel(*refs):
    refs[-2][...] = sum(piece[...].astype(F32) for piece in refs[:GROUP]).astype(BF16)
    refs[-1][...] = refs[GROUP][...]


def layers_kernel(
    own, partner, slope_own, slope_partner, arrived, last, own_dh, give_dh, own_cot, give_cot
):
    upstream = jnp.where(lax.axis_index("row") == lax.axis_size("row") - 1, last[...], arrived[...])

    def run(odd, even):
        dh, cot = layer(upstream, odd[1][...], odd[0][...])
        odd[2][...], odd[3][...] = dh, cot
        even[2][...], even[3][...] = layer(cot, even[1][...], even[0][...])

    by_core(
        lax.axis_index("core"), run, (own, slope_own, own_dh, own_cot), (partner, slope_partner, give_dh, give_cot)
    )


def put_factor(tokens, whole):
    width = tokens.shape[1]
    size = width // GROUP
    half = size // 2
    columns = [tokens[:, u * size:(u + 1) * size] for u in range(GROUP)]
    for u in range(GROUP):
        pair = jnp.concatenate([columns[u], columns[(u + 1) % GROUP]], axis=1)
        main = moment(columns[u], pair).astype(BF16)
        whole[u, :, :2 * size] = main[:half]
        whole[u, :, 2 * size:4 * size] = main[half:]
    for u in range(2):
        corner = moment(columns[u], columns[u + 2]).astype(BF16)
        whole[u, :, 4 * size:5 * size] = corner[:half]
        whole[u + 2, :, 4 * size:5 * size] = corner[half:]


def act_kernel(local, after, *refs):
    parts, (tokens, whole) = refs[:GROUP], refs[GROUP:]
    micro, rows = local.shape[:2]
    for m in range(micro):
        tokens[m * rows:(m + 1) * rows] = local[m]
    put_factor(tokens, whole)
    for step, part in enumerate(parts):
        part[...] = whole[group_place() ^ step]


def add_kernel(left, right, *refs):
    refs[-1][...] = (left[...].astype(F32) + right[...].astype(F32)).astype(BF16)


def grad_kernel(local, dh_own, dh_got, after, *refs):
    factors, grads, (inputs, tokens, whole, rest) = refs[:GROUP], refs[GROUP:2 * GROUP], refs[2 * GROUP:]
    rows, width = local.shape[1:]
    inputs[:rows] = local[lax.axis_index("core")]
    inputs[rows:] = local[1 - lax.axis_index("core")]
    tokens[:rows] = dh_own[...]
    tokens[rows:] = dh_got[...]
    put_factor(tokens, whole)
    size = width // GROUP
    half = size // 2
    for u in range(GROUP):
        grad = moment(inputs[:, u * size:(u + 1) * size], tokens[...]).astype(BF16)
        rest[u, :, :width] = grad[:half]
        rest[u, :, width:] = grad[half:]
    for step in range(GROUP):
        factors[step][...] = whole[group_place() ^ step]
        grads[step][...] = rest[group_place() ^ step]


def invert(total, count):
    row = lax.broadcasted_iota(jnp.int32, total.shape, 0)
    column = lax.broadcasted_iota(jnp.int32, total.shape, 1)
    eye = (row == column).astype(F32)
    ridge = 0.01
    mean = total[...].astype(F32) * (1.0 / count)
    full = mean + ridge * eye
    scale = lax.rsqrt(jnp.sum(full * full, keepdims=True))
    squared = dot(total[...], total[...]) * (1.0 / count) ** 2 + ridge * (mean + full)
    second = (2.0 * scale) * full - squared * (scale * scale)
    last = 2.0 * (eye - second) + dot(second, second)
    tail = 2.0 * last - dot(second, last)
    inner = dot(total[...], tail) * (scale * (1.0 / count))
    return (((2.0 - ridge * scale) * tail - inner) * scale).astype(BF16)


def through_kernel(count, through, after, *refs):
    through_copy = refs[GROUP + 1]
    through_copy[...] = through[...]
    inverse_kernel(count, after, *refs[:GROUP + 1], *refs[GROUP + 2:])


def inverse_kernel(count, after, *refs):
    pieces, (result, blocks, total) = refs[:GROUP], refs[GROUP:]
    for step, piece in enumerate(pieces):
        blocks[group_place() ^ step] = piece[...]
    size = total.shape[0] // GROUP

    def both(row, column, value):
        total[row * size:(row + 1) * size, column * size:(column + 1) * size] = value
        if row != column:
            turned = value.astype(F32).T.astype(BF16)
            total[column * size:(column + 1) * size, row * size:(row + 1) * size] = turned

    for u in range(GROUP):
        main = jnp.concatenate([blocks[u, :, :2 * size], blocks[u, :, 2 * size:4 * size]])
        both(u, u, main[:, :size])
        both(u, (u + 1) % GROUP, main[:, size:])
    for u in range(2):
        both(u, u + 2, jnp.concatenate([blocks[u, :, 4 * size:], blocks[u + 2, :, 4 * size:]]))
    result[...] = invert(total, count)


def update_kernel(act_inv, out_inv, own_cot, other_cot, *refs):
    pieces, (result, cot, grad, update, done) = refs[:GROUP], refs[GROUP:]
    copies = [
        pltpu.make_async_copy(own_cot, cot.at[lax.axis_index("core")], done.at[0]),
        pltpu.make_async_copy(other_cot, cot.at[1 - lax.axis_index("core")], done.at[1]),
    ]
    for copy in copies:
        copy.start()
    half, twice = pieces[0].shape
    width = twice // 2
    for step, piece in enumerate(pieces):
        start = pl.multiple_of((group_place() ^ step) * 2 * half, 2 * half)
        grad[pl.ds(start, half)] = piece[:, :width]
        grad[pl.ds(start + half, half)] = piece[:, width:]
    left = dot(act_inv[...], grad[...]).astype(BF16)
    for part in range(2):
        rows = slice(part * width // 2, (part + 1) * width // 2)
        update[rows] = dot(left[rows], out_inv[...])
        copies.append(pltpu.make_async_copy(update.at[rows], result.at[rows], done.at[2 + part]))
        copies[-1].start()
    for copy in copies:
        copy.wait()


def send(parts):
    got = {0: parts[0]}
    for step in (3, 1, 2):
        got[step] = lax.ppermute(parts[step], ("near", "side"), [(i, i ^ step) for i in range(GROUP)])
    return [got[step] for step in range(GROUP)]


def exchange(value, after=(), flops=0):
    step = 1
    while step < lax.axis_size("far"):
        route = [(i, i ^ step) for i in range(lax.axis_size("far"))]
        got = lax.ppermute(value, "far", route)
        value = call(add_kernel, flops, value, [VMEM] * 2 + [ANY] * len(after))(value, got, *after)
        step *= 2
    return value


def body(acts, weights, cot_last):
    pairs = lax.axis_size("row")
    row = lax.axis_index("row")
    core = lax.axis_index("core")
    weight = weights[0]
    local = acts[0]
    micro, rows, width = local.shape
    tokens = micro * rows
    count = tokens * GROUP * lax.axis_size("far")
    odd = core == 1

    def mine_of(pair):
        return jnp.where(odd, pair[1], pair[0])

    def array(*shape, dtype=BF16):
        return jax.ShapeDtypeStruct(shape, dtype)

    def near_copy(value):
        return jnp.where(core > 1, jnp.zeros_like(value), value)

    partner = lax.ppermute(weight, "core", SWAP)
    partner_local = lax.ppermute(local, "core", SWAP)
    block = array(rows, width)
    slope = array(rows, width, dtype=F32)
    own, kept, last, slope_own, slope_partner, down = call(
        first_kernel,
        8 * rows * width**2,
        [array(width, width), array(micro, rows, width), block, slope, slope, block],
        [VMEM] * 5,
    )(near_copy(weight), near_copy(local), near_copy(cot_last), partner, partner_local)
    first = down
    for turn in range(1, pairs):
        upstream = lax.ppermute(down, "row", [(r, r - 1) for r in range(1, pairs)])
        arrived = upstream if turn == 1 else jnp.where(row == pairs - 1 - turn, upstream, arrived)
        if turn < pairs - 1:
            cot = layer(upstream, mine_of((slope_partner, slope_own)), mine_of((partner, own)))[1]
            down = layer(cot, mine_of((slope_own, slope_partner)), mine_of((own, partner)))[1]

    size = width // GROUP
    factor = 5 * size
    act_parts = call(
        act_kernel,
        2 * tokens * width**2,
        [array(size // 2, factor)] * GROUP,
        [VMEM, ANY],
        [pltpu.VMEM((tokens, width), BF16), pltpu.VMEM((GROUP, size // 2, factor), BF16)],
    )(kept, first)
    act_pieces = send(act_parts)

    own_dh, give_dh, own_cot, give_cot = call(
        layers_kernel, 64 * rows * width**2, [block] * 4, [VMEM] * 6
    )(own, partner, slope_own, slope_partner, arrived, last)
    act_sum = call(sum_kernel, 24 * width**3, array(size // 2, factor), [VMEM] * GROUP + [ANY])(
        *(act_pieces[step] for step in (0, 3, 1, 2)), own_dh
    )
    got_dh = lax.ppermute(give_dh, "core", SWAP)

    parts = call(
        grad_kernel,
        4 * tokens * width**2,
        [array(size // 2, factor)] * GROUP + [array(size // 2, 2 * width)] * GROUP,
        [VMEM] * 3 + [ANY],
        [pltpu.VMEM((tokens, width), BF16)] * 2
        + [pltpu.VMEM((GROUP, size // 2, factor), BF16), pltpu.VMEM((GROUP, size // 2, 2 * width), BF16)],
    )(kept, own_dh, got_dh, act_sum)

    pieces = send(parts[:GROUP])
    factors, act_part = call(
        pass_kernel, 0, [array(size // 2, factor)] * 2, [VMEM] * (GROUP + 1)
    )(*(pieces[step] for step in (0, 3, 1, 2)), exchange(act_sum, flops=16 * width**3))
    out = send([exchange(factors)] * GROUP)
    pieces = send(parts[GROUP:])
    total, act_part = call(
        pass_kernel, 0, [array(size // 2, 2 * width), array(size // 2, factor)], [VMEM] * (GROUP + 1)
    )(*(pieces[step] for step in (0, 3, 1, 2)), act_part)
    act = send([act_part] * GROUP)

    def inverse(pieces, after, *through):
        return call(
            functools.partial(through_kernel if through else inverse_kernel, count),
            20 * width**3,
            [array(width, width)] + [array(*value.shape) for value in through],
            [VMEM] * len(through) + [ANY] + [VMEM] * GROUP,
            [pltpu.VMEM((GROUP, size // 2, factor), BF16), pltpu.VMEM((width, width), BF16)],
        )(*through, after, *pieces)

    total = exchange(total, (*out, act[2]))
    grad = send([total] * GROUP)
    out_inv, give_cot = inverse(out, total, give_cot)
    (act_inv,) = inverse(act, total)
    other_cot = lax.ppermute(give_cot, "core", SWAP)
    update, cot = call(
        update_kernel,
        10 * width**3,
        [array(width, width, dtype=F32), array(micro, rows, width)],
        [VMEM] * (4 + GROUP),
        [
            pltpu.VMEM((width, width), BF16),
            pltpu.VMEM((width, width), F32),
            pltpu.SemaphoreType.DMA((4,)),
        ],
        HBM,
    )(act_inv, out_inv, own_cot, other_cot, *grad)
    return (cot[None], update[None])


def solution(mesh):
    sections, shards = mesh.devices.shape
    finer = Mesh(
        np.reshape(mesh.devices, (sections // 2, 2, shards // GROUP, 2, 2)),
        ("row", "core", "far", "near", "side"),
    )
    section, dp = ("row", "core"), ("far", "near", "side")
    placed = (P(section, None, dp, None), P(section, None, None), P(None, dp, None))
    return jax.shard_map(
        body,
        mesh=finer,
        in_specs=placed,
        out_specs=(P(section, None, dp, None), P(section, None, None)),
        check_vma=False,
    )
```

```python
import functools

import jax
import jax.numpy as jnp
import numpy as np
from jax import lax
from jax.experimental import pallas as pl
from jax.experimental.pallas import tpu as pltpu
from jax.sharding import Mesh, PartitionSpec as P

BF16 = jnp.bfloat16
F32 = jnp.float32
SWAP = [(0, 1), (1, 0)]
VMEM = pl.BlockSpec(memory_space=pltpu.VMEM)
ANY = pl.BlockSpec(memory_space=pl.ANY)
HBM = pl.BlockSpec(memory_space=pltpu.HBM)
GROUP = 4


def silu_slope(pre):
    sig = jax.nn.sigmoid(pre)
    return sig * (1.0 + pre * (1.0 - sig))


def slope_of(inputs, matrix):
    return silu_slope(jnp.dot(inputs, matrix, preferred_element_type=F32))


def layer(upstream, slope, matrix):
    dh = (upstream.astype(F32) * slope).astype(BF16)
    back = lax.dot_general(dh, matrix, (((1,), (1,)), ((), ())), preferred_element_type=F32)
    return dh, (upstream.astype(F32) + back).astype(BF16)


def by_core(core, run, own, partner):
    @pl.when(core == 1)
    def _():
        run(own, partner)

    @pl.when(core == 0)
    def _():
        run(partner, own)


def moment(left, right):
    return lax.dot_general(left, right, (((0,), (0,)), ((), ())), preferred_element_type=F32)


def group_place():
    return 2 * lax.axis_index("near") + lax.axis_index("side")


def dot(left, right):
    return jnp.dot(left.astype(BF16), right.astype(BF16), preferred_element_type=F32)


def call(kernel, flops, out_shape, in_specs, scratch=(), out_spec=VMEM):
    return pl.pallas_call(
        kernel,
        out_shape=jax.tree.map(lambda v: jax.ShapeDtypeStruct(v.shape, v.dtype), out_shape),
        in_specs=in_specs,
        out_specs=jax.tree.map(lambda _: out_spec, out_shape),
        scratch_shapes=list(scratch),
        cost_estimate=pl.CostEstimate(flops=flops, bytes_accessed=1 << 20, transcendentals=0),
        compiler_params=pltpu.CompilerParams(vmem_limit_bytes=32 << 20),
    )


def first_kernel(
    weight, local, cot_last, partner, partner_local,
    own, kept, last, slope_own, slope_partner, down,
):
    core = lax.axis_index("core")
    last[...] = cot_last[core]
    slope_own[...] = slope_of(local[core], weight[...])
    slope_partner[...] = slope_of(partner_local[core], partner[...])

    def run(odd, even):
        cot = layer(last[...], odd[1][...], odd[0][...])[1]
        down[...] = layer(cot, even[1][...], even[0][...])[1]

    by_core(core, run, (weight, slope_own), (partner, slope_partner))
    own[...] = weight[...]
    kept[...] = local[...]


def sum_kernel(*refs):
    result = refs[-1]
    result[...] = sum(piece[...].astype(F32) for piece in refs[:GROUP]).astype(BF16)


def pass_kernel(*refs):
    refs[-2][...] = sum(piece[...].astype(F32) for piece in refs[:GROUP]).astype(BF16)
    refs[-1][...] = refs[GROUP][...]


def layers_kernel(
    own, partner, slope_own, slope_partner, arrived, last, own_dh, give_dh, own_cot, give_cot
):
    upstream = jnp.where(lax.axis_index("row") == lax.axis_size("row") - 1, last[...], arrived[...])

    def run(odd, even):
        dh, cot = layer(upstream, odd[1][...], odd[0][...])
        odd[2][...], odd[3][...] = dh, cot
        even[2][...], even[3][...] = layer(cot, even[1][...], even[0][...])

    by_core(
        lax.axis_index("core"), run, (own, slope_own, own_dh, own_cot), (partner, slope_partner, give_dh, give_cot)
    )


def put_factor(tokens, whole):
    width = tokens.shape[1]
    size = width // GROUP
    half = size // 2
    columns = [tokens[:, u * size:(u + 1) * size] for u in range(GROUP)]
    for u in range(GROUP):
        pair = jnp.concatenate([columns[u], columns[(u + 1) % GROUP]], axis=1)
        main = moment(columns[u], pair).astype(BF16)
        whole[u, :, :2 * size] = main[:half]
        whole[u, :, 2 * size:4 * size] = main[half:]
    for u in range(2):
        corner = moment(columns[u], columns[u + 2]).astype(BF16)
        whole[u, :, 4 * size:5 * size] = corner[:half]
        whole[u + 2, :, 4 * size:5 * size] = corner[half:]


def act_kernel(local, after, *refs):
    parts, (tokens, whole) = refs[:GROUP], refs[GROUP:]
    micro, rows = local.shape[:2]
    for m in range(micro):
        tokens[m * rows:(m + 1) * rows] = local[m]
    put_factor(tokens, whole)
    for step, part in enumerate(parts):
        part[...] = whole[group_place() ^ step]


def add_kernel(left, right, *refs):
    refs[-1][...] = (left[...].astype(F32) + right[...].astype(F32)).astype(BF16)


def grad_kernel(local, dh_own, dh_got, after, *refs):
    factors, grads, (inputs, tokens, whole, rest) = refs[:GROUP], refs[GROUP:2 * GROUP], refs[2 * GROUP:]
    rows, width = local.shape[1:]
    inputs[:rows] = local[lax.axis_index("core")]
    inputs[rows:] = local[1 - lax.axis_index("core")]
    tokens[:rows] = dh_own[...]
    tokens[rows:] = dh_got[...]
    put_factor(tokens, whole)
    size = width // GROUP
    half = size // 2
    for u in range(GROUP):
        grad = moment(inputs[:, u * size:(u + 1) * size], tokens[...]).astype(BF16)
        rest[u, :, :width] = grad[:half]
        rest[u, :, width:] = grad[half:]
    for step in range(GROUP):
        factors[step][...] = whole[group_place() ^ step]
        grads[step][...] = rest[group_place() ^ step]


def invert(total, count):
    row = lax.broadcasted_iota(jnp.int32, total.shape, 0)
    column = lax.broadcasted_iota(jnp.int32, total.shape, 1)
    eye = (row == column).astype(F32)
    ridge = 0.01
    mean = total[...].astype(F32) * (1.0 / count)
    full = mean + ridge * eye
    scale = lax.rsqrt(jnp.sum(full * full, keepdims=True))
    squared = dot(total[...], total[...]) * (1.0 / count) ** 2 + ridge * (mean + full)
    second = (2.0 * scale) * full - squared * (scale * scale)
    last = 2.0 * (eye - second) + dot(second, second)
    tail = 2.0 * last - dot(second, last)
    inner = dot(total[...], tail) * (scale * (1.0 / count))
    return (((2.0 - ridge * scale) * tail - inner) * scale).astype(BF16)


def through_kernel(count, through, after, *refs):
    through_copy = refs[GROUP + 1]
    through_copy[...] = through[...]
    inverse_kernel(count, after, *refs[:GROUP + 1], *refs[GROUP + 2:])


def inverse_kernel(count, after, *refs):
    pieces, (result, blocks, total) = refs[:GROUP], refs[GROUP:]
    for step, piece in enumerate(pieces):
        blocks[group_place() ^ step] = piece[...]
    size = total.shape[0] // GROUP

    def both(row, column, value):
        total[row * size:(row + 1) * size, column * size:(column + 1) * size] = value
        if row != column:
            turned = value.astype(F32).T.astype(BF16)
            total[column * size:(column + 1) * size, row * size:(row + 1) * size] = turned

    for u in range(GROUP):
        main = jnp.concatenate([blocks[u, :, :2 * size], blocks[u, :, 2 * size:4 * size]])
        both(u, u, main[:, :size])
        both(u, (u + 1) % GROUP, main[:, size:])
    for u in range(2):
        both(u, u + 2, jnp.concatenate([blocks[u, :, 4 * size:], blocks[u + 2, :, 4 * size:]]))
    result[...] = invert(total, count)


def update_kernel(act_inv, out_inv, own_cot, other_cot, *refs):
    pieces, (result, cot, grad, update, done) = refs[:GROUP], refs[GROUP:]
    copies = [
        pltpu.make_async_copy(own_cot, cot.at[lax.axis_index("core")], done.at[0]),
        pltpu.make_async_copy(other_cot, cot.at[1 - lax.axis_index("core")], done.at[1]),
    ]
    for copy in copies:
        copy.start()
    half, twice = pieces[0].shape
    width = twice // 2
    for step, piece in enumerate(pieces):
        start = pl.multiple_of((group_place() ^ step) * 2 * half, 2 * half)
        grad[pl.ds(start, half)] = piece[:, :width]
        grad[pl.ds(start + half, half)] = piece[:, width:]
    left = dot(act_inv[...], grad[...]).astype(BF16)
    for part in range(2):
        rows = slice(part * width // 2, (part + 1) * width // 2)
        update[rows] = dot(left[rows], out_inv[...])
        copies.append(pltpu.make_async_copy(update.at[rows], result.at[rows], done.at[2 + part]))
        copies[-1].start()
    for copy in copies:
        copy.wait()


def send(parts):
    got = {0: parts[0]}
    for step in (3, 1, 2):
        got[step] = lax.ppermute(parts[step], ("near", "side"), [(i, i ^ step) for i in range(GROUP)])
    return [got[step] for step in range(GROUP)]


def exchange(value, after=(), flops=0):
    step = 1
    while step < lax.axis_size("far"):
        route = [(i, i ^ step) for i in range(lax.axis_size("far"))]
        got = lax.ppermute(value, "far", route)
        value = call(add_kernel, flops, value, [VMEM] * 2 + [ANY] * len(after))(value, got, *after)
        step *= 2
    return value


def body(acts, weights, cot_last):
    pairs = lax.axis_size("row")
    row = lax.axis_index("row")
    core = lax.axis_index("core")
    weight = weights[0]
    local = acts[0]
    micro, rows, width = local.shape
    tokens = micro * rows
    count = tokens * GROUP * lax.axis_size("far")
    odd = core == 1

    def mine_of(pair):
        return jnp.where(odd, pair[1], pair[0])

    def array(*shape, dtype=BF16):
        return jax.ShapeDtypeStruct(shape, dtype)

    def near_copy(value):
        return jnp.where(core > 1, jnp.zeros_like(value), value)

    partner = lax.ppermute(weight, "core", SWAP)
    partner_local = lax.ppermute(local, "core", SWAP)
    block = array(rows, width)
    slope = array(rows, width, dtype=F32)
    own, kept, last, slope_own, slope_partner, down = call(
        first_kernel,
        8 * rows * width**2,
        [array(width, width), array(micro, rows, width), block, slope, slope, block],
        [VMEM] * 5,
    )(near_copy(weight), near_copy(local), near_copy(cot_last), partner, partner_local)
    first = down
    for turn in range(1, pairs):
        upstream = lax.ppermute(down, "row", [(r, r - 1) for r in range(1, pairs)])
        arrived = upstream if turn == 1 else jnp.where(row == pairs - 1 - turn, upstream, arrived)
        if turn < pairs - 1:
            cot = layer(upstream, mine_of((slope_partner, slope_own)), mine_of((partner, own)))[1]
            down = layer(cot, mine_of((slope_own, slope_partner)), mine_of((own, partner)))[1]

    size = width // GROUP
    factor = 5 * size
    act_parts = call(
        act_kernel,
        2 * tokens * width**2,
        [array(size // 2, factor)] * GROUP,
        [VMEM, ANY],
        [pltpu.VMEM((tokens, width), BF16), pltpu.VMEM((GROUP, size // 2, factor), BF16)],
    )(kept, first)
    act_pieces = send(act_parts)

    own_dh, give_dh, own_cot, give_cot = call(
        layers_kernel, 64 * rows * width**2, [block] * 4, [VMEM] * 6
    )(own, partner, slope_own, slope_partner, arrived, last)
    act_sum = call(sum_kernel, 24 * width**3, array(size // 2, factor), [VMEM] * GROUP + [ANY])(
        *(act_pieces[step] for step in (0, 3, 1, 2)), own_dh
    )
    got_dh = lax.ppermute(give_dh, "core", SWAP)

    parts = call(
        grad_kernel,
        4 * tokens * width**2,
        [array(size // 2, factor)] * GROUP + [array(size // 2, 2 * width)] * GROUP,
        [VMEM] * 3 + [ANY],
        [pltpu.VMEM((tokens, width), BF16)] * 2
        + [pltpu.VMEM((GROUP, size // 2, factor), BF16), pltpu.VMEM((GROUP, size // 2, 2 * width), BF16)],
    )(kept, own_dh, got_dh, act_sum)

    pieces = send(parts[:GROUP])
    factors, act_part = call(
        pass_kernel, 0, [array(size // 2, factor)] * 2, [VMEM] * (GROUP + 1)
    )(*(pieces[step] for step in (0, 3, 1, 2)), exchange(act_sum, flops=16 * width**3))
    out = send([exchange(factors)] * GROUP)
    pieces = send(parts[GROUP:])
    total, act_part = call(
        pass_kernel, 0, [array(size // 2, 2 * width), array(size // 2, factor)], [VMEM] * (GROUP + 1)
    )(*(pieces[step] for step in (0, 3, 1, 2)), act_part)
    act = send([act_part] * GROUP)

    def inverse(pieces, after, *through):
        return call(
            functools.partial(through_kernel if through else inverse_kernel, count),
            20 * width**3,
            [array(width, width)] + [array(*value.shape) for value in through],
            [VMEM] * len(through) + [ANY] + [VMEM] * GROUP,
            [pltpu.VMEM((GROUP, size // 2, factor), BF16), pltpu.VMEM((width, width), BF16)],
        )(*through, after, *pieces)

    total = exchange(total, (*out, act[3]))
    grad = send([total] * GROUP)
    out_inv, give_cot = inverse(out, total, give_cot)
    (act_inv,) = inverse(act, total)
    other_cot = lax.ppermute(give_cot, "core", SWAP)
    update, cot = call(
        update_kernel,
        10 * width**3,
        [array(width, width, dtype=F32), array(micro, rows, width)],
        [VMEM] * (4 + GROUP),
        [
            pltpu.VMEM((width, width), BF16),
            pltpu.VMEM((width, width), F32),
            pltpu.SemaphoreType.DMA((4,)),
        ],
        HBM,
    )(act_inv, out_inv, own_cot, other_cot, *grad)
    return (cot[None], update[None])


def solution(mesh):
    sections, shards = mesh.devices.shape
    finer = Mesh(
        np.reshape(mesh.devices, (sections // 2, 2, shards // GROUP, 2, 2)),
        ("row", "core", "far", "near", "side"),
    )
    section, dp = ("row", "core"), ("far", "near", "side")
    placed = (P(section, None, dp, None), P(section, None, None), P(None, dp, None))
    return jax.shard_map(
        body,
        mesh=finer,
        in_specs=placed,
        out_specs=(P(section, None, dp, None), P(section, None, None)),
        check_vma=False,
    )
```

```python
import functools

import jax
import jax.numpy as jnp
import numpy as np
from jax import lax
from jax.experimental import pallas as pl
from jax.experimental.pallas import tpu as pltpu
from jax.sharding import Mesh, PartitionSpec as P

BF16 = jnp.bfloat16
F32 = jnp.float32
SWAP = [(0, 1), (1, 0)]
VMEM = pl.BlockSpec(memory_space=pltpu.VMEM)
ANY = pl.BlockSpec(memory_space=pl.ANY)
HBM = pl.BlockSpec(memory_space=pltpu.HBM)
GROUP = 4


def silu_slope(pre):
    sig = jax.nn.sigmoid(pre)
    return sig * (1.0 + pre * (1.0 - sig))


def slope_of(inputs, matrix):
    return silu_slope(jnp.dot(inputs, matrix, preferred_element_type=F32))


def layer(upstream, slope, matrix):
    dh = (upstream.astype(F32) * slope).astype(BF16)
    back = lax.dot_general(dh, matrix, (((1,), (1,)), ((), ())), preferred_element_type=F32)
    return dh, (upstream.astype(F32) + back).astype(BF16)


def by_core(core, run, own, partner):
    @pl.when(core == 1)
    def _():
        run(own, partner)

    @pl.when(core == 0)
    def _():
        run(partner, own)


def moment(left, right):
    return lax.dot_general(left, right, (((0,), (0,)), ((), ())), preferred_element_type=F32)


def group_place():
    return 2 * lax.axis_index("near") + lax.axis_index("side")


def dot(left, right):
    return jnp.dot(left.astype(BF16), right.astype(BF16), preferred_element_type=F32)


def call(kernel, flops, out_shape, in_specs, scratch=(), out_spec=VMEM):
    return pl.pallas_call(
        kernel,
        out_shape=jax.tree.map(lambda v: jax.ShapeDtypeStruct(v.shape, v.dtype), out_shape),
        in_specs=in_specs,
        out_specs=jax.tree.map(lambda _: out_spec, out_shape),
        scratch_shapes=list(scratch),
        cost_estimate=pl.CostEstimate(flops=flops, bytes_accessed=1 << 20, transcendentals=0),
        compiler_params=pltpu.CompilerParams(vmem_limit_bytes=32 << 20),
    )


def first_kernel(own, partner, local, partner_local, cot_last, slope_own, slope_partner, down):
    core = lax.axis_index("core")
    slope_own[...] = slope_of(local[core], own[...])
    slope_partner[...] = slope_of(partner_local[core], partner[...])

    def run(odd, even):
        cot = layer(cot_last[core], odd[1][...], odd[0][...])[1]
        down[...] = layer(cot, even[1][...], even[0][...])[1]

    by_core(core, run, (own, slope_own), (partner, slope_partner))


def sum_kernel(*refs):
    result = refs[-1]
    result[...] = sum(piece[...].astype(F32) for piece in refs[:GROUP]).astype(BF16)


def pass_kernel(*refs):
    refs[-2][...] = sum(piece[...].astype(F32) for piece in refs[:GROUP]).astype(BF16)
    refs[-1][...] = refs[GROUP][...]


def layers_kernel(
    own, partner, slope_own, slope_partner, arrived, last, own_dh, give_dh, own_cot, give_cot
):
    upstream = jnp.where(lax.axis_index("row") == lax.axis_size("row") - 1, last[lax.axis_index("core")], arrived[...])

    def run(odd, even):
        dh, cot = layer(upstream, odd[1][...], odd[0][...])
        odd[2][...], odd[3][...] = dh, cot
        even[2][...], even[3][...] = layer(cot, even[1][...], even[0][...])

    by_core(
        lax.axis_index("core"), run, (own, slope_own, own_dh, own_cot), (partner, slope_partner, give_dh, give_cot)
    )


def put_factor(tokens, whole):
    width = tokens.shape[1]
    size = width // GROUP
    half = size // 2
    columns = [tokens[:, u * size:(u + 1) * size] for u in range(GROUP)]
    for u in range(GROUP):
        pair = jnp.concatenate([columns[u], columns[(u + 1) % GROUP]], axis=1)
        main = moment(columns[u], pair).astype(BF16)
        whole[u, :, :2 * size] = main[:half]
        whole[u, :, 2 * size:4 * size] = main[half:]
    for u in range(2):
        corner = moment(columns[u], columns[u + 2]).astype(BF16)
        whole[u, :, 4 * size:5 * size] = corner[:half]
        whole[u + 2, :, 4 * size:5 * size] = corner[half:]


def act_kernel(local, after, *refs):
    parts, (tokens, whole) = refs[:GROUP], refs[GROUP:]
    micro, rows = local.shape[:2]
    for m in range(micro):
        tokens[m * rows:(m + 1) * rows] = local[m]
    put_factor(tokens, whole)
    for step, part in enumerate(parts):
        part[...] = whole[group_place() ^ step]


def add_kernel(left, right, *refs):
    refs[-1][...] = (left[...].astype(F32) + right[...].astype(F32)).astype(BF16)


def grad_kernel(local, dh_own, dh_got, after, *refs):
    factors, grads, (inputs, tokens, whole, rest) = refs[:GROUP], refs[GROUP:2 * GROUP], refs[2 * GROUP:]
    rows, width = local.shape[1:]
    inputs[:rows] = local[lax.axis_index("core")]
    inputs[rows:] = local[1 - lax.axis_index("core")]
    tokens[:rows] = dh_own[...]
    tokens[rows:] = dh_got[...]
    put_factor(tokens, whole)
    size = width // GROUP
    half = size // 2
    for u in range(GROUP):
        grad = moment(inputs[:, u * size:(u + 1) * size], tokens[...]).astype(BF16)
        rest[u, :, :width] = grad[:half]
        rest[u, :, width:] = grad[half:]
    for step in range(GROUP):
        factors[step][...] = whole[group_place() ^ step]
        grads[step][...] = rest[group_place() ^ step]


def invert(total, count):
    row = lax.broadcasted_iota(jnp.int32, total.shape, 0)
    column = lax.broadcasted_iota(jnp.int32, total.shape, 1)
    eye = (row == column).astype(F32)
    ridge = 0.01
    mean = total[...].astype(F32) * (1.0 / count)
    full = mean + ridge * eye
    scale = lax.rsqrt(jnp.sum(full * full, keepdims=True))
    squared = dot(total[...], total[...]) * (1.0 / count) ** 2 + ridge * (mean + full)
    second = (2.0 * scale) * full - squared * (scale * scale)
    last = 2.0 * (eye - second) + dot(second, second)
    tail = 2.0 * last - dot(second, last)
    inner = dot(total[...], tail) * (scale * (1.0 / count))
    return (((2.0 - ridge * scale) * tail - inner) * scale).astype(BF16)


def through_kernel(count, through, after, *refs):
    through_copy = refs[GROUP + 1]
    through_copy[...] = through[...]
    inverse_kernel(count, after, *refs[:GROUP + 1], *refs[GROUP + 2:])


def inverse_kernel(count, after, *refs):
    pieces, (result, blocks, total) = refs[:GROUP], refs[GROUP:]
    for step, piece in enumerate(pieces):
        blocks[group_place() ^ step] = piece[...]
    size = total.shape[0] // GROUP

    def both(row, column, value):
        total[row * size:(row + 1) * size, column * size:(column + 1) * size] = value
        if row != column:
            turned = value.astype(F32).T.astype(BF16)
            total[column * size:(column + 1) * size, row * size:(row + 1) * size] = turned

    for u in range(GROUP):
        main = jnp.concatenate([blocks[u, :, :2 * size], blocks[u, :, 2 * size:4 * size]])
        both(u, u, main[:, :size])
        both(u, (u + 1) % GROUP, main[:, size:])
    for u in range(2):
        both(u, u + 2, jnp.concatenate([blocks[u, :, 4 * size:], blocks[u + 2, :, 4 * size:]]))
    result[...] = invert(total, count)


def update_kernel(act_inv, out_inv, own_cot, other_cot, *refs):
    pieces, (result, cot, grad, update, done) = refs[:GROUP], refs[GROUP:]
    copies = [
        pltpu.make_async_copy(own_cot, cot.at[lax.axis_index("core")], done.at[0]),
        pltpu.make_async_copy(other_cot, cot.at[1 - lax.axis_index("core")], done.at[1]),
    ]
    for copy in copies:
        copy.start()
    half, twice = pieces[0].shape
    width = twice // 2
    for step, piece in enumerate(pieces):
        start = pl.multiple_of((group_place() ^ step) * 2 * half, 2 * half)
        grad[pl.ds(start, half)] = piece[:, :width]
        grad[pl.ds(start + half, half)] = piece[:, width:]
    left = dot(act_inv[...], grad[...]).astype(BF16)
    for part in range(2):
        rows = slice(part * width // 2, (part + 1) * width // 2)
        update[rows] = dot(left[rows], out_inv[...])
        copies.append(pltpu.make_async_copy(update.at[rows], result.at[rows], done.at[2 + part]))
        copies[-1].start()
    for copy in copies:
        copy.wait()


def send(parts):
    got = {0: parts[0]}
    for step in (3, 1, 2):
        got[step] = lax.ppermute(parts[step], ("near", "side"), [(i, i ^ step) for i in range(GROUP)])
    return [got[step] for step in range(GROUP)]


def exchange(value, after=(), flops=0):
    step = 1
    while step < lax.axis_size("far"):
        route = [(i, i ^ step) for i in range(lax.axis_size("far"))]
        got = lax.ppermute(value, "far", route)
        value = call(add_kernel, flops, value, [VMEM] * 2 + [ANY] * len(after))(value, got, *after)
        step *= 2
    return value


def body(acts, weights, cot_last):
    pairs = lax.axis_size("row")
    row = lax.axis_index("row")
    core = lax.axis_index("core")
    weight = weights[0]
    local = acts[0]
    micro, rows, width = local.shape
    tokens = micro * rows
    count = tokens * GROUP * lax.axis_size("far")
    odd = core == 1

    def mine_of(pair):
        return jnp.where(odd, pair[1], pair[0])

    def array(*shape, dtype=BF16):
        return jax.ShapeDtypeStruct(shape, dtype)

    def near_copy(value):
        return jnp.where(core > 1, jnp.zeros_like(value), value)

    partner = lax.ppermute(weight, "core", SWAP)
    partner_local = lax.ppermute(local, "core", SWAP)
    block = array(rows, width)
    slope = array(rows, width, dtype=F32)
    own, kept, last = near_copy(weight), near_copy(local), near_copy(cot_last)
    slope_own, slope_partner, down = call(
        first_kernel, 8 * rows * width**2, [slope, slope, block], [VMEM] * 5
    )(own, partner, kept, partner_local, last)
    first = down
    for turn in range(1, pairs):
        upstream = lax.ppermute(down, "row", [(r, r - 1) for r in range(1, pairs)])
        arrived = upstream if turn == 1 else jnp.where(row == pairs - 1 - turn, upstream, arrived)
        if turn < pairs - 1:
            cot = layer(upstream, mine_of((slope_partner, slope_own)), mine_of((partner, own)))[1]
            down = layer(cot, mine_of((slope_own, slope_partner)), mine_of((own, partner)))[1]

    size = width // GROUP
    factor = 5 * size
    act_parts = call(
        act_kernel,
        2 * tokens * width**2,
        [array(size // 2, factor)] * GROUP,
        [VMEM, ANY],
        [pltpu.VMEM((tokens, width), BF16), pltpu.VMEM((GROUP, size // 2, factor), BF16)],
    )(kept, first)
    act_pieces = send(act_parts)

    own_dh, give_dh, own_cot, give_cot = call(
        layers_kernel, 64 * rows * width**2, [block] * 4, [VMEM] * 6
    )(own, partner, slope_own, slope_partner, arrived, last)
    act_sum = call(sum_kernel, 24 * width**3, array(size // 2, factor), [VMEM] * GROUP + [ANY])(
        *(act_pieces[step] for step in (0, 3, 1, 2)), own_dh
    )
    got_dh = lax.ppermute(give_dh, "core", SWAP)

    parts = call(
        grad_kernel,
        4 * tokens * width**2,
        [array(size // 2, factor)] * GROUP + [array(size // 2, 2 * width)] * GROUP,
        [VMEM] * 3 + [ANY],
        [pltpu.VMEM((tokens, width), BF16)] * 2
        + [pltpu.VMEM((GROUP, size // 2, factor), BF16), pltpu.VMEM((GROUP, size // 2, 2 * width), BF16)],
    )(kept, own_dh, got_dh, act_sum)

    pieces = send(parts[:GROUP])
    factors, act_part = call(
        pass_kernel, 0, [array(size // 2, factor)] * 2, [VMEM] * (GROUP + 1)
    )(*(pieces[step] for step in (0, 3, 1, 2)), exchange(act_sum, flops=16 * width**3))
    out = send([exchange(factors)] * GROUP)
    pieces = send(parts[GROUP:])
    total, act_part = call(
        pass_kernel, 0, [array(size // 2, 2 * width), array(size // 2, factor)], [VMEM] * (GROUP + 1)
    )(*(pieces[step] for step in (0, 3, 1, 2)), act_part)
    act = send([act_part] * GROUP)

    def inverse(pieces, after, *through):
        return call(
            functools.partial(through_kernel if through else inverse_kernel, count),
            20 * width**3,
            [array(width, width)] + [array(*value.shape) for value in through],
            [VMEM] * len(through) + [ANY] + [VMEM] * GROUP,
            [pltpu.VMEM((GROUP, size // 2, factor), BF16), pltpu.VMEM((width, width), BF16)],
        )(*through, after, *pieces)

    total = exchange(total, (*out, act[1]))
    grad = send([total] * GROUP)
    out_inv, give_cot = inverse(out, total, give_cot)
    (act_inv,) = inverse(act, total)
    other_cot = lax.ppermute(give_cot, "core", SWAP)
    update, cot = call(
        update_kernel,
        10 * width**3,
        [array(width, width, dtype=F32), array(micro, rows, width)],
        [VMEM] * (4 + GROUP),
        [
            pltpu.VMEM((width, width), BF16),
            pltpu.VMEM((width, width), F32),
            pltpu.SemaphoreType.DMA((4,)),
        ],
        HBM,
    )(act_inv, out_inv, own_cot, other_cot, *grad)
    return (cot[None], update[None])


def solution(mesh):
    sections, shards = mesh.devices.shape
    finer = Mesh(
        np.reshape(mesh.devices, (sections // 2, 2, shards // GROUP, 2, 2)),
        ("row", "core", "far", "near", "side"),
    )
    section, dp = ("row", "core"), ("far", "near", "side")
    placed = (P(section, None, dp, None), P(section, None, None), P(None, dp, None))
    return jax.shard_map(
        body,
        mesh=finer,
        in_specs=placed,
        out_specs=(P(section, None, dp, None), P(section, None, None)),
        check_vma=False,
    )
```
